512 devices in a mesh: dom: 128 (over y, z, core), sub: 4 (over x).
Axes of the slice: x: 4, y: 8, z: 8, core: 2. Of those that a mesh axis runs over, the one named last changes fastest.
Arguments:
- fields: float32 [6, 20, 524288], P(None, None, ('dom', 'sub')), may hold values from -6 to 6
- geometry: float32 [9, 524288], P(None, ('dom', 'sub')), may hold values from -4 to 4
- normals: float32 [3, 4, 524288], P(None, None, ('dom', 'sub')), may hold values from -3 to 3
- face_scale: float32 [4, 524288], P(None, ('dom', 'sub')), may hold values from 0.5 to 3
- derivatives: float32 [3, 20, 20], replicated, may hold values from -1.25 to 1.25
- lift_matrix: float32 [20, 40], replicated, may hold values from -1 to 1
- face_nbr: int32 [4, 524288], P(None, ('dom', 'sub')), may hold values from 0 to 4607, as said below
- send_rows: int32 [262144], P(('dom', 'sub')), may hold values from 64 to 1024, as said below
- fine_slots: int32 [65536], P(('dom', 'sub')), may hold values from 0 to 511, as said below
- export_rows: int32 [2, 8192], P(None, ('dom', 'sub')), may hold values from 0 to 127, as said below
- fine_nbr: int32 [4, 65536], P(None, ('dom', 'sub')), may hold values from 0 to 640
Outputs:
- fields_out: float32 [6, 20, 524288], P(None, None, ('dom', 'sub'))
The draws below stay inside these ranges and needn't reach their ends.
Inputs may be any that keep to these rules, and one draw needn't show every extreme that they name: `face_nbr`: A wall face holds its own number 4 (e - p * 1024) + f. Codes from 4096 up occur only on the first 64 and the last 64 elements of a device: the first 64 use 4 * 1024 to 4351, the last 64 use 4 * 1024 + 4 * 64 and above. `send_rows`: entry p * 512 + j * 4 + c is the row within device p of the c-th element that p hands to the device of dom index j and p's sub index; 1024 marks an empty slot, and filled slots come first in each group of 4. Each group holds 0, 2 or 4 elements; in each sub index half of the dom indices hand 2 * 128 elements each, each of them 4 to some device, the others hand none. Handed rows are distinct and lie in 64 to 959. `fine_slots`: the 128 entries of a device are the filled slots j * 4 + c addressed to it (j the sender's dom index), each exactly once, in some order. `export_rows`: each row of a device holds 16 distinct positions among its 128 fine elements.
All inputs are finite; a program needn't handle non-finite values.
Results may differ from the reference program's by a relative error of at most 0.0001.
Values sent between devices are 32-bit elements; how exact they have to be, the bound alone decides.
No kernel may reach another device: no remote copies, remote signals or barrier semaphores. Data moves between devices by JAX's collectives and lax.ppermute only.
A program may use at most 128 MiB of HBM per device.

```python
import math
import jax
import jax.numpy as jnp
import numpy as np
from jax import lax

NP = 20
NFP = 10
CE = 1024
FINE_DEV = 128
SUBSTEPS = 4
NB = 64
PB = 16
CAP = 4
SLOTS = 512
ELEMENTS = 524288
FINE_TOT = 65536
N_DOM = 128
N_SUB = 4
DEVICES = 512


def column_routing(column_key):
    subkeys = jax.random.split(column_key, 4)
    owner_order = jax.random.permutation(subkeys[0], N_DOM)
    receiver_order = jax.random.permutation(subkeys[1], N_DOM)
    half_dom = N_DOM // 2
    is_owner = owner_order < half_dom
    sign_one = jnp.where(owner_order < N_DOM // 4, 1, -1)
    sign_two = jnp.where((owner_order < N_DOM // 8) | (owner_order >= N_DOM // 4) & (owner_order < 3 * N_DOM // 8), 1, -1)
    recv_one = jnp.where(receiver_order < half_dom, 1, -1)
    recv_two = jnp.where((receiver_order < N_DOM // 4) | (receiver_order >= half_dom) & (receiver_order < 3 * N_DOM // 4), 1, -1)
    counts = CAP // 2 * (1 + (sign_one[:, None] * recv_one[None, :] + sign_two[:, None] * recv_two[None, :]) // 2)
    counts = jnp.where(is_owner[:, None], counts, 0)
    row_keys = jax.random.split(subkeys[2], N_DOM)

    def owner_pick(row_key):
        return jax.random.permutation(row_key, CE - 2 * NB)[:2 * FINE_DEV] + NB
    owner_rows = jax.vmap(owner_pick)(row_keys)
    starts = jnp.cumsum(counts, axis=1) - counts
    places = jnp.arange(CAP)
    filled = places[None, None, :] < counts[:, :, None]
    rank_index = jnp.minimum(starts[:, :, None] + places[None, None, :], 2 * FINE_DEV - 1)
    chosen_rows = owner_rows[jnp.arange(N_DOM)[:, None, None], rank_index]
    send_table = jnp.where(filled, chosen_rows, CE).reshape(N_DOM, SLOTS)
    slot_flags = filled.transpose(1, 0, 2).reshape(N_DOM, SLOTS)
    slot_keys = jax.random.split(subkeys[3], N_DOM)

    def receiver_slots(slot_key, flags_row):
        scores = jax.random.permutation(slot_key, SLOTS)
        return jnp.argsort(jnp.where(flags_row, scores, scores + SLOTS), stable=True)[:FINE_DEV]
    slot_table = jax.vmap(receiver_slots)(slot_keys, slot_flags)
    return (send_table, slot_table)


def fine_routing(key):
    sends, slot_table = jax.vmap(column_routing)(jax.random.split(key, N_SUB))
    sends = sends.transpose(1, 0, 2).reshape(DEVICES * SLOTS)
    slot_table = slot_table.transpose(1, 0, 2).reshape(DEVICES * FINE_DEV)
    return (sends.astype(jnp.int32), slot_table.astype(jnp.int32))


def draw_send_rows(key, part):
    shared = fine_routing(key)
    return shared[0]


def draw_fine_slots(key, part):
    shared = fine_routing(key)
    return shared[1]


def draw_face_nbr(key, part):
    key = jax.random.fold_in(key, 11)
    subkeys = jax.random.split(key, 4)
    grid_shape = (4, ELEMENTS)
    element = jnp.arange(ELEMENTS)[None, :] + jnp.zeros((4, 1), jnp.int32)
    facets = jnp.arange(4)[:, None] + jnp.zeros((1, ELEMENTS), jnp.int32)
    own_row = element % CE
    category = jax.random.randint(subkeys[0], grid_shape, 0, 10)
    any_row = jax.random.randint(subkeys[1], grid_shape, 0, CE)
    any_face = jax.random.randint(subkeys[2], grid_shape, 0, 4)
    rim_row = jax.random.randint(subkeys[3], grid_shape, 0, NB)
    inside = 4 * any_row + any_face
    lower_face = 4 * CE + 4 * rim_row + any_face
    upper_face = 4 * CE + 4 * NB + 4 * rim_row + any_face
    self_face = 4 * own_row + facets
    result = jnp.where(category == 0, self_face, jnp.where((category <= 3) & (own_row < NB), lower_face, jnp.where((category <= 3) & (own_row >= CE - NB), upper_face, inside)))
    return result.astype(jnp.int32)


def draw_export_rows(key, part):
    key = jax.random.fold_in(key, 5)

    def one_device(device_key):
        pair_keys = jax.random.split(device_key)
        return jnp.stack([jax.random.permutation(pair_keys[0], FINE_DEV)[:PB], jax.random.permutation(pair_keys[1], FINE_DEV)[:PB]])
    export_lists = jax.vmap(one_device)(jax.random.split(key, DEVICES))
    return export_lists.transpose(1, 0, 2).reshape(2, DEVICES * PB).astype(jnp.int32)


def draw_fine_nbr(key, part):
    key = jax.random.fold_in(key, 7)
    subkeys = jax.random.split(key, 3)
    grid_shape = (4, FINE_DEV * DEVICES)
    category = jax.random.randint(subkeys[0], grid_shape, 0, 10)
    nearby = jax.random.randint(subkeys[1], grid_shape, 0, 4 * FINE_DEV)
    remote = jax.random.randint(subkeys[2], grid_shape, 0, 4 * PB)
    result = jnp.where(category < 6, nearby, jnp.where(category == 6, 4 * FINE_DEV + remote, jnp.where(category == 7, 4 * FINE_DEV + 4 * PB + remote, 4 * FINE_DEV + 8 * PB)))
    return result.astype(jnp.int32)


def block_levels(own_key, dims, shards, smallest, largest):
    level, own = 1.0, jax.random.fold_in(own_key, 6)
    for dim, blocks in shards:
        heights = jnp.exp(jax.random.uniform(jax.random.fold_in(own, dim), (blocks,), jnp.float32, smallest / len(shards), largest / len(shards)))
        level = level * jnp.repeat(heights, dims[dim] // blocks).reshape([-1 if axis == dim else 1 for axis in range(len(dims))])
    return level


def normal_values(own_key, dims, deviation, bound, cuts=(), held_as=jnp.bfloat16):
    entries = deviation * jax.random.normal(own_key, dims, jnp.float32)
    if cuts:
        entries = entries * block_levels(own_key, dims, cuts, -0.22, 0.18)
    return jnp.clip(entries, -bound, bound).astype(held_as)


def setup_inputs(seed: int = 0) -> dict:
    streams_of = jax.random.split(jax.random.key(seed), 12)
    return {
        "fields": normal_values(streams_of[0], (6, NP, ELEMENTS), 1.0, 6.0, ((2, 512),), jnp.float32),
        "geometry": normal_values(streams_of[1], (9, ELEMENTS), 0.8, 4.0, ((1, 512),), jnp.float32),
        "normals": normal_values(streams_of[2], (3, 4, ELEMENTS), 0.6, 3.0, ((2, 512),), jnp.float32),
        "face_scale": jnp.clip(jnp.exp(math.log(3.0) - 1.7917595 * jax.random.uniform(streams_of[3], (4, ELEMENTS), jnp.float32) ** block_levels(streams_of[3], (4, ELEMENTS), ((1, 512),), -0.2, 0.2)), 0.5, 3.0),
        "derivatives": normal_values(streams_of[4], (3, NP, NP), NP ** -0.5, 1.25, (), jnp.float32),
        "lift_matrix": normal_values(streams_of[5], (NP, 4 * NFP), (4 * NFP) ** -0.5, 1.0, (), jnp.float32),
        "face_nbr": draw_face_nbr(jax.random.fold_in(streams_of[11], 71), 0),
        "send_rows": draw_send_rows(jax.random.fold_in(streams_of[11], 71), 0),
        "fine_slots": draw_fine_slots(jax.random.fold_in(streams_of[11], 71), 0),
        "export_rows": draw_export_rows(jax.random.fold_in(streams_of[11], 71), 0),
        "fine_nbr": draw_fine_nbr(jax.random.fold_in(streams_of[11], 71), 0),
    }


coarse_step = 0.2
highest = lax.Precision.HIGHEST


def face_table():
    places = [(along_r, along_s, along_t) for along_t in range(4) for along_s in range(4 - along_t) for along_r in range(4 - along_t - along_s)]
    bottom_face = [number for number, location in enumerate(places) if location[2] == 0]
    front_face = [number for number, location in enumerate(places) if location[1] == 0]
    slanted = [number for number, location in enumerate(places) if location[0] + location[1] + location[2] == 3]
    beside = [number for number, location in enumerate(places) if location[0] == 0]
    return np.array([bottom_face, front_face, slanted, beside], dtype=np.int32).T


def traces_of(vector_field, face_nodes):
    return vector_field[:, face_nodes, :]


def curl_of(vector_field, geometry, derivatives):
    local_grad = jnp.einsum('apq,cqe->acpe', derivatives, vector_field, precision=highest)
    factors = geometry.reshape(3, 3, geometry.shape[-1])

    def derivative(axis_out, component):
        return factors[axis_out, 0] * local_grad[0, component] + factors[axis_out, 1] * local_grad[1, component] + factors[axis_out, 2] * local_grad[2, component]

    return jnp.stack([derivative(1, 2) - derivative(2, 1), derivative(2, 0) - derivative(0, 2), derivative(0, 1) - derivative(1, 0)])


def cross_product(normals, jump_values):
    return jnp.stack([normals[1] * jump_values[2] - normals[2] * jump_values[1], normals[2] * jump_values[0] - normals[0] * jump_values[2], normals[0] * jump_values[1] - normals[1] * jump_values[0]])


def lift_of(lift_matrix, face_scale, flux_values):
    scaled = flux_values * face_scale
    shaped = lift_matrix.reshape(lift_matrix.shape[0], 4, lift_matrix.shape[1] // 4)
    return 0.5 * jnp.einsum('pfn,cnfe->cpe', shaped, scaled, precision=highest)


def magnetic_rate(curl_e, efield, outside, normals, face_scale, lift_matrix, face_nodes):
    jump_values = outside - traces_of(efield, face_nodes)
    return -curl_e - lift_of(lift_matrix, face_scale, cross_product(normals, jump_values))


def electric_rate(curl_h, hfield, outside, normals, face_scale, lift_matrix, face_nodes):
    jump_values = outside - traces_of(hfield, face_nodes)
    return curl_h + lift_of(lift_matrix, face_scale, cross_product(normals, jump_values))


def global_faces(face_nbr):
    element = jnp.arange(ELEMENTS, dtype=jnp.int32)[None, :]
    device = element // CE
    quarter = face_nbr // 4
    target = jnp.where(face_nbr < 4 * CE, device * CE + quarter,
                       jnp.where(face_nbr < 4 * CE + 4 * NB, ((device - 1) % DEVICES) * CE + CE - NB + quarter - CE,
                                 ((device + 1) % DEVICES) * CE + quarter - CE - NB))
    wall = face_nbr == 4 * (element % CE) + jnp.arange(4, dtype=jnp.int32)[:, None]
    return (face_nbr % 4) * ELEMENTS + target, wall


def exterior_global(vector_field, flat_index, wall, mirror_sign, face_nodes):
    interior = traces_of(vector_field, face_nodes)
    flat_traces = interior.reshape(vector_field.shape[0], interior.shape[1], 4 * vector_field.shape[2])
    return jnp.where(wall, mirror_sign * interior, flat_traces[:, :, flat_index])


def reference(fields, geometry, normals, face_scale, derivatives, lift_matrix, face_nbr, send_rows, fine_slots, export_rows, fine_nbr):
    face_nodes = face_table()
    flat_index, wall = global_faces(face_nbr)
    fine_index = jnp.arange(FINE_TOT, dtype=jnp.int32)
    receiver = fine_index // FINE_DEV
    source = (fine_slots // CAP) * N_SUB + receiver % N_SUB
    source_row = send_rows[source * SLOTS + (receiver // N_SUB) * CAP + fine_slots % CAP]
    fine_elements = source * CE + source_row
    held_e = exterior_global(fields[:3], flat_index, wall, -1.0, face_nodes)[..., fine_elements]
    held_h = exterior_global(fields[3:], flat_index, wall, 1.0, face_nodes)[..., fine_elements]

    local_end = 4 * FINE_DEV
    remote_span = 4 * PB
    below_dev = ((receiver - 1) % DEVICES)[None, :]
    above_dev = ((receiver + 1) % DEVICES)[None, :]
    first_part = jnp.clip(fine_nbr - local_end, 0, remote_span - 1)
    second_part = jnp.clip(fine_nbr - local_end - remote_span, 0, remote_span - 1)
    below_row = export_rows[1][below_dev * PB + first_part // 4]
    above_row = export_rows[0][above_dev * PB + second_part // 4]
    nearby_face = fine_nbr < local_end
    lower_side = fine_nbr < local_end + remote_span
    target = jnp.where(nearby_face, receiver[None, :] * FINE_DEV + fine_nbr // 4,
                       jnp.where(lower_side, below_dev * FINE_DEV + below_row, above_dev * FINE_DEV + above_row))
    target_face = jnp.where(nearby_face, fine_nbr % 4, jnp.where(lower_side, first_part % 4, second_part % 4))
    fine_flat_index = target_face * FINE_TOT + target
    frozen = fine_nbr == local_end + 2 * remote_span

    def fine_outside(vector_field, held_part):
        flat_traces = traces_of(vector_field, face_nodes).reshape(3, NFP, 4 * FINE_TOT)
        return jnp.where(frozen, held_part, flat_traces[:, :, fine_flat_index])

    geometry_fine = geometry[:, fine_elements]
    normals_fine = normals[:, :, fine_elements]
    scale_fine = face_scale[:, fine_elements]
    efield = fields[:3][:, :, fine_elements]
    hfield = fields[3:][:, :, fine_elements]
    fine_step = coarse_step / SUBSTEPS
    for substep in range(SUBSTEPS):
        outside = fine_outside(efield, held_e)
        hfield = hfield + fine_step * magnetic_rate(curl_of(efield, geometry_fine, derivatives), efield, outside, normals_fine, scale_fine, lift_matrix, face_nodes)
        outside = fine_outside(hfield, held_h)
        efield = efield + fine_step * electric_rate(curl_of(hfield, geometry_fine, derivatives), hfield, outside, normals_fine, scale_fine, lift_matrix, face_nodes)
    merged = fields.at[:, :, fine_elements].set(jnp.concatenate([efield, hfield]))

    efield = merged[:3]
    hfield = merged[3:]
    outside = exterior_global(efield, flat_index, wall, -1.0, face_nodes)
    hfield = hfield + coarse_step * magnetic_rate(curl_of(efield, geometry, derivatives), efield, outside, normals, face_scale, lift_matrix, face_nodes)
    outside = exterior_global(hfield, flat_index, wall, 1.0, face_nodes)
    efield = efield + coarse_step * electric_rate(curl_of(hfield, geometry, derivatives), hfield, outside, normals, face_scale, lift_matrix, face_nodes)
    return jnp.concatenate([efield, hfield])
```

```python
import functools

import jax
import jax.numpy as jnp
import numpy as np
from jax import lax
from jax.experimental import pallas as pl
from jax.experimental.pallas import tpu as pltpu
from jax.sharding import PartitionSpec as P

SUBSTEPS = 4
COARSE_STEP = 0.2
FINE_STEP = COARSE_STEP / SUBSTEPS
LANES = 128
VMEM_BYTES = 48 * 2**20
RING = ("dom", "sub")
highest = lax.Precision.HIGHEST


def face_table():
    places = [
        (along_r, along_s, along_t)
        for along_t in range(4)
        for along_s in range(4 - along_t)
        for along_r in range(4 - along_t - along_s)
    ]
    bottom = [i for i, at in enumerate(places) if at[2] == 0]
    front = [i for i, at in enumerate(places) if at[1] == 0]
    slanted = [i for i, at in enumerate(places) if sum(at) == 3]
    beside = [i for i, at in enumerate(places) if at[0] == 0]
    return [bottom, front, slanted, beside]


def runs_of(nodes):
    runs = []
    for place, node in enumerate(nodes):
        if runs and runs[-1][1] + runs[-1][2] == node:
            runs[-1][2] += 1
        else:
            runs.append([place, node, 1])
    return runs


RUNS = [runs_of(nodes) for nodes in face_table()]


def take(block, lane):
    return jnp.take_along_axis(block, lane, axis=1, mode="promise_in_bounds")


def rows8(row):
    return jnp.broadcast_to(row, (8, LANES))


def lanes_at(block):
    if isinstance(block, int):
        return slice(block * LANES, (block + 1) * LANES)
    return pl.ds(pl.multiple_of(block * LANES, LANES), LANES)


def gather32(sources, which, lane, start):
    groups = list(start)
    for number, source in enumerate(sources):
        hit = which == number
        for group in range(4):
            groups[group] = jnp.where(hit, take(source(group), lane), groups[group])
    return groups


def spread_normals(normal_rows, out_ref):
    for c in range(3):
        for f in range(4):
            out_ref[c, f * 10 : f * 10 + 10, :] = jnp.broadcast_to(normal_rows(c, f), (10, LANES))


def regroup(jump_ref, sorted_ref):
    for f in range(4):
        for c in range(3):
            sorted_ref[c, f * 10 : f * 10 + 10, :] = jump_ref[f, c * 10 : c * 10 + 10, :]


def crossed(normals, jumps):
    def part(c):
        a, b = (c + 1) % 3, (c + 2) % 3
        return normals[a] * jumps[b] - normals[b] * jumps[a]

    return [part(c) for c in range(3)]


def curl_part(c, factor, grad):
    m, n = (c + 1) % 3, (c + 2) % 3
    total = factor(m, 0) * grad(0, n) - factor(n, 0) * grad(0, m)
    for a in (1, 2):
        total += factor(m, a) * grad(a, n) - factor(n, a) * grad(a, m)
    return total


def stack_derivatives(derivatives_ref, out_ref):
    out_ref[...] = jnp.zeros_like(out_ref)
    for a in range(3):
        out_ref[a * 24 : a * 24 + 20, :] = derivatives_ref[a]


def dot(a, b):
    return jnp.dot(a, b, precision=highest, preferred_element_type=jnp.float32)


def inverse_of(row_of, count, width, none):
    columns = [
        jnp.transpose(jnp.broadcast_to(row_of(b), (LANES, LANES))) for b in range(count)
    ]
    lane = lax.broadcasted_iota(jnp.int32, (LANES, LANES), 1)
    number = lax.broadcasted_iota(jnp.int32, (LANES, LANES), 0)
    out = []
    for w in range(width):
        best = jnp.full((LANES, LANES), none, jnp.int32)
        for b in range(count):
            best = jnp.maximum(
                best, jnp.where(columns[b] == lane + w * LANES, number + b * LANES, none)
            )
        out.append(jnp.max(best, axis=0, keepdims=True))
    return out


def pack_kernel(
    fields_ref, geometry_ref, normals_ref, scale_ref, nbr_ref, send_ref,
    out_ref, ends_ref, home_ref,
    flat_ref, nb_ref, pool_ref, feature_ref,
):
    own = fields_ref.shape[2]
    for c in range(6):
        flat_ref[c * 20 : c * 20 + 20, :] = fields_ref[c]
    flat_ref[120:129, :] = geometry_ref[...]
    for c in range(3):
        flat_ref[129 + 4 * c : 133 + 4 * c, :] = normals_ref[c] * scale_ref[...]
    flat_ref[141:144, :] = jnp.zeros((3, own), jnp.float32)
    nb_ref[0:4, :] = nbr_ref[...]
    nb_ref[4:8, :] = nbr_ref[...]
    low_half = lax.broadcasted_iota(jnp.int32, (20, LANES), 1) < LANES // 2
    for c in range(3):
        ends_ref[c * 20 : c * 20 + 20, :] = jnp.where(
            low_half, fields_ref[c, :, 0:LANES], fields_ref[c, :, own - LANES : own]
        )
    ends_ref[60:64, :] = jnp.zeros((4, LANES), jnp.float32)
    for eh in range(2):
        for f in range(4):
            for c in range(3):
                for place, node, length in RUNS[f]:
                    pool_ref[eh, f, c * 10 + place : c * 10 + place + length, :] = fields_ref[
                        eh * 3 + c, node : node + length, :
                    ]
            pool_ref[eh, f, 30:32, :] = jnp.zeros((2, own), jnp.float32)
    blocks = own // LANES
    sublane = lax.broadcasted_iota(jnp.int32, (8, LANES), 0)

    def slots(sb, carry):
        row = rows8(jnp.minimum(send_ref[pl.ds(sb, 1), :], own - 1))
        lane, which = row & (LANES - 1), row >> 7
        hits = [which == b for b in range(blocks)]
        for group in range(18):
            value = take(flat_ref[group * 8 : group * 8 + 8, 0:LANES], lane)
            for b in range(1, blocks):
                value = jnp.where(
                    hits[b], take(flat_ref[group * 8 : group * 8 + 8, lanes_at(b)], lane), value
                )
            feature_ref[group * 8 : group * 8 + 8, lanes_at(sb)] = value
        nbr = take(nb_ref[:, 0:LANES], lane)
        for b in range(1, blocks):
            nbr = jnp.where(hits[b], take(nb_ref[:, lanes_at(b)], lane), nbr)
        wall = jnp.where(nbr == 4 * row + sublane, -1.0, 1.0)
        for f in range(4):
            code = rows8(nbr[f : f + 1, :])
            sign = rows8(wall[f : f + 1, :])
            lane_f = (code >> 2) & (LANES - 1)
            which_f = (code & 3) * blocks + (code >> 9)
            groups = [jnp.zeros((8, LANES), jnp.float32)] * 8
            for number in range(4 * blocks):
                hit = which_f == number
                for group in range(8):
                    block = pool_ref[
                        group // 4,
                        number // blocks,
                        group % 4 * 8 : group % 4 * 8 + 8,
                        lanes_at(number % blocks),
                    ]
                    groups[group] = jnp.where(hit, take(block, lane_f), groups[group])
            for group in range(8):
                value = groups[group] * sign if group < 4 else groups[group]
                length = 8 if group % 4 < 3 else 6
                at = 144 + (group // 4 * 4 + f) * 30 + group % 4 * 8
                feature_ref[at : at + length, lanes_at(sb)] = value[:length]
        return carry

    lax.fori_loop(0, send_ref.shape[0], slots, 0)
    out_ref[...] = jnp.transpose(feature_ref[...])
    homes = inverse_of(lambda b: send_ref[b : b + 1, :], send_ref.shape[0], blocks, -1)
    for b in range(blocks):
        home_ref[b : b + 1, :] = homes[b]


def fine_pool(state_ref, pool_ref):
    for f in range(4):
        for c in range(3):
            for place, node, length in RUNS[f]:
                pool_ref[f, c * 10 + place : c * 10 + place + length, :] = state_ref[
                    node : node + length, lanes_at(c)
                ]
        pool_ref[f, 30:32, :] = jnp.zeros((2, LANES), jnp.float32)


def exported(pool_ref, lane):
    face = lax.broadcasted_iota(jnp.int32, (8, LANES), 1) & 3
    zero = jnp.zeros((8, LANES), jnp.float32)
    return gather32(
        [lambda g, f=f: pool_ref[f, g * 8 : g * 8 + 8, :] for f in range(4)], face, lane, [zero] * 4
    )


def unpack_kernel(
    received_ref, slots_ref, nbr_ref, export_ref, ends_ref,
    efield_ref, hfield_ref, normal_ref, geometry_ref, held_ref, pool_ref, halo_ref, lane_ref,
    back_ref,
    feature_ref, picked_ref, small_ref,
):
    slot_blocks = received_ref.shape[0] // LANES
    feature_ref[...] = jnp.transpose(received_ref[...])
    slot = rows8(slots_ref[...])
    lane, which = slot & (LANES - 1), slot >> 7
    hits = [which == b for b in range(slot_blocks)]
    for group in range(feature_ref.shape[0] // 8):
        at = slice(group * 8, group * 8 + 8)
        value = take(feature_ref[at, 0:LANES], lane)
        for b in range(1, slot_blocks):
            value = jnp.where(hits[b], take(feature_ref[at, lanes_at(b)], lane), value)
        picked_ref[at, :] = value
    for c in range(3):
        efield_ref[:, lanes_at(c)] = picked_ref[c * 20 : c * 20 + 20, :]
        hfield_ref[:, lanes_at(c)] = picked_ref[60 + c * 20 : 80 + c * 20, :]
    geometry_ref[...] = picked_ref[120:136, :]
    spread_normals(
        lambda c, f: picked_ref[129 + 4 * c + f : 130 + 4 * c + f, :], normal_ref
    )
    frozen_code = 4 * LANES + 4 * 2 * export_ref.shape[1]
    for f in range(4):
        frozen = jnp.broadcast_to(nbr_ref[f : f + 1, :] == frozen_code, (30, LANES))
        for eh in range(2):
            at = 144 + (eh * 4 + f) * 30
            held_ref[eh, f, 0:30, :] = jnp.where(frozen, picked_ref[at : at + 30, :], 0.0)
            held_ref[eh, f, 30:32, :] = jnp.zeros((2, LANES), jnp.float32)
    width = export_ref.shape[1]
    small_ref[...] = jnp.zeros_like(small_ref)
    small_ref[0:2, 0:width] = export_ref[...]
    place = lax.broadcasted_iota(jnp.int32, (8, LANES), 1)
    both = take(small_ref[...], (place >> 2) & (width - 1))
    lane_ref[...] = jnp.where(place < LANES // 2, rows8(both[1:2, :]), rows8(both[0:1, :]))
    fine_pool(efield_ref, pool_ref)
    groups = exported(pool_ref, lane_ref[...])
    for g in range(4):
        halo_ref[g * 8 : g * 8 + 8, :] = groups[g]
    halo_ref[32:96, :] = ends_ref[...]
    backs = inverse_of(lambda b: slots_ref[...], 1, slot_blocks, 0)
    for b in range(slot_blocks):
        back_ref[b : b + 1, :] = backs[b]


def fine_rate(
    source_ref, pool_ref, low_ref, high_ref, held_ref, normal_ref, geometry_ref, nbr_ref,
    derivatives_ref, lift_ref,
    stack_ref, jump_ref, sorted_ref, flux_ref,
):
    stack_derivatives(derivatives_ref, stack_ref)
    grads = dot(stack_ref[...], source_ref[...])
    half = lax.broadcasted_iota(jnp.int32, (8, LANES), 1) < LANES // 2
    halo = [
        jnp.where(half, low_ref[g * 8 : g * 8 + 8, :], high_ref[g * 8 : g * 8 + 8, :])
        for g in range(4)
    ]
    sources = [lambda g, f=f: pool_ref[f, g * 8 : g * 8 + 8, :] for f in range(4)]
    sources.append(lambda g: halo[g])
    for f in range(4):
        code = rows8(nbr_ref[f : f + 1, :])
        local = code < 4 * LANES
        which = jnp.where(local, code & 3, code >> 7)
        lane = jnp.where(local, code >> 2, code) & (LANES - 1)
        groups = gather32(
            sources, which, lane, [held_ref[f, g * 8 : g * 8 + 8, :] for g in range(4)]
        )
        for g in range(4):
            jump_ref[f, g * 8 : g * 8 + 8, :] = groups[g] - pool_ref[f, g * 8 : g * 8 + 8, :]
    regroup(jump_ref, sorted_ref)
    flux = crossed([normal_ref[c] for c in range(3)], [sorted_ref[c] for c in range(3)])
    for c in range(3):
        flux_ref[:, lanes_at(c)] = flux[c]
    lifted = dot(0.5 * lift_ref[...], flux_ref[...])

    def factor(m, a):
        return geometry_ref[3 * m + a : 3 * m + a + 1, :]

    def grad(a, c):
        return grads[a * 24 : a * 24 + 20, c * LANES : (c + 1) * LANES]

    return [
        curl_part(c, factor, grad) + lifted[:, c * LANES : (c + 1) * LANES] for c in range(3)
    ]


def fine_kernel(
    magnetic,
    source_ref, target_ref, pool_ref, low_ref, high_ref, held_ref, normal_ref, geometry_ref,
    nbr_ref, lane_ref, derivatives_ref, lift_ref,
    out_ref, new_pool_ref, halo_ref,
    *scratch,
):
    field = 0 if magnetic else 1
    step = -FINE_STEP if magnetic else FINE_STEP
    rate = fine_rate(
        source_ref, pool_ref, low_ref, high_ref, held_ref.at[field], normal_ref, geometry_ref,
        nbr_ref, derivatives_ref, lift_ref, *scratch,
    )
    for c in range(3):
        out_ref[:, lanes_at(c)] = target_ref[:, lanes_at(c)] + step * rate[c]
    fine_pool(out_ref, new_pool_ref)
    groups = exported(new_pool_ref, lane_ref[...])
    for g in range(4):
        halo_ref[g * 8 : g * 8 + 8, :] = groups[g]


def last_fine_kernel(
    source_ref, target_ref, pool_ref, low_ref, high_ref, held_ref, normal_ref, geometry_ref,
    nbr_ref, back_ref, derivatives_ref, lift_ref,
    out_ref,
    result_ref, feature_ref,
    *scratch,
):
    rate = fine_rate(
        source_ref, pool_ref, low_ref, high_ref, held_ref.at[1], normal_ref, geometry_ref,
        nbr_ref, derivatives_ref, lift_ref, *scratch,
    )
    for c in range(3):
        result_ref[c * 20 : c * 20 + 20, :] = target_ref[:, lanes_at(c)] + FINE_STEP * rate[c]
        result_ref[60 + c * 20 : 80 + c * 20, :] = source_ref[:, lanes_at(c)]
    result_ref[120:128, :] = jnp.zeros((8, LANES), jnp.float32)
    for b in range(back_ref.shape[0]):
        lane = rows8(back_ref[b : b + 1, :])
        for g in range(16):
            feature_ref[g * 8 : g * 8 + 8, lanes_at(b)] = take(
                result_ref[g * 8 : g * 8 + 8, :], lane
            )
    out_ref[...] = jnp.transpose(feature_ref[...])


def coarse_pool(field_ref, first, pool_ref):
    own = field_ref.shape[2]
    for f in range(4):
        for c in range(3):
            for place, node, length in RUNS[f]:
                pool_ref[f, c * 10 + place : c * 10 + place + length, 0:own] = field_ref[
                    first + c, node : node + length, :
                ]


def halo_rows(below, above):
    half = lax.broadcasted_iota(jnp.int32, below.shape, 1) >= LANES // 2
    return pltpu.roll(jnp.where(half, below, above), LANES // 2, 1)


def coarse_halo(halo, store):
    for f in range(4):
        for c in range(3):
            for place, node, length in RUNS[f]:
                store(f, c * 10 + place, length, halo[c * 20 + node : c * 20 + node + length, :])


def coarse_flux(
    blocks, mirror, nbr_ref, normals_ref, scale_ref, pool_ref, flux_ref, jump_ref, sorted_ref,
    spread_ref,
):
    own_blocks = flux_ref.shape[2] // LANES
    sources = [
        lambda g, n=n: pool_ref[n // blocks, g * 8 : g * 8 + 8, lanes_at(n % blocks)]
        for n in range(4 * blocks)
    ]
    lane_number = lax.broadcasted_iota(jnp.int32, (8, LANES), 1)
    zero = jnp.zeros((8, LANES), jnp.float32)

    def one(eb, carry):
        at = lanes_at(eb)
        for f in range(4):
            code = rows8(nbr_ref[f : f + 1, at])
            block = code >> 9
            which = jnp.where(block < blocks, (code & 3) * blocks + block, 4 * blocks)
            groups = gather32(sources, which, (code >> 2) & (LANES - 1), [zero] * 4)
            if mirror:
                wall = code == 4 * (lane_number + eb * LANES) + f
                sign = jnp.where(wall, -1.0, 1.0)
                groups = [group * sign for group in groups]
            for g in range(4):
                jump_ref[f, g * 8 : g * 8 + 8, :] = (
                    groups[g] - pool_ref[f, g * 8 : g * 8 + 8, at]
                )
        regroup(jump_ref, sorted_ref)
        scale = scale_ref[:, at]
        scaled = [normals_ref[c, :, at] * scale for c in range(3)]
        spread_normals(lambda c, f: scaled[c][f : f + 1, :], spread_ref)
        flux = crossed([spread_ref[c] for c in range(3)], [sorted_ref[c] for c in range(3)])
        for c in range(3):
            flux_ref[c, :, at] = flux[c]
        return carry

    lax.fori_loop(0, own_blocks, one, 0)


def coarse_update(
    step, source, target, out, geometry_ref, derivatives_ref, lift_ref, stack_ref, flux_ref,
    grad_ref, lifted_ref,
):
    own_blocks = flux_ref.shape[2] // LANES
    stack_derivatives(derivatives_ref, stack_ref)
    lift = 0.5 * lift_ref[...]
    for c in range(3):
        grad_ref[c] = dot(stack_ref[...], source(c))
        lifted_ref[c] = dot(lift, flux_ref[c])

    def one(eb, carry):
        at = lanes_at(eb)

        def factor(m, a):
            return geometry_ref[3 * m + a : 3 * m + a + 1, at]

        def grad(a, c):
            return grad_ref[c, a * 24 : a * 24 + 20, at]

        for c in range(3):
            out(c, at, target(c, at) + step * (curl_part(c, factor, grad) + lifted_ref[c, :, at]))
        return carry

    lax.fori_loop(0, own_blocks, one, 0)


def coarse_magnetic_kernel(
    returned_ref, home_ref, fields_ref, below_ref, above_ref, geometry_ref, normals_ref,
    scale_ref, nbr_ref, derivatives_ref, lift_ref,
    merged_ref, ends_ref,
    flat_ref, back_ref, pool_ref, flux_ref, jump_ref, sorted_ref, spread_ref, stack_ref,
    grad_ref, lifted_ref,
):
    own = fields_ref.shape[2]
    slot_blocks = returned_ref.shape[0] // LANES
    back_ref[...] = jnp.transpose(returned_ref[...])
    for c in range(6):
        flat_ref[c * 20 : c * 20 + 20, :] = fields_ref[c]

    def merge(eb, carry):
        at = lanes_at(eb)
        home = rows8(home_ref[pl.ds(eb, 1), :])
        lane = home & (LANES - 1)
        hits = [(home >> 7) == b for b in range(slot_blocks)]
        for group in range(15):
            rows = slice(group * 8, group * 8 + 8)
            value = flat_ref[rows, at]
            for b in range(slot_blocks):
                value = jnp.where(hits[b], take(back_ref[rows, lanes_at(b)], lane), value)
            flat_ref[rows, at] = value
        return carry

    lax.fori_loop(0, own // LANES, merge, 0)
    for c in range(6):
        merged_ref[c] = flat_ref[c * 20 : c * 20 + 20, :]
    coarse_pool(merged_ref, 0, pool_ref)
    halo = halo_rows(below_ref[32:96, :], above_ref[32:96, :])

    def store(f, place, length, value):
        pool_ref[f, place : place + length, own : own + LANES] = value

    coarse_halo(halo, store)
    coarse_flux(
        own // LANES + 1, True, nbr_ref, normals_ref, scale_ref, pool_ref, flux_ref, jump_ref,
        sorted_ref, spread_ref,
    )

    def out(c, at, value):
        merged_ref[3 + c, :, at] = value

    coarse_update(
        -COARSE_STEP, lambda c: merged_ref[c], lambda c, at: merged_ref[3 + c, :, at], out,
        geometry_ref, derivatives_ref, lift_ref, stack_ref, flux_ref, grad_ref, lifted_ref,
    )
    low_half = lax.broadcasted_iota(jnp.int32, (20, LANES), 1) < LANES // 2
    for c in range(3):
        ends_ref[c * 20 : c * 20 + 20, :] = jnp.where(
            low_half, merged_ref[3 + c, :, 0:LANES], merged_ref[3 + c, :, own - LANES : own]
        )
    ends_ref[60:64, :] = jnp.zeros((4, LANES), jnp.float32)


def coarse_electric_kernel(
    merged_ref, geometry_ref, normals_ref, scale_ref, nbr_ref, derivatives_ref, lift_ref,
    out_ref,
    pool_ref, flux_ref, jump_ref, sorted_ref, spread_ref, stack_ref, grad_ref, lifted_ref,
):
    own = merged_ref.shape[2]
    coarse_pool(merged_ref, 3, pool_ref)
    coarse_flux(
        own // LANES, False, nbr_ref, normals_ref, scale_ref, pool_ref, flux_ref, jump_ref,
        sorted_ref, spread_ref,
    )

    def out(c, at, value):
        out_ref[c, :, at] = value

    coarse_update(
        COARSE_STEP, lambda c: merged_ref[3 + c], lambda c, at: merged_ref[c, :, at], out,
        geometry_ref, derivatives_ref, lift_ref, stack_ref, flux_ref, grad_ref, lifted_ref,
    )


def finish_kernel(
    merged_ref, electric_ref, below_ref, above_ref, normals_ref, scale_ref, nbr_ref, lift_ref,
    out_ref,
    pool_ref, flux_ref, jump_ref, sorted_ref, spread_ref,
):
    own = merged_ref.shape[2]
    halo = halo_rows(below_ref[...], above_ref[...])

    def store(f, place, length, value):
        pool_ref[f, place : place + length, :] = value

    coarse_halo(halo, store)
    zero = jnp.zeros((8, LANES), jnp.float32)
    sources = [lambda g, f=f: pool_ref[f, g * 8 : g * 8 + 8, :] for f in range(4)]
    ends = (0, own // LANES - 1)
    for number, eb in enumerate(ends):
        at = lanes_at(eb)
        for f in range(4):
            code = rows8(nbr_ref[f : f + 1, at])
            which = jnp.where(code >= 4 * own, code & 3, 4)
            groups = gather32(sources, which, (code >> 2) & (LANES - 1), [zero] * 4)
            for g in range(4):
                jump_ref[f, g * 8 : g * 8 + 8, :] = groups[g]
        regroup(jump_ref, sorted_ref)
        scale = scale_ref[:, at]
        scaled = [normals_ref[c, :, at] * scale for c in range(3)]
        spread_normals(lambda c, f: scaled[c][f : f + 1, :], spread_ref)
        flux = crossed([spread_ref[c] for c in range(3)], [sorted_ref[c] for c in range(3)])
        for c in range(3):
            flux_ref[:, lanes_at(number * 3 + c)] = flux[c]
    lifted = dot(0.5 * lift_ref[...], flux_ref[...])
    for c in range(3):
        out_ref[c, :, LANES : own - LANES] = electric_ref[c, :, LANES : own - LANES]
        for number, eb in enumerate(ends):
            at = (number * 3 + c) * LANES
            out_ref[c, :, lanes_at(eb)] = (
                electric_ref[c, :, lanes_at(eb)] + COARSE_STEP * lifted[:, at : at + LANES]
            )
        out_ref[3 + c] = merged_ref[3 + c]


def call(kernel, outs, scratch, *args):
    whole = pl.BlockSpec(memory_space=pltpu.VMEM)
    return pl.pallas_call(
        kernel,
        out_shape=[jax.ShapeDtypeStruct(shape, dtype) for shape, dtype in outs],
        in_specs=[whole] * len(args),
        out_specs=[whole] * len(outs),
        scratch_shapes=[pltpu.VMEM(shape, dtype) for shape, dtype in scratch],
        compiler_params=pltpu.CompilerParams(vmem_limit_bytes=VMEM_BYTES),
    )(*args)


def exchange(block):
    count = lax.axis_size(RING)
    up = [(i, (i + 1) % count) for i in range(count)]
    down = [(target, source) for source, target in up]
    return lax.ppermute(block, RING, up), lax.ppermute(block, RING, down)


def swap_slots(rows, width):
    peers = lax.axis_size("dom")
    chunks = rows.reshape(peers, rows.shape[0] // peers, width)
    return lax.all_to_all(chunks, "dom", split_axis=0, concat_axis=0, tiled=True).reshape(
        rows.shape[0], width
    )


def per_device(
    fields, geometry, normals, face_scale, derivatives, lift_matrix, face_nbr, send_rows,
    fine_slots, export_rows, fine_nbr,
):
    f32, i32 = jnp.float32, jnp.int32
    own = fields.shape[2]
    slots = send_rows.shape[0]
    fine = fine_slots.shape[0]
    send = send_rows.reshape(slots // LANES, LANES)
    packed, ends, home = call(
        pack_kernel,
        [((slots, 384), f32), ((64, LANES), f32), ((own // LANES, LANES), i32)],
        [((144, own), f32), ((8, own), i32), ((2, 4, 32, own), f32), ((384, slots), f32)],
        fields, geometry, normals, face_scale, face_nbr, send,
    )
    received = swap_slots(packed, 384)
    state, traces = ((20, 3 * fine), f32), ((4, 32, fine), f32)
    efield, hfield, normal, factors, held, pool, halo, lane, back = call(
        unpack_kernel,
        [
            state, state, ((3, 40, fine), f32), ((16, fine), f32), ((2, 4, 32, fine), f32),
            traces, ((96, fine), f32), ((8, fine), i32), ((slots // LANES, LANES), i32),
        ],
        [((384, slots), f32), ((384, fine), f32), ((8, LANES), i32)],
        received, fine_slots.reshape(1, fine), fine_nbr, export_rows, ends,
    )
    scratch = [((72, 20), f32), traces, ((3, 40, fine), f32), ((40, 3 * fine), f32)]
    first = None
    for half in range(2 * SUBSTEPS - 1):
        below, above = exchange(halo)
        first = first or (below, above)
        magnetic = half % 2 == 0
        source, target = (efield, hfield) if magnetic else (hfield, efield)
        new, pool, halo = call(
            functools.partial(fine_kernel, magnetic),
            [state, traces, ((32, fine), f32)],
            scratch,
            source, target, pool, below, above, held, normal, factors, fine_nbr, lane,
            derivatives, lift_matrix,
        )
        efield, hfield = (efield, new) if magnetic else (new, hfield)
    below, above = exchange(halo)
    (outgoing,) = call(
        last_fine_kernel,
        [((slots, LANES), f32)],
        [((128, fine), f32), ((128, slots), f32)] + scratch,
        hfield, efield, pool, below, above, held, normal, factors, fine_nbr, back, derivatives,
        lift_matrix,
    )
    returned = swap_slots(outgoing, LANES)
    work = [
        ((3, 40, own), f32), ((4, 32, LANES), f32), ((3, 40, LANES), f32), ((3, 40, LANES), f32),
        ((72, 20), f32), ((3, 72, own), f32), ((3, 20, own), f32),
    ]
    merged, ends = call(
        coarse_magnetic_kernel,
        [((6, 20, own), f32), ((64, LANES), f32)],
        [((120, own), f32), ((128, slots), f32), ((4, 32, own + LANES), f32)] + work,
        returned, home, fields, first[0], first[1], geometry, normals, face_scale, face_nbr,
        derivatives, lift_matrix,
    )
    below, above = exchange(ends)
    (electric,) = call(
        coarse_electric_kernel,
        [((3, 20, own), f32)],
        [((4, 32, own), f32)] + work,
        merged, geometry, normals, face_scale, face_nbr, derivatives, lift_matrix,
    )
    (out,) = call(
        finish_kernel,
        [((6, 20, own), f32)],
        [
            traces, ((40, 6 * LANES), f32), ((4, 32, LANES), f32), ((3, 40, LANES), f32),
            ((3, 40, LANES), f32),
        ],
        merged, electric, below, above, normals, face_scale, face_nbr, lift_matrix,
    )
    return out


def solution(mesh):
    return jax.shard_map(
        per_device,
        mesh=mesh,
        in_specs=(
            P(None, None, ("dom", "sub")),
            P(None, ("dom", "sub")),
            P(None, None, ("dom", "sub")),
            P(None, ("dom", "sub")),
            P(),
            P(),
            P(None, ("dom", "sub")),
            P(("dom", "sub")),
            P(("dom", "sub")),
            P(None, ("dom", "sub")),
            P(None, ("dom", "sub")),
        ),
        out_specs=P(None, None, ("dom", "sub")),
        check_vma=False,
    )
```

```python
import functools

import jax
import jax.numpy as jnp
import numpy as np
from jax import lax
from jax.experimental import pallas as pl
from jax.experimental.pallas import tpu as pltpu
from jax.sharding import PartitionSpec as P

SUBSTEPS = 4
COARSE_STEP = 0.2
FINE_STEP = COARSE_STEP / SUBSTEPS
LANES = 128
VMEM_BYTES = 40 * 2**20
PACK_VMEM_BYTES = 60 * 2**20
RING = ("dom", "sub")
highest = lax.Precision.HIGHEST


def face_table():
    places = [
        (along_r, along_s, along_t)
        for along_t in range(4)
        for along_s in range(4 - along_t)
        for along_r in range(4 - along_t - along_s)
    ]
    bottom = [i for i, at in enumerate(places) if at[2] == 0]
    front = [i for i, at in enumerate(places) if at[1] == 0]
    slanted = [i for i, at in enumerate(places) if sum(at) == 3]
    beside = [i for i, at in enumerate(places) if at[0] == 0]
    return [bottom, front, slanted, beside]


def runs_of(nodes):
    runs = []
    for place, node in enumerate(nodes):
        if runs and runs[-1][1] + runs[-1][2] == node:
            runs[-1][2] += 1
        else:
            runs.append([place, node, 1])
    return runs


RUNS = [runs_of(nodes) for nodes in face_table()]


def seat(block, rows, columns):
    chip, core = block // 2, block % 2
    y, z = chip // columns, chip % columns
    if y % 2:
        z, core = columns - 1 - z, 1 - core
    return (y * columns + z) * 2 + core


def seats(count):
    chips = count // 2
    rows = max(r for r in range(1, chips + 1) if chips % r == 0 and r * r <= chips)
    return np.array([seat(block, rows, chips // rows) for block in range(count)], np.int32)


def slot_order(count, cap):
    block_at = np.argsort(seats(count))
    return (block_at[:, None] * cap + np.arange(cap)[None, :]).reshape(-1).astype(np.int32)


def take(block, lane):
    return jnp.take_along_axis(block, lane, axis=1, mode="promise_in_bounds")


def rows8(row):
    return jnp.broadcast_to(row, (8, LANES))


def lanes_at(block):
    if isinstance(block, int):
        return slice(block * LANES, (block + 1) * LANES)
    return pl.ds(pl.multiple_of(block * LANES, LANES), LANES)


def gather32(sources, which, lane, start):
    groups = list(start)
    for number, source in enumerate(sources):
        hit = which == number
        for group in range(4):
            groups[group] = jnp.where(hit, take(source(group), lane), groups[group])
    return groups


def spread_normals(normal_rows, out_ref):
    for c in range(3):
        for f in range(4):
            out_ref[c, f * 10 : f * 10 + 10, :] = jnp.broadcast_to(normal_rows(c, f), (10, LANES))


def regroup(jump_ref, sorted_ref):
    for f in range(4):
        for c in range(3):
            sorted_ref[c, f * 10 : f * 10 + 10, :] = jump_ref[f, c * 10 : c * 10 + 10, :]


def crossed(normals, jumps):
    def part(c):
        a, b = (c + 1) % 3, (c + 2) % 3
        return normals[a] * jumps[b] - normals[b] * jumps[a]

    return [part(c) for c in range(3)]


def curl_part(c, factor, grad):
    m, n = (c + 1) % 3, (c + 2) % 3
    total = factor(m, 0) * grad(0, n) - factor(n, 0) * grad(0, m)
    for a in (1, 2):
        total += factor(m, a) * grad(a, n) - factor(n, a) * grad(a, m)
    return total


def stack_derivatives(derivatives_ref, out_ref):
    out_ref[...] = jnp.zeros_like(out_ref)
    for a in range(3):
        out_ref[a * 24 : a * 24 + 20, :] = derivatives_ref[a]


def dot(a, b):
    return jnp.dot(a, b, precision=highest, preferred_element_type=jnp.float32)


def inverse_of(row_of, count, width, none):
    columns = [
        jnp.transpose(jnp.broadcast_to(row_of(b), (LANES, LANES))) for b in range(count)
    ]
    lane = lax.broadcasted_iota(jnp.int32, (LANES, LANES), 1)
    number = lax.broadcasted_iota(jnp.int32, (LANES, LANES), 0)
    out = []
    for w in range(width):
        best = jnp.full((LANES, LANES), none, jnp.int32)
        for b in range(count):
            best = jnp.maximum(
                best, jnp.where(columns[b] == lane + w * LANES, number + b * LANES, none)
            )
        out.append(jnp.max(best, axis=0, keepdims=True))
    return out


def pack_kernel(
    plain_send_hbm, order_hbm, fields_hbm, nbr_hbm, geometry_hbm, normals_hbm, scale_hbm,
    out_ref, ends_ref, home_ref,
    plain_send_ref, order_ref, fields_ref, nbr_ref, geometry_ref, normals_ref, scale_ref,
    send_ref, flat_ref, nb_ref, pool_ref, feature_ref,
    *sems,
):
    pairs = [
        (plain_send_hbm, plain_send_ref), (order_hbm, order_ref), (fields_hbm, fields_ref),
        (nbr_hbm, nbr_ref), (geometry_hbm, geometry_ref), (normals_hbm, normals_ref),
        (scale_hbm, scale_ref),
    ]
    copies = [pltpu.make_async_copy(a, b, sem) for (a, b), sem in zip(pairs, sems)]
    for copy in copies:
        copy.start()
    copies[0].wait()
    copies[1].wait()
    own = fields_ref.shape[2]
    send_blocks = plain_send_ref.shape[0]
    for sb in range(send_blocks):
        order = rows8(order_ref[sb : sb + 1, :])
        row = jnp.zeros((8, LANES), jnp.int32)
        for b in range(send_blocks):
            block = take(rows8(plain_send_ref[b : b + 1, :]), order & (LANES - 1))
            row = jnp.where((order >> 7) == b, block, row)
        send_ref[sb : sb + 1, :] = row[0:1, :]
    homes = inverse_of(lambda b: send_ref[b : b + 1, :], send_blocks, own // LANES, -1)
    for b in range(own // LANES):
        home_ref[b : b + 1, :] = homes[b]
    for copy in copies[2:]:
        copy.wait()
    for c in range(6):
        flat_ref[c * 20 : c * 20 + 20, :] = fields_ref[c]
    flat_ref[120:129, :] = geometry_ref[...]
    for c in range(3):
        flat_ref[129 + 4 * c : 133 + 4 * c, :] = normals_ref[c] * scale_ref[...]
    flat_ref[141:144, :] = jnp.zeros((3, own), jnp.float32)
    nb_ref[0:4, :] = nbr_ref[...]
    nb_ref[4:8, :] = nbr_ref[...]
    low_half = lax.broadcasted_iota(jnp.int32, (20, LANES), 1) < LANES // 2
    for c in range(3):
        ends_ref[c * 20 : c * 20 + 20, :] = jnp.where(
            low_half, fields_ref[c, :, 0:LANES], fields_ref[c, :, own - LANES : own]
        )
    ends_ref[60:64, :] = jnp.zeros((4, LANES), jnp.float32)
    for eh in range(2):
        for f in range(4):
            for c in range(3):
                for place, node, length in RUNS[f]:
                    pool_ref[eh, f, c * 10 + place : c * 10 + place + length, :] = fields_ref[
                        eh * 3 + c, node : node + length, :
                    ]
            pool_ref[eh, f, 30:32, :] = jnp.zeros((2, own), jnp.float32)
    blocks = own // LANES
    sublane = lax.broadcasted_iota(jnp.int32, (8, LANES), 0)

    def slots(sb, carry):
        row = rows8(jnp.minimum(send_ref[pl.ds(sb, 1), :], own - 1))
        lane, which = row & (LANES - 1), row >> 7
        hits = [which == b for b in range(blocks)]
        for group in range(18):
            value = take(flat_ref[group * 8 : group * 8 + 8, 0:LANES], lane)
            for b in range(1, blocks):
                value = jnp.where(
                    hits[b], take(flat_ref[group * 8 : group * 8 + 8, lanes_at(b)], lane), value
                )
            feature_ref[group * 8 : group * 8 + 8, lanes_at(sb)] = value
        nbr = take(nb_ref[:, 0:LANES], lane)
        for b in range(1, blocks):
            nbr = jnp.where(hits[b], take(nb_ref[:, lanes_at(b)], lane), nbr)
        wall = jnp.where(nbr == 4 * row + sublane, -1.0, 1.0)
        for f in range(4):
            code = rows8(nbr[f : f + 1, :])
            sign = rows8(wall[f : f + 1, :])
            lane_f = (code >> 2) & (LANES - 1)
            which_f = (code & 3) * blocks + (code >> 9)
            groups = [jnp.zeros((8, LANES), jnp.float32)] * 8
            for number in range(4 * blocks):
                hit = which_f == number
                for group in range(8):
                    block = pool_ref[
                        group // 4,
                        number // blocks,
                        group % 4 * 8 : group % 4 * 8 + 8,
                        lanes_at(number % blocks),
                    ]
                    groups[group] = jnp.where(hit, take(block, lane_f), groups[group])
            for group in range(8):
                value = groups[group] * sign if group < 4 else groups[group]
                length = 8 if group % 4 < 3 else 6
                at = 144 + (group // 4 * 4 + f) * 30 + group % 4 * 8
                feature_ref[at : at + length, lanes_at(sb)] = value[:length]
        return carry

    lax.fori_loop(0, send_blocks, slots, 0)
    out_ref[...] = jnp.transpose(feature_ref[...])


def fine_pool(state_ref, pool_ref):
    for f in range(4):
        for c in range(3):
            for place, node, length in RUNS[f]:
                pool_ref[f, c * 10 + place : c * 10 + place + length, :] = state_ref[
                    node : node + length, lanes_at(c)
                ]
        pool_ref[f, 30:32, :] = jnp.zeros((2, LANES), jnp.float32)


def exported(pool_ref, lane):
    face = lax.broadcasted_iota(jnp.int32, (8, LANES), 1) & 3
    zero = jnp.zeros((8, LANES), jnp.float32)
    return gather32(
        [lambda g, f=f: pool_ref[f, g * 8 : g * 8 + 8, :] for f in range(4)], face, lane, [zero] * 4
    )


def unpack_kernel(
    width, received_ref, table_ref,
    efield_ref, hfield_ref, normal_ref, geometry_ref, held_ref, pool_ref, halo_ref, lane_ref,
    back_ref,
    feature_ref, picked_ref,
):
    nbr_ref, slots_ref = table_ref.at[0:4], table_ref.at[4:5]
    slot_blocks = received_ref.shape[0] // LANES
    feature_ref[...] = jnp.transpose(received_ref[...])
    slot = rows8(slots_ref[...])
    lane, which = slot & (LANES - 1), slot >> 7
    hits = [which == b for b in range(slot_blocks)]
    for group in range(feature_ref.shape[0] // 8):
        at = slice(group * 8, group * 8 + 8)
        value = take(feature_ref[at, 0:LANES], lane)
        for b in range(1, slot_blocks):
            value = jnp.where(hits[b], take(feature_ref[at, lanes_at(b)], lane), value)
        picked_ref[at, :] = value
    for c in range(3):
        efield_ref[:, lanes_at(c)] = picked_ref[c * 20 : c * 20 + 20, :]
        hfield_ref[:, lanes_at(c)] = picked_ref[60 + c * 20 : 80 + c * 20, :]
    geometry_ref[...] = picked_ref[120:136, :]
    spread_normals(
        lambda c, f: picked_ref[129 + 4 * c + f : 130 + 4 * c + f, :], normal_ref
    )
    frozen_code = 4 * LANES + 4 * 2 * width
    for f in range(4):
        frozen = jnp.broadcast_to(nbr_ref[f : f + 1, :] == frozen_code, (30, LANES))
        for eh in range(2):
            at = 144 + (eh * 4 + f) * 30
            held_ref[eh, f, 0:30, :] = jnp.where(frozen, picked_ref[at : at + 30, :], 0.0)
            held_ref[eh, f, 30:32, :] = jnp.zeros((2, LANES), jnp.float32)
    place = lax.broadcasted_iota(jnp.int32, (8, LANES), 1)
    both = take(table_ref[...], (place >> 2) & (width - 1))
    lane_ref[...] = jnp.where(place < LANES // 2, rows8(both[6:7, :]), rows8(both[5:6, :]))
    fine_pool(efield_ref, pool_ref)
    groups = exported(pool_ref, lane_ref[...])
    for g in range(4):
        halo_ref[g * 8 : g * 8 + 8, :] = groups[g]
    backs = inverse_of(lambda b: slots_ref[...], 1, slot_blocks, 0)
    for b in range(slot_blocks):
        back_ref[b : b + 1, :] = backs[b]


def fine_rate(
    source_ref, pool_ref, low_ref, high_ref, held_ref, normal_ref, geometry_ref, nbr_ref,
    derivatives_ref, lift_ref,
    stack_ref, jump_ref, sorted_ref, flux_ref,
):
    stack_derivatives(derivatives_ref, stack_ref)
    grads = dot(stack_ref[...], source_ref[...])
    half = lax.broadcasted_iota(jnp.int32, (8, LANES), 1) < LANES // 2
    halo = [
        jnp.where(half, low_ref[g * 8 : g * 8 + 8, :], high_ref[g * 8 : g * 8 + 8, :])
        for g in range(4)
    ]
    sources = [lambda g, f=f: pool_ref[f, g * 8 : g * 8 + 8, :] for f in range(4)]
    sources.append(lambda g: halo[g])
    for f in range(4):
        code = rows8(nbr_ref[f : f + 1, :])
        local = code < 4 * LANES
        which = jnp.where(local, code & 3, code >> 7)
        lane = jnp.where(local, code >> 2, code) & (LANES - 1)
        groups = gather32(
            sources, which, lane, [held_ref[f, g * 8 : g * 8 + 8, :] for g in range(4)]
        )
        for g in range(4):
            jump_ref[f, g * 8 : g * 8 + 8, :] = groups[g] - pool_ref[f, g * 8 : g * 8 + 8, :]
    regroup(jump_ref, sorted_ref)
    flux = crossed([normal_ref[c] for c in range(3)], [sorted_ref[c] for c in range(3)])
    for c in range(3):
        flux_ref[:, lanes_at(c)] = flux[c]
    lifted = dot(0.5 * lift_ref[...], flux_ref[...])

    def factor(m, a):
        return geometry_ref[3 * m + a : 3 * m + a + 1, :]

    def grad(a, c):
        return grads[a * 24 : a * 24 + 20, c * LANES : (c + 1) * LANES]

    return [
        curl_part(c, factor, grad) + lifted[:, c * LANES : (c + 1) * LANES] for c in range(3)
    ]


def fine_kernel(
    magnetic,
    source_ref, target_ref, pool_ref, low_ref, high_ref, held_ref, normal_ref, geometry_ref,
    nbr_ref, lane_ref, derivatives_ref, lift_ref,
    out_ref, new_pool_ref, halo_ref,
    *scratch,
):
    field = 0 if magnetic else 1
    step = -FINE_STEP if magnetic else FINE_STEP
    rate = fine_rate(
        source_ref, pool_ref, low_ref, high_ref, held_ref.at[field], normal_ref, geometry_ref,
        nbr_ref, derivatives_ref, lift_ref, *scratch,
    )
    for c in range(3):
        out_ref[:, lanes_at(c)] = target_ref[:, lanes_at(c)] + step * rate[c]
    fine_pool(out_ref, new_pool_ref)
    groups = exported(new_pool_ref, lane_ref[...])
    for g in range(4):
        halo_ref[g * 8 : g * 8 + 8, :] = groups[g]


def last_fine_kernel(
    source_ref, target_ref, pool_ref, low_ref, high_ref, held_ref, normal_ref, geometry_ref,
    nbr_ref, back_ref, derivatives_ref, lift_ref,
    out_ref,
    result_ref, feature_ref,
    *scratch,
):
    rate = fine_rate(
        source_ref, pool_ref, low_ref, high_ref, held_ref.at[1], normal_ref, geometry_ref,
        nbr_ref, derivatives_ref, lift_ref, *scratch,
    )
    for c in range(3):
        result_ref[c * 20 : c * 20 + 20, :] = target_ref[:, lanes_at(c)] + FINE_STEP * rate[c]
        result_ref[60 + c * 20 : 80 + c * 20, :] = source_ref[:, lanes_at(c)]
    result_ref[120:128, :] = jnp.zeros((8, LANES), jnp.float32)
    for b in range(back_ref.shape[0]):
        lane = rows8(back_ref[b : b + 1, :])
        for g in range(16):
            feature_ref[g * 8 : g * 8 + 8, lanes_at(b)] = take(
                result_ref[g * 8 : g * 8 + 8, :], lane
            )
    out_ref[...] = jnp.transpose(feature_ref[...])


def coarse_pool(field_ref, first, pool_ref):
    own = field_ref.shape[2]
    for f in range(4):
        for c in range(3):
            for place, node, length in RUNS[f]:
                pool_ref[f, c * 10 + place : c * 10 + place + length, 0:own] = field_ref[
                    first + c, node : node + length, :
                ]


def halo_rows(below, above):
    half = lax.broadcasted_iota(jnp.int32, below.shape, 1) >= LANES // 2
    return pltpu.roll(jnp.where(half, below, above), LANES // 2, 1)


def coarse_halo(halo, store):
    for f in range(4):
        for c in range(3):
            for place, node, length in RUNS[f]:
                store(f, c * 10 + place, length, halo[c * 20 + node : c * 20 + node + length, :])


def coarse_flux(
    blocks, mirror, nbr_ref, normals_ref, scale_ref, pool_ref, flux_ref, jump_ref, sorted_ref,
    spread_ref,
):
    own_blocks = flux_ref.shape[2] // LANES
    sources = [
        lambda g, n=n: pool_ref[n // blocks, g * 8 : g * 8 + 8, lanes_at(n % blocks)]
        for n in range(4 * blocks)
    ]
    lane_number = lax.broadcasted_iota(jnp.int32, (8, LANES), 1)
    zero = jnp.zeros((8, LANES), jnp.float32)

    def one(eb, carry):
        at = lanes_at(eb)
        for f in range(4):
            code = rows8(nbr_ref[f : f + 1, at])
            block = code >> 9
            which = jnp.where(block < blocks, (code & 3) * blocks + block, 4 * blocks)
            groups = gather32(sources, which, (code >> 2) & (LANES - 1), [zero] * 4)
            if mirror:
                wall = code == 4 * (lane_number + eb * LANES) + f
                sign = jnp.where(wall, -1.0, 1.0)
                groups = [group * sign for group in groups]
            for g in range(4):
                jump_ref[f, g * 8 : g * 8 + 8, :] = (
                    groups[g] - pool_ref[f, g * 8 : g * 8 + 8, at]
                )
        regroup(jump_ref, sorted_ref)
        scale = scale_ref[:, at]
        scaled = [normals_ref[c, :, at] * scale for c in range(3)]
        spread_normals(lambda c, f: scaled[c][f : f + 1, :], spread_ref)
        flux = crossed([spread_ref[c] for c in range(3)], [sorted_ref[c] for c in range(3)])
        for c in range(3):
            flux_ref[c, :, at] = flux[c]
        return carry

    lax.fori_loop(0, own_blocks, one, 0)


def coarse_update(
    step, source, target, out, geometry_ref, derivatives_ref, lift_ref, stack_ref, flux_ref,
    grad_ref, lifted_ref,
):
    own_blocks = flux_ref.shape[2] // LANES
    stack_derivatives(derivatives_ref, stack_ref)
    lift = 0.5 * lift_ref[...]
    for c in range(3):
        grad_ref[c] = dot(stack_ref[...], source(c))
        lifted_ref[c] = dot(lift, flux_ref[c])

    def one(eb, carry):
        at = lanes_at(eb)

        def factor(m, a):
            return geometry_ref[3 * m + a : 3 * m + a + 1, at]

        def grad(a, c):
            return grad_ref[c, a * 24 : a * 24 + 20, at]

        for c in range(3):
            out(c, at, target(c, at) + step * (curl_part(c, factor, grad) + lifted_ref[c, :, at]))
        return carry

    lax.fori_loop(0, own_blocks, one, 0)


def coarse_magnetic_kernel(
    returned_ref, home_ref, fields_ref, below_ref, above_ref, geometry_ref, normals_ref,
    scale_ref, nbr_ref, derivatives_ref, lift_ref,
    merged_ref, ends_ref,
    flat_ref, back_ref, pool_ref, flux_ref, jump_ref, sorted_ref, spread_ref, stack_ref,
    grad_ref, lifted_ref,
):
    own = fields_ref.shape[2]
    slot_blocks = returned_ref.shape[0] // LANES
    back_ref[...] = jnp.transpose(returned_ref[...])
    for c in range(6):
        flat_ref[c * 20 : c * 20 + 20, :] = fields_ref[c]

    def merge(eb, carry):
        at = lanes_at(eb)
        home = rows8(home_ref[pl.ds(eb, 1), :])
        lane = home & (LANES - 1)
        hits = [(home >> 7) == b for b in range(slot_blocks)]
        for group in range(15):
            rows = slice(group * 8, group * 8 + 8)
            value = flat_ref[rows, at]
            for b in range(slot_blocks):
                value = jnp.where(hits[b], take(back_ref[rows, lanes_at(b)], lane), value)
            flat_ref[rows, at] = value
        return carry

    lax.fori_loop(0, own // LANES, merge, 0)
    for c in range(6):
        merged_ref[c] = flat_ref[c * 20 : c * 20 + 20, :]
    coarse_pool(merged_ref, 0, pool_ref)
    halo = halo_rows(below_ref[...], above_ref[...])

    def store(f, place, length, value):
        pool_ref[f, place : place + length, own : own + LANES] = value

    coarse_halo(halo, store)
    coarse_flux(
        own // LANES + 1, True, nbr_ref, normals_ref, scale_ref, pool_ref, flux_ref, jump_ref,
        sorted_ref, spread_ref,
    )

    def out(c, at, value):
        merged_ref[3 + c, :, at] = value

    coarse_update(
        -COARSE_STEP, lambda c: merged_ref[c], lambda c, at: merged_ref[3 + c, :, at], out,
        geometry_ref, derivatives_ref, lift_ref, stack_ref, flux_ref, grad_ref, lifted_ref,
    )
    low_half = lax.broadcasted_iota(jnp.int32, (20, LANES), 1) < LANES // 2
    for c in range(3):
        ends_ref[c * 20 : c * 20 + 20, :] = jnp.where(
            low_half, merged_ref[3 + c, :, 0:LANES], merged_ref[3 + c, :, own - LANES : own]
        )
    ends_ref[60:64, :] = jnp.zeros((4, LANES), jnp.float32)


def coarse_electric_kernel(
    merged_ref, geometry_ref, normals_ref, scale_ref, nbr_ref, derivatives_ref, lift_ref,
    out_ref,
    pool_ref, flux_ref, jump_ref, sorted_ref, spread_ref, stack_ref, grad_ref, lifted_ref,
):
    own = merged_ref.shape[2]
    coarse_pool(merged_ref, 3, pool_ref)
    coarse_flux(
        own // LANES, False, nbr_ref, normals_ref, scale_ref, pool_ref, flux_ref, jump_ref,
        sorted_ref, spread_ref,
    )

    def out(c, at, value):
        out_ref[c, :, at] = value

    coarse_update(
        COARSE_STEP, lambda c: merged_ref[3 + c], lambda c, at: merged_ref[c, :, at], out,
        geometry_ref, derivatives_ref, lift_ref, stack_ref, flux_ref, grad_ref, lifted_ref,
    )


def finish_kernel(
    merged_ref, electric_ref, below_ref, above_ref, normals_ref, scale_ref, nbr_ref, lift_ref,
    out_ref,
    pool_ref, flux_ref, jump_ref, sorted_ref, spread_ref,
):
    own = merged_ref.shape[2]
    halo = halo_rows(below_ref[...], above_ref[...])

    def store(f, place, length, value):
        pool_ref[f, place : place + length, :] = value

    coarse_halo(halo, store)
    zero = jnp.zeros((8, LANES), jnp.float32)
    sources = [lambda g, f=f: pool_ref[f, g * 8 : g * 8 + 8, :] for f in range(4)]
    ends = (0, own // LANES - 1)
    for number, eb in enumerate(ends):
        at = lanes_at(eb)
        for f in range(4):
            code = rows8(nbr_ref[f : f + 1, at])
            which = jnp.where(code >= 4 * own, code & 3, 4)
            groups = gather32(sources, which, (code >> 2) & (LANES - 1), [zero] * 4)
            for g in range(4):
                jump_ref[f, g * 8 : g * 8 + 8, :] = groups[g]
        regroup(jump_ref, sorted_ref)
        scale = scale_ref[:, at]
        scaled = [normals_ref[c, :, at] * scale for c in range(3)]
        spread_normals(lambda c, f: scaled[c][f : f + 1, :], spread_ref)
        flux = crossed([spread_ref[c] for c in range(3)], [sorted_ref[c] for c in range(3)])
        for c in range(3):
            flux_ref[:, lanes_at(number * 3 + c)] = flux[c]
    lifted = dot(0.5 * lift_ref[...], flux_ref[...])
    for c in range(3):
        out_ref[c, :, LANES : own - LANES] = electric_ref[c, :, LANES : own - LANES]
        for number, eb in enumerate(ends):
            at = (number * 3 + c) * LANES
            out_ref[c, :, lanes_at(eb)] = (
                electric_ref[c, :, lanes_at(eb)] + COARSE_STEP * lifted[:, at : at + LANES]
            )
        out_ref[3 + c] = merged_ref[3 + c]


def call(kernel, outs, scratch, *args, hbm=(), vmem=VMEM_BYTES):
    whole = pl.BlockSpec(memory_space=pltpu.VMEM)
    specs = [
        pl.BlockSpec(memory_space=pltpu.HBM) if number in hbm else whole for number in range(len(args))
    ]
    return pl.pallas_call(
        kernel,
        out_shape=[jax.ShapeDtypeStruct(shape, dtype) for shape, dtype in outs],
        in_specs=specs,
        out_specs=[whole] * len(outs),
        scratch_shapes=[pltpu.VMEM(shape, dtype) for shape, dtype in scratch]
        + [pltpu.SemaphoreType.DMA(())] * len(hbm),
        compiler_params=pltpu.CompilerParams(vmem_limit_bytes=vmem),
    )(*args)


def device_of(block):
    sub = lax.axis_size("sub")
    return int(seats(lax.axis_size("dom"))[block // sub]) * sub + block % sub


def shifted(block, by, place=int):
    count = lax.axis_size(RING)
    pairs = [(place(i), place((i + by) % count)) for i in range(count)]
    return lax.ppermute(block, RING, pairs)


def exchange(block, place=int):
    return shifted(block, 1, place), shifted(block, -1, place)


def swap_slots(rows, width):
    peers = lax.axis_size("dom")
    chunks = rows.reshape(peers, rows.shape[0] // peers, width)
    return lax.all_to_all(chunks, "dom", split_axis=0, concat_axis=0, tiled=True).reshape(
        rows.shape[0], width
    )


def per_device(
    fields, geometry, normals, face_scale, derivatives, lift_matrix, face_nbr, send_rows,
    fine_slots, export_rows, fine_nbr,
):
    f32, i32 = jnp.float32, jnp.int32
    own = fields.shape[2]
    slots = send_rows.shape[0]
    fine = fine_slots.shape[0]
    width = export_rows.shape[1]
    table = jnp.concatenate(
        [
            fine_nbr,
            fine_slots.reshape(1, fine),
            jnp.pad(export_rows, ((0, 0), (0, fine - width))),
            jnp.zeros((1, fine), i32),
        ]
    )
    count = lax.axis_size(RING)
    table = lax.ppermute(table, RING, [(i, device_of(i)) for i in range(count)])
    send = send_rows.reshape(slots // LANES, LANES)
    order = slot_order(lax.axis_size("dom"), slots // lax.axis_size("dom"))
    packed, ends, home = call(
        pack_kernel,
        [((slots, 384), f32), ((64, LANES), f32), ((own // LANES, LANES), i32)],
        [
            (send.shape, i32), (send.shape, i32), (fields.shape, f32), (face_nbr.shape, i32),
            (geometry.shape, f32), (normals.shape, f32), (face_scale.shape, f32),
            (send.shape, i32), ((144, own), f32), ((8, own), i32), ((2, 4, 32, own), f32),
            ((384, slots), f32),
        ],
        send, jnp.asarray(order.reshape(send.shape)), fields, face_nbr, geometry, normals,
        face_scale,
        hbm=range(7),
        vmem=PACK_VMEM_BYTES,
    )
    received = swap_slots(packed, 384)
    state, traces = ((20, 3 * fine), f32), ((4, 32, fine), f32)
    efield, hfield, normal, factors, held, pool, halo, lane, back = call(
        functools.partial(unpack_kernel, width),
        [
            state, state, ((3, 40, fine), f32), ((16, fine), f32), ((2, 4, 32, fine), f32),
            traces, ((32, fine), f32), ((8, fine), i32), ((slots // LANES, LANES), i32),
        ],
        [((384, slots), f32), ((384, fine), f32)],
        received, table,
    )
    scratch = [((72, 20), f32), traces, ((3, 40, fine), f32), ((40, 3 * fine), f32)]
    end_parts = []
    for half in range(2 * SUBSTEPS - 1):
        below, above = exchange(halo, device_of)
        if half in (0, 1):
            halo, ends = lax.optimization_barrier((halo, ends))
            part = shifted(ends, 1 - 2 * half)
            below, above, part = lax.optimization_barrier((below, above, part))
            end_parts.append(part)
        magnetic = half % 2 == 0
        source, target = (efield, hfield) if magnetic else (hfield, efield)
        new, pool, halo = call(
            functools.partial(fine_kernel, magnetic),
            [state, traces, ((32, fine), f32)],
            scratch,
            source, target, pool, below, above, held, normal, factors, table, lane,
            derivatives, lift_matrix,
        )
        efield, hfield = (efield, new) if magnetic else (new, hfield)
    below, above = exchange(halo, device_of)
    (outgoing,) = call(
        last_fine_kernel,
        [((slots, LANES), f32)],
        [((128, fine), f32), ((128, slots), f32)] + scratch,
        hfield, efield, pool, below, above, held, normal, factors, table, back, derivatives,
        lift_matrix,
    )
    returned = swap_slots(outgoing, LANES)
    work = [
        ((3, 40, own), f32), ((4, 32, LANES), f32), ((3, 40, LANES), f32), ((3, 40, LANES), f32),
        ((72, 20), f32), ((3, 72, own), f32), ((3, 20, own), f32),
    ]
    merged, ends = call(
        coarse_magnetic_kernel,
        [((6, 20, own), f32), ((64, LANES), f32)],
        [((120, own), f32), ((128, slots), f32), ((4, 32, own + LANES), f32)] + work,
        returned, home, fields, end_parts[0], end_parts[1], geometry, normals, face_scale, face_nbr,
        derivatives, lift_matrix,
    )
    below, above = exchange(ends)
    (electric,) = call(
        coarse_electric_kernel,
        [((3, 20, own), f32)],
        [((4, 32, own), f32)] + work,
        merged, geometry, normals, face_scale, face_nbr, derivatives, lift_matrix,
    )
    (out,) = call(
        finish_kernel,
        [((6, 20, own), f32)],
        [
            traces, ((40, 6 * LANES), f32), ((4, 32, LANES), f32), ((3, 40, LANES), f32),
            ((3, 40, LANES), f32),
        ],
        merged, electric, below, above, normals, face_scale, face_nbr, lift_matrix,
    )
    return out


def solution(mesh):
    return jax.shard_map(
        per_device,
        mesh=mesh,
        in_specs=(
            P(None, None, ("dom", "sub")),
            P(None, ("dom", "sub")),
            P(None, None, ("dom", "sub")),
            P(None, ("dom", "sub")),
            P(),
            P(),
            P(None, ("dom", "sub")),
            P(("dom", "sub")),
            P(("dom", "sub")),
            P(None, ("dom", "sub")),
            P(None, ("dom", "sub")),
        ),
        out_specs=P(None, None, ("dom", "sub")),
        check_vma=False,
    )
```

```python
import functools

import jax
import jax.numpy as jnp
import numpy as np
from jax import lax
from jax.experimental import pallas as pl
from jax.experimental.pallas import tpu as pltpu
from jax.sharding import PartitionSpec as P

SUBSTEPS = 4
COARSE_STEP = 0.2
FINE_STEP = COARSE_STEP / SUBSTEPS
LANES = 128
VMEM_BYTES = 40 * 2**20
PACK_VMEM_BYTES = 60 * 2**20
RING = ("dom", "sub")
highest = lax.Precision.HIGHEST


def face_table():
    places = [
        (along_r, along_s, along_t)
        for along_t in range(4)
        for along_s in range(4 - along_t)
        for along_r in range(4 - along_t - along_s)
    ]
    bottom = [i for i, at in enumerate(places) if at[2] == 0]
    front = [i for i, at in enumerate(places) if at[1] == 0]
    slanted = [i for i, at in enumerate(places) if sum(at) == 3]
    beside = [i for i, at in enumerate(places) if at[0] == 0]
    return [bottom, front, slanted, beside]


def runs_of(nodes):
    runs = []
    for place, node in enumerate(nodes):
        if runs and runs[-1][1] + runs[-1][2] == node:
            runs[-1][2] += 1
        else:
            runs.append([place, node, 1])
    return runs


RUNS = [runs_of(nodes) for nodes in face_table()]


def seat(block, rows, columns):
    chip, core = block // 2, block % 2
    y, z = chip // columns, chip % columns
    if y % 2:
        z, core = columns - 1 - z, 1 - core
    return (y * columns + z) * 2 + core


def seats(count):
    chips = count // 2
    rows = max(r for r in range(1, chips + 1) if chips % r == 0 and r * r <= chips)
    return np.array([seat(block, rows, chips // rows) for block in range(count)], np.int32)


def slot_order(count, cap):
    block_at = np.argsort(seats(count))
    return (block_at[:, None] * cap + np.arange(cap)[None, :]).reshape(-1).astype(np.int32)


def take(block, lane):
    return jnp.take_along_axis(block, lane, axis=1, mode="promise_in_bounds")


def rows8(row):
    return jnp.broadcast_to(row, (8, LANES))


def lanes_at(block):
    if isinstance(block, int):
        return slice(block * LANES, (block + 1) * LANES)
    return pl.ds(pl.multiple_of(block * LANES, LANES), LANES)


def gather32(sources, which, lane, start):
    groups = list(start)
    for number, source in enumerate(sources):
        hit = which == number
        for group in range(4):
            groups[group] = jnp.where(hit, take(source(group), lane), groups[group])
    return groups


def spread_normals(normal_rows, out_ref):
    for c in range(3):
        for f in range(4):
            out_ref[c, f * 10 : f * 10 + 10, :] = jnp.broadcast_to(normal_rows(c, f), (10, LANES))


def regroup(jump_ref, sorted_ref):
    for f in range(4):
        for c in range(3):
            sorted_ref[c, f * 10 : f * 10 + 10, :] = jump_ref[f, c * 10 : c * 10 + 10, :]


def crossed(normals, jumps):
    def part(c):
        a, b = (c + 1) % 3, (c + 2) % 3
        return normals[a] * jumps[b] - normals[b] * jumps[a]

    return [part(c) for c in range(3)]


def curl_part(c, factor, grad):
    m, n = (c + 1) % 3, (c + 2) % 3
    total = factor(m, 0) * grad(0, n) - factor(n, 0) * grad(0, m)
    for a in (1, 2):
        total += factor(m, a) * grad(a, n) - factor(n, a) * grad(a, m)
    return total


def stack_derivatives(derivatives_ref, out_ref):
    out_ref[...] = jnp.zeros_like(out_ref)
    for a in range(3):
        out_ref[a * 24 : a * 24 + 20, :] = derivatives_ref[a]


def dot(a, b):
    return jnp.dot(a, b, precision=highest, preferred_element_type=jnp.float32)


def inverse_of(row_of, count, width, none):
    columns = [
        jnp.transpose(jnp.broadcast_to(row_of(b), (LANES, LANES))) for b in range(count)
    ]
    lane = lax.broadcasted_iota(jnp.int32, (LANES, LANES), 1)
    number = lax.broadcasted_iota(jnp.int32, (LANES, LANES), 0)
    out = []
    for w in range(width):
        best = jnp.full((LANES, LANES), none, jnp.int32)
        for b in range(count):
            best = jnp.maximum(
                best, jnp.where(columns[b] == lane + w * LANES, number + b * LANES, none)
            )
        out.append(jnp.max(best, axis=0, keepdims=True))
    return out


def pack_kernel(
    plain_send_hbm, order_hbm, fields_hbm, nbr_hbm, geometry_hbm, normals_hbm, scale_hbm,
    out_ref, ends_ref, home_ref, slot_ref, before_ref,
    plain_send_ref, order_ref, fields_ref, nbr_ref, geometry_ref, normals_ref, scale_ref,
    send_ref, rank_ref, row_ref, flat_ref, nb_ref, pool_ref, dense_ref, feature_ref,
    *sems,
):
    pairs = [
        (plain_send_hbm, plain_send_ref), (order_hbm, order_ref), (fields_hbm, fields_ref),
        (nbr_hbm, nbr_ref), (geometry_hbm, geometry_ref), (normals_hbm, normals_ref),
        (scale_hbm, scale_ref),
    ]
    copies = [pltpu.make_async_copy(a, b, sem) for (a, b), sem in zip(pairs, sems)]
    for copy in copies:
        copy.start()
    copies[0].wait()
    copies[1].wait()
    own = fields_ref.shape[2]
    blocks = own // LANES
    send_blocks = plain_send_ref.shape[0]
    dense_blocks = dense_ref.shape[1] // LANES
    for sb in range(send_blocks):
        order = rows8(order_ref[sb : sb + 1, :])
        row = jnp.zeros((8, LANES), jnp.int32)
        for b in range(send_blocks):
            block = take(rows8(plain_send_ref[b : b + 1, :]), order & (LANES - 1))
            row = jnp.where((order >> 7) == b, block, row)
        send_ref[sb : sb + 1, :] = row[0:1, :]
    upper = lax.broadcasted_iota(jnp.int32, (LANES, LANES), 0) <= lax.broadcasted_iota(
        jnp.int32, (LANES, LANES), 1
    )
    upper = jnp.where(upper, 1.0, 0.0)
    total = jnp.full((8, LANES), -1.0, jnp.float32)
    for sb in range(send_blocks):
        filled = rows8(send_ref[sb : sb + 1, :]) < own
        counts = jnp.where(filled, 1.0, 0.0)
        rank = total + dot(counts, upper)
        total += jnp.sum(counts, axis=1, keepdims=True)
        rank = jnp.where(filled, rank.astype(jnp.int32), LANES * LANES)
        rank_ref[sb : sb + 1, :] = rank[0:1, :]
    slots = inverse_of(lambda b: rank_ref[b : b + 1, :], send_blocks, dense_blocks, -1)
    for b in range(dense_blocks):
        slot_ref[b : b + 1, :] = slots[b]
        slot = rows8(slots[b])
        row = jnp.full((8, LANES), LANES * LANES, jnp.int32)
        for sb in range(send_blocks):
            block = take(rows8(send_ref[sb : sb + 1, :]), slot & (LANES - 1))
            row = jnp.where((slot >> 7) == sb, block, row)
        row_ref[b : b + 1, :] = row[0:1, :]
    homes = inverse_of(lambda b: row_ref[b : b + 1, :], dense_blocks, blocks, -1)
    for b in range(blocks):
        home_ref[b : b + 1, :] = homes[b]
    for copy in copies[2:]:
        copy.wait()
    for c in range(6):
        flat_ref[c * 20 : c * 20 + 20, :] = fields_ref[c]
    flat_ref[120:129, :] = geometry_ref[...]
    for c in range(3):
        flat_ref[129 + 4 * c : 133 + 4 * c, :] = normals_ref[c] * scale_ref[...]
    flat_ref[141:144, :] = jnp.zeros((3, own), jnp.float32)
    nb_ref[0:4, :] = nbr_ref[...]
    nb_ref[4:8, :] = nbr_ref[...]
    low_half = lax.broadcasted_iota(jnp.int32, (20, LANES), 1) < LANES // 2
    for c in range(3):
        ends_ref[c * 20 : c * 20 + 20, :] = jnp.where(
            low_half, fields_ref[c, :, 0:LANES], fields_ref[c, :, own - LANES : own]
        )
    ends_ref[60:64, :] = jnp.zeros((4, LANES), jnp.float32)
    for eh in range(2):
        for f in range(4):
            for c in range(3):
                for place, node, length in RUNS[f]:
                    pool_ref[eh, f, c * 10 + place : c * 10 + place + length, :] = fields_ref[
                        eh * 3 + c, node : node + length, :
                    ]
            pool_ref[eh, f, 30:32, :] = jnp.zeros((2, own), jnp.float32)
    sublane = lax.broadcasted_iota(jnp.int32, (8, LANES), 0)

    def pick(db, carry):
        row = rows8(jnp.minimum(row_ref[pl.ds(db, 1), :], own - 1))
        lane, which = row & (LANES - 1), row >> 7
        hits = [which == b for b in range(blocks)]
        for group in range(18):
            rows = slice(group * 8, group * 8 + 8)
            value = take(flat_ref[rows, 0:LANES], lane)
            for b in range(1, blocks):
                value = jnp.where(hits[b], take(flat_ref[rows, lanes_at(b)], lane), value)
            dense_ref[rows, lanes_at(db)] = value
        nbr = take(nb_ref[:, 0:LANES], lane)
        for b in range(1, blocks):
            nbr = jnp.where(hits[b], take(nb_ref[:, lanes_at(b)], lane), nbr)
        wall = jnp.where(nbr == 4 * row + sublane, -1.0, 1.0)
        for f in range(4):
            code = rows8(nbr[f : f + 1, :])
            sign = rows8(wall[f : f + 1, :])
            lane_f = (code >> 2) & (LANES - 1)
            which_f = (code & 3) * blocks + (code >> 9)
            groups = [jnp.zeros((8, LANES), jnp.float32)] * 8
            for number in range(4 * blocks):
                hit = which_f == number
                for group in range(8):
                    block = pool_ref[
                        group // 4,
                        number // blocks,
                        group % 4 * 8 : group % 4 * 8 + 8,
                        lanes_at(number % blocks),
                    ]
                    groups[group] = jnp.where(hit, take(block, lane_f), groups[group])
            for group in range(8):
                value = groups[group] * sign if group < 4 else groups[group]
                length = 8 if group % 4 < 3 else 6
                at = 144 + (group // 4 * 4 + f) * 30 + group % 4 * 8
                dense_ref[at : at + length, lanes_at(db)] = value[:length]
        return carry

    lax.fori_loop(0, dense_blocks, pick, 0)
    before_ref[...] = dense_ref[0:64, :]
    chunks = LANES * out_ref.shape[0] // (send_blocks * LANES)
    for sb in range(send_blocks):
        rank = rows8(rank_ref[sb : sb + 1, :])
        lane = rank & (LANES - 1)
        hits = [(rank >> 7) == b for b in range(dense_blocks)]
        for group in range(dense_ref.shape[0] // 8):
            rows = slice(group * 8, group * 8 + 8)
            value = jnp.zeros((8, LANES), jnp.float32)
            for b in range(dense_blocks):
                value = jnp.where(hits[b], take(dense_ref[rows, lanes_at(b)], lane), value)
            feature_ref[rows, :] = value
        out_ref[sb * chunks : (sb + 1) * chunks] = jnp.transpose(feature_ref[...]).reshape(
            chunks, LANES // chunks, feature_ref.shape[0]
        )


def fine_pool(state_ref, pool_ref):
    for f in range(4):
        for c in range(3):
            for place, node, length in RUNS[f]:
                pool_ref[f, c * 10 + place : c * 10 + place + length, :] = state_ref[
                    node : node + length, lanes_at(c)
                ]
        pool_ref[f, 30:32, :] = jnp.zeros((2, LANES), jnp.float32)


def exported(pool_ref, lane):
    face = lax.broadcasted_iota(jnp.int32, (8, LANES), 1) & 3
    zero = jnp.zeros((8, LANES), jnp.float32)
    return gather32(
        [lambda g, f=f: pool_ref[f, g * 8 : g * 8 + 8, :] for f in range(4)], face, lane, [zero] * 4
    )


def unpack_kernel(
    width, received_ref, table_ref,
    efield_ref, hfield_ref, normal_ref, geometry_ref, held_ref, pool_ref, halo_ref, lane_ref,
    back_ref,
    feature_ref, picked_ref,
):
    nbr_ref, slots_ref = table_ref.at[0:4], table_ref.at[4:5]
    slot_blocks = received_ref.shape[0] // LANES
    feature_ref[...] = jnp.transpose(received_ref[...])
    slot = rows8(slots_ref[...])
    lane, which = slot & (LANES - 1), slot >> 7
    hits = [which == b for b in range(slot_blocks)]
    for group in range(feature_ref.shape[0] // 8):
        at = slice(group * 8, group * 8 + 8)
        value = take(feature_ref[at, 0:LANES], lane)
        for b in range(1, slot_blocks):
            value = jnp.where(hits[b], take(feature_ref[at, lanes_at(b)], lane), value)
        picked_ref[at, :] = value
    for c in range(3):
        efield_ref[:, lanes_at(c)] = picked_ref[c * 20 : c * 20 + 20, :]
        hfield_ref[:, lanes_at(c)] = picked_ref[60 + c * 20 : 80 + c * 20, :]
    geometry_ref[...] = picked_ref[120:136, :]
    spread_normals(
        lambda c, f: picked_ref[129 + 4 * c + f : 130 + 4 * c + f, :], normal_ref
    )
    frozen_code = 4 * LANES + 4 * 2 * width
    for f in range(4):
        frozen = jnp.broadcast_to(nbr_ref[f : f + 1, :] == frozen_code, (30, LANES))
        for eh in range(2):
            at = 144 + (eh * 4 + f) * 30
            held_ref[eh, f, 0:30, :] = jnp.where(frozen, picked_ref[at : at + 30, :], 0.0)
            held_ref[eh, f, 30:32, :] = jnp.zeros((2, LANES), jnp.float32)
    place = lax.broadcasted_iota(jnp.int32, (8, LANES), 1)
    both = take(table_ref[...], (place >> 2) & (width - 1))
    lane_ref[...] = jnp.where(place < LANES // 2, rows8(both[6:7, :]), rows8(both[5:6, :]))
    fine_pool(efield_ref, pool_ref)
    groups = exported(pool_ref, lane_ref[...])
    for g in range(4):
        halo_ref[g * 8 : g * 8 + 8, :] = groups[g]
    backs = inverse_of(lambda b: slots_ref[...], 1, slot_blocks, 0)
    for b in range(slot_blocks):
        back_ref[b : b + 1, :] = backs[b]


def fine_rate(
    source_ref, pool_ref, low_ref, high_ref, held_ref, normal_ref, geometry_ref, nbr_ref,
    derivatives_ref, lift_ref,
    stack_ref, jump_ref, sorted_ref, flux_ref,
):
    stack_derivatives(derivatives_ref, stack_ref)
    grads = dot(stack_ref[...], source_ref[...])
    half = lax.broadcasted_iota(jnp.int32, (8, LANES), 1) < LANES // 2
    halo = [
        jnp.where(half, low_ref[g * 8 : g * 8 + 8, :], high_ref[g * 8 : g * 8 + 8, :])
        for g in range(4)
    ]
    sources = [lambda g, f=f: pool_ref[f, g * 8 : g * 8 + 8, :] for f in range(4)]
    sources.append(lambda g: halo[g])
    for f in range(4):
        code = rows8(nbr_ref[f : f + 1, :])
        local = code < 4 * LANES
        which = jnp.where(local, code & 3, code >> 7)
        lane = jnp.where(local, code >> 2, code) & (LANES - 1)
        groups = gather32(
            sources, which, lane, [held_ref[f, g * 8 : g * 8 + 8, :] for g in range(4)]
        )
        for g in range(4):
            jump_ref[f, g * 8 : g * 8 + 8, :] = groups[g] - pool_ref[f, g * 8 : g * 8 + 8, :]
    regroup(jump_ref, sorted_ref)
    flux = crossed([normal_ref[c] for c in range(3)], [sorted_ref[c] for c in range(3)])
    for c in range(3):
        flux_ref[:, lanes_at(c)] = flux[c]
    lifted = dot(0.5 * lift_ref[...], flux_ref[...])

    def factor(m, a):
        return geometry_ref[3 * m + a : 3 * m + a + 1, :]

    def grad(a, c):
        return grads[a * 24 : a * 24 + 20, c * LANES : (c + 1) * LANES]

    return [
        curl_part(c, factor, grad) + lifted[:, c * LANES : (c + 1) * LANES] for c in range(3)
    ]


def fine_kernel(
    magnetic,
    source_ref, target_ref, pool_ref, low_ref, high_ref, held_ref, normal_ref, geometry_ref,
    nbr_ref, lane_ref, derivatives_ref, lift_ref,
    out_ref, new_pool_ref, halo_ref,
    *scratch,
):
    field = 0 if magnetic else 1
    step = -FINE_STEP if magnetic else FINE_STEP
    rate = fine_rate(
        source_ref, pool_ref, low_ref, high_ref, held_ref.at[field], normal_ref, geometry_ref,
        nbr_ref, derivatives_ref, lift_ref, *scratch,
    )
    for c in range(3):
        out_ref[:, lanes_at(c)] = target_ref[:, lanes_at(c)] + step * rate[c]
    fine_pool(out_ref, new_pool_ref)
    groups = exported(new_pool_ref, lane_ref[...])
    for g in range(4):
        halo_ref[g * 8 : g * 8 + 8, :] = groups[g]


def last_fine_kernel(
    source_ref, target_ref, pool_ref, low_ref, high_ref, held_ref, normal_ref, geometry_ref,
    nbr_ref, back_ref, derivatives_ref, lift_ref,
    out_ref,
    result_ref, feature_ref,
    *scratch,
):
    rate = fine_rate(
        source_ref, pool_ref, low_ref, high_ref, held_ref.at[1], normal_ref, geometry_ref,
        nbr_ref, derivatives_ref, lift_ref, *scratch,
    )
    for c in range(3):
        result_ref[c * 20 : c * 20 + 20, :] = target_ref[:, lanes_at(c)] + FINE_STEP * rate[c]
        result_ref[60 + c * 20 : 80 + c * 20, :] = source_ref[:, lanes_at(c)]
    result_ref[120:128, :] = jnp.zeros((8, LANES), jnp.float32)
    for b in range(back_ref.shape[0]):
        lane = rows8(back_ref[b : b + 1, :])
        for g in range(16):
            feature_ref[g * 8 : g * 8 + 8, lanes_at(b)] = take(
                result_ref[g * 8 : g * 8 + 8, :], lane
            )
    out_ref[...] = jnp.transpose(feature_ref[...])


def coarse_pool(field_ref, first, pool_ref):
    own = field_ref.shape[2]
    for f in range(4):
        for c in range(3):
            for place, node, length in RUNS[f]:
                pool_ref[f, c * 10 + place : c * 10 + place + length, 0:own] = field_ref[
                    first + c, node : node + length, :
                ]


def halo_rows(below, above):
    half = lax.broadcasted_iota(jnp.int32, below.shape, 1) >= LANES // 2
    return pltpu.roll(jnp.where(half, below, above), LANES // 2, 1)


def coarse_halo(halo, store):
    for f in range(4):
        for c in range(3):
            for place, node, length in RUNS[f]:
                store(f, c * 10 + place, length, halo[c * 20 + node : c * 20 + node + length, :])


def coarse_flux(
    sources, number_of, mirror, nbr_ref, normals_ref, scale_ref, own_ref, flux_ref, jump_ref,
    sorted_ref, spread_ref, ends=None,
):
    own_blocks = flux_ref.shape[2] // LANES
    lane_number = lax.broadcasted_iota(jnp.int32, (8, LANES), 1)
    zero = jnp.zeros((8, LANES), jnp.float32)

    def one(eb, outer):
        at = lanes_at(eb)
        for f in range(4):
            code = rows8(nbr_ref[f : f + 1, at])
            which, lane = number_of(f, at, code)
            groups = gather32(sources, which, lane, [zero] * 4)
            if mirror:
                wall = code == 4 * (lane_number + eb * LANES) + f
                sign = jnp.where(wall, -1.0, 1.0)
                groups = [group * sign for group in groups]
            if outer:
                face = jnp.where(code >= 4 * own_blocks * LANES, code & 3, 4)
                groups = gather32(ends, face, (code >> 2) & (LANES - 1), groups)
            for g in range(4):
                jump_ref[f, g * 8 : g * 8 + 8, :] = (
                    groups[g] - own_ref[f, g * 8 : g * 8 + 8, at]
                )
        regroup(jump_ref, sorted_ref)
        scale = scale_ref[:, at]
        scaled = [normals_ref[c, :, at] * scale for c in range(3)]
        spread_normals(lambda c, f: scaled[c][f : f + 1, :], spread_ref)
        flux = crossed([spread_ref[c] for c in range(3)], [sorted_ref[c] for c in range(3)])
        for c in range(3):
            flux_ref[c, :, at] = flux[c]

    def inner(eb, carry):
        one(eb, False)
        return carry

    if ends is None:
        lax.fori_loop(0, own_blocks, inner, 0)
    else:
        one(0, True)
        lax.fori_loop(1, own_blocks - 1, inner, 0)
        one(own_blocks - 1, True)


def own_faces(pool_ref, own):
    blocks = own // LANES
    sources = [
        lambda g, n=n: pool_ref[n // blocks, g * 8 : g * 8 + 8, lanes_at(n % blocks)]
        for n in range(4 * blocks)
    ]

    def number_of(f, at, code):
        block = code >> 9
        which = jnp.where(block < blocks, (code & 3) * blocks + block, 4 * blocks)
        return which, (code >> 2) & (LANES - 1)

    return sources, number_of


def coarse_update(
    step, source, target, out, geometry_ref, derivatives_ref, lift_ref, stack_ref, flux_ref,
    grad_ref, lifted_ref,
):
    own_blocks = flux_ref.shape[2] // LANES
    stack_derivatives(derivatives_ref, stack_ref)
    lift = 0.5 * lift_ref[...]
    for c in range(3):
        grad_ref[c] = dot(stack_ref[...], source(c))
        lifted_ref[c] = dot(lift, flux_ref[c])

    def one(eb, carry):
        at = lanes_at(eb)

        def factor(m, a):
            return geometry_ref[3 * m + a : 3 * m + a + 1, at]

        def grad(a, c):
            return grad_ref[c, a * 24 : a * 24 + 20, at]

        for c in range(3):
            out(c, at, target(c, at) + step * (curl_part(c, factor, grad) + lifted_ref[c, :, at]))
        return carry

    lax.fori_loop(0, own_blocks, one, 0)


def early_kernel(
    fields_ref, home_ref, geometry_ref, normals_ref, scale_ref, nbr_ref, derivatives_ref, lift_ref,
    magnetic_ref, code_ref,
    pool_ref, flux_ref, jump_ref, sorted_ref, spread_ref, stack_ref, grad_ref, lifted_ref,
):
    own = fields_ref.shape[2]
    blocks = own // LANES
    coarse_pool(fields_ref, 0, pool_ref)
    sources, number_of = own_faces(pool_ref, own)
    coarse_flux(
        sources, number_of, True, nbr_ref, normals_ref, scale_ref, pool_ref, flux_ref, jump_ref,
        sorted_ref, spread_ref,
    )

    def out(c, at, value):
        magnetic_ref[c, :, at] = value

    coarse_update(
        -COARSE_STEP, lambda c: fields_ref[c], lambda c, at: fields_ref[3 + c, :, at], out,
        geometry_ref, derivatives_ref, lift_ref, stack_ref, flux_ref, grad_ref, lifted_ref,
    )
    width = jump_ref.shape[2] * 2

    def locate(eb, carry):
        at = lanes_at(eb)
        for f in range(4):
            code = rows8(nbr_ref[f : f + 1, at])
            home = jnp.full((8, LANES), -1, jnp.int32)
            for b in range(blocks):
                block = take(rows8(home_ref[b : b + 1, :]), (code >> 2) & (LANES - 1))
                home = jnp.where((code >> 9) == b, block, home)
            code_ref[f : f + 1, at] = jnp.where(home < 0, -1, (code & 3) * width + home)[0:1, :]
        return carry

    lax.fori_loop(0, blocks, locate, 0)


def merge_kernel(
    returned_ref, home_ref, slot_ref, before_ref, code_ref, magnetic_ref, fields_ref, below_ref,
    above_ref, geometry_ref, normals_ref, scale_ref, nbr_ref, derivatives_ref, lift_ref,
    merged_ref, ends_ref,
    flat_ref, back_ref, dense_ref, change_ref, fine_pool_ref, end_pool_ref,
    pool_ref, flux_ref, jump_ref, sorted_ref, spread_ref, stack_ref, grad_ref, lifted_ref,
):
    own = fields_ref.shape[2]
    slot_blocks = returned_ref.shape[0] // LANES
    dense_blocks = dense_ref.shape[1] // LANES
    back_ref[...] = jnp.transpose(returned_ref[...])
    for db in range(dense_blocks):
        slot = rows8(slot_ref[db : db + 1, :])
        lane = slot & (LANES - 1)
        hits = [(slot >> 7) == b for b in range(slot_blocks)]
        for group in range(15):
            rows = slice(group * 8, group * 8 + 8)
            value = jnp.zeros((8, LANES), jnp.float32)
            for b in range(slot_blocks):
                value = jnp.where(hits[b], take(back_ref[rows, lanes_at(b)], lane), value)
            dense_ref[rows, lanes_at(db)] = value
    for c in range(6):
        flat_ref[c * 20 : c * 20 + 20, :] = fields_ref[c]

    def merge(eb, carry):
        at = lanes_at(eb)
        home = rows8(home_ref[pl.ds(eb, 1), :])
        lane = home & (LANES - 1)
        hits = [(home >> 7) == b for b in range(dense_blocks)]
        for group in range(15):
            rows = slice(group * 8, group * 8 + 8)
            value = flat_ref[rows, at]
            for b in range(dense_blocks):
                value = jnp.where(hits[b], take(dense_ref[rows, lanes_at(b)], lane), value)
            flat_ref[rows, at] = value
        return carry

    lax.fori_loop(0, own // LANES, merge, 0)
    for c in range(6):
        merged_ref[c] = flat_ref[c * 20 : c * 20 + 20, :]
    for c in range(3):
        change_ref[c] = merged_ref[c] - fields_ref[c]
    coarse_pool(change_ref, 0, pool_ref)
    dense_ref[0:64, :] = dense_ref[0:64, :] - before_ref[...]
    for f in range(4):
        for c in range(3):
            for place, node, length in RUNS[f]:
                rows = slice(c * 10 + place, c * 10 + place + length)
                first = c * 20 + node
                fine_pool_ref[f, rows, :] = dense_ref[first : first + length, :]
    halo = halo_rows(below_ref[...], above_ref[...])

    def store(f, place, length, value):
        end_pool_ref[f, place : place + length, :] = value

    coarse_halo(halo, store)
    sources = [
        lambda g, n=n: fine_pool_ref[
            n // dense_blocks, g * 8 : g * 8 + 8, lanes_at(n % dense_blocks)
        ]
        for n in range(4 * dense_blocks)
    ]
    ends = [lambda g, f=f: end_pool_ref[f, g * 8 : g * 8 + 8, :] for f in range(4)]

    def number_of(f, at, code):
        fine = rows8(code_ref[f : f + 1, at])
        return fine >> 7, fine & (LANES - 1)

    coarse_flux(
        sources, number_of, True, nbr_ref, normals_ref, scale_ref, pool_ref, flux_ref, jump_ref,
        sorted_ref, spread_ref, ends,
    )

    def target(c, at):
        return magnetic_ref[c, :, at] + (merged_ref[3 + c, :, at] - fields_ref[3 + c, :, at])

    def out(c, at, value):
        merged_ref[3 + c, :, at] = value

    coarse_update(
        -COARSE_STEP, lambda c: change_ref[c], target, out,
        geometry_ref, derivatives_ref, lift_ref, stack_ref, flux_ref, grad_ref, lifted_ref,
    )
    low_half = lax.broadcasted_iota(jnp.int32, (20, LANES), 1) < LANES // 2
    for c in range(3):
        ends_ref[c * 20 : c * 20 + 20, :] = jnp.where(
            low_half, merged_ref[3 + c, :, 0:LANES], merged_ref[3 + c, :, own - LANES : own]
        )
    ends_ref[60:64, :] = jnp.zeros((4, LANES), jnp.float32)


def coarse_electric_kernel(
    merged_ref, geometry_ref, normals_ref, scale_ref, nbr_ref, derivatives_ref, lift_ref,
    out_ref,
    pool_ref, flux_ref, jump_ref, sorted_ref, spread_ref, stack_ref, grad_ref, lifted_ref,
):
    own = merged_ref.shape[2]
    coarse_pool(merged_ref, 3, pool_ref)
    sources, number_of = own_faces(pool_ref, own)
    coarse_flux(
        sources, number_of, False, nbr_ref, normals_ref, scale_ref, pool_ref, flux_ref, jump_ref,
        sorted_ref, spread_ref,
    )

    def out(c, at, value):
        out_ref[c, :, at] = value

    coarse_update(
        COARSE_STEP, lambda c: merged_ref[3 + c], lambda c, at: merged_ref[c, :, at], out,
        geometry_ref, derivatives_ref, lift_ref, stack_ref, flux_ref, grad_ref, lifted_ref,
    )


def finish_kernel(
    merged_ref, electric_ref, below_ref, above_ref, normals_ref, scale_ref, nbr_ref, lift_ref,
    out_ref,
    pool_ref, flux_ref, jump_ref, sorted_ref, spread_ref,
):
    own = merged_ref.shape[2]
    halo = halo_rows(below_ref[...], above_ref[...])

    def store(f, place, length, value):
        pool_ref[f, place : place + length, :] = value

    coarse_halo(halo, store)
    zero = jnp.zeros((8, LANES), jnp.float32)
    sources = [lambda g, f=f: pool_ref[f, g * 8 : g * 8 + 8, :] for f in range(4)]
    ends = (0, own // LANES - 1)
    for number, eb in enumerate(ends):
        at = lanes_at(eb)
        for f in range(4):
            code = rows8(nbr_ref[f : f + 1, at])
            which = jnp.where(code >= 4 * own, code & 3, 4)
            groups = gather32(sources, which, (code >> 2) & (LANES - 1), [zero] * 4)
            for g in range(4):
                jump_ref[f, g * 8 : g * 8 + 8, :] = groups[g]
        regroup(jump_ref, sorted_ref)
        scale = scale_ref[:, at]
        scaled = [normals_ref[c, :, at] * scale for c in range(3)]
        spread_normals(lambda c, f: scaled[c][f : f + 1, :], spread_ref)
        flux = crossed([spread_ref[c] for c in range(3)], [sorted_ref[c] for c in range(3)])
        for c in range(3):
            flux_ref[:, lanes_at(number * 3 + c)] = flux[c]
    lifted = dot(0.5 * lift_ref[...], flux_ref[...])
    for c in range(3):
        out_ref[c, :, LANES : own - LANES] = electric_ref[c, :, LANES : own - LANES]
        for number, eb in enumerate(ends):
            at = (number * 3 + c) * LANES
            out_ref[c, :, lanes_at(eb)] = (
                electric_ref[c, :, lanes_at(eb)] + COARSE_STEP * lifted[:, at : at + LANES]
            )
        out_ref[3 + c] = merged_ref[3 + c]


def call(kernel, outs, scratch, *args, hbm=(), vmem=VMEM_BYTES):
    whole = pl.BlockSpec(memory_space=pltpu.VMEM)
    specs = [
        pl.BlockSpec(memory_space=pltpu.HBM) if number in hbm else whole for number in range(len(args))
    ]
    return pl.pallas_call(
        kernel,
        out_shape=[jax.ShapeDtypeStruct(shape, dtype) for shape, dtype in outs],
        in_specs=specs,
        out_specs=[whole] * len(outs),
        scratch_shapes=[pltpu.VMEM(shape, dtype) for shape, dtype in scratch]
        + [pltpu.SemaphoreType.DMA(())] * len(hbm),
        compiler_params=pltpu.CompilerParams(vmem_limit_bytes=vmem),
    )(*args)


def device_of(block):
    sub = lax.axis_size("sub")
    return int(seats(lax.axis_size("dom"))[block // sub]) * sub + block % sub


def shifted(block, by, place=int):
    count = lax.axis_size(RING)
    pairs = [(place(i), place((i + by) % count)) for i in range(count)]
    return lax.ppermute(block, RING, pairs)


def exchange(block, place=int):
    return shifted(block, 1, place), shifted(block, -1, place)


def swap_slots(rows):
    width = rows.shape[-1]
    chunks = rows.reshape(lax.axis_size("dom"), -1, width)
    return lax.all_to_all(chunks, "dom", split_axis=0, concat_axis=0, tiled=True).reshape(-1, width)


def per_device(
    fields, geometry, normals, face_scale, derivatives, lift_matrix, face_nbr, send_rows,
    fine_slots, export_rows, fine_nbr,
):
    f32, i32 = jnp.float32, jnp.int32
    own = fields.shape[2]
    slots = send_rows.shape[0]
    fine = fine_slots.shape[0]
    width = export_rows.shape[1]
    table = jnp.concatenate(
        [
            fine_nbr,
            fine_slots.reshape(1, fine),
            jnp.pad(export_rows, ((0, 0), (0, fine - width))),
            jnp.zeros((1, fine), i32),
        ]
    )
    count = lax.axis_size(RING)
    table = lax.ppermute(table, RING, [(i, device_of(i)) for i in range(count)])
    send = send_rows.reshape(slots // LANES, LANES)
    order = slot_order(lax.axis_size("dom"), slots // lax.axis_size("dom"))
    dense = 2 * fine
    packed, ends, home, dense_slots, before = call(
        pack_kernel,
        [
            ((lax.axis_size("dom"), slots // lax.axis_size("dom"), 384), f32), ((64, LANES), f32),
            ((own // LANES, LANES), i32), ((dense // LANES, LANES), i32), ((64, dense), f32),
        ],
        [
            (send.shape, i32), (send.shape, i32), (fields.shape, f32), (face_nbr.shape, i32),
            (geometry.shape, f32), (normals.shape, f32), (face_scale.shape, f32),
            (send.shape, i32), (send.shape, i32), ((dense // LANES, LANES), i32),
            ((144, own), f32), ((8, own), i32), ((2, 4, 32, own), f32), ((384, dense), f32),
            ((384, LANES), f32),
        ],
        send, jnp.asarray(order.reshape(send.shape)), fields, face_nbr, geometry, normals,
        face_scale,
        hbm=range(7),
        vmem=PACK_VMEM_BYTES,
    )
    received = swap_slots(packed)
    ends_below, ends_above = exchange(ends)
    work = [
        ((3, 40, own), f32), ((4, 32, LANES), f32), ((3, 40, LANES), f32), ((3, 40, LANES), f32),
        ((72, 20), f32), ((3, 72, own), f32), ((3, 20, own), f32),
    ]
    early, fine_code = call(
        early_kernel,
        [((3, 20, own), f32), (face_nbr.shape, i32)],
        [((4, 32, own), f32)] + work,
        fields, home, geometry, normals, face_scale, face_nbr, derivatives, lift_matrix,
    )
    received, table, ends_below, ends_above, early, fine_code = lax.optimization_barrier(
        (received, table, ends_below, ends_above, early, fine_code)
    )
    state, traces = ((20, 3 * fine), f32), ((4, 32, fine), f32)
    efield, hfield, normal, factors, held, pool, halo, lane, back = call(
        functools.partial(unpack_kernel, width),
        [
            state, state, ((3, 40, fine), f32), ((16, fine), f32), ((2, 4, 32, fine), f32),
            traces, ((32, fine), f32), ((8, fine), i32), ((slots // LANES, LANES), i32),
        ],
        [((384, slots), f32), ((384, fine), f32)],
        received, table,
    )
    scratch = [((72, 20), f32), traces, ((3, 40, fine), f32), ((40, 3 * fine), f32)]
    for half in range(2 * SUBSTEPS - 1):
        below, above = exchange(halo, device_of)
        magnetic = half % 2 == 0
        source, target = (efield, hfield) if magnetic else (hfield, efield)
        new, pool, halo = call(
            functools.partial(fine_kernel, magnetic),
            [state, traces, ((32, fine), f32)],
            scratch,
            source, target, pool, below, above, held, normal, factors, table, lane,
            derivatives, lift_matrix,
        )
        efield, hfield = (efield, new) if magnetic else (new, hfield)
    below, above = exchange(halo, device_of)
    (outgoing,) = call(
        last_fine_kernel,
        [((slots, LANES), f32)],
        [((128, fine), f32), ((128, slots), f32)] + scratch,
        hfield, efield, pool, below, above, held, normal, factors, table, back, derivatives,
        lift_matrix,
    )
    returned = swap_slots(outgoing)
    merged, ends = call(
        merge_kernel,
        [((6, 20, own), f32), ((64, LANES), f32)],
        [
            ((120, own), f32), ((128, slots), f32), ((120, dense), f32), ((3, 20, own), f32),
            ((4, 32, dense), f32), traces, ((4, 32, own), f32),
        ] + work,
        returned, home, dense_slots, before, fine_code, early, fields, ends_below, ends_above,
        geometry, normals, face_scale, face_nbr, derivatives, lift_matrix,
    )
    below, above = exchange(ends)
    (electric,) = call(
        coarse_electric_kernel,
        [((3, 20, own), f32)],
        [((4, 32, own), f32)] + work,
        merged, geometry, normals, face_scale, face_nbr, derivatives, lift_matrix,
    )
    (out,) = call(
        finish_kernel,
        [((6, 20, own), f32)],
        [
            traces, ((40, 6 * LANES), f32), ((4, 32, LANES), f32), ((3, 40, LANES), f32),
            ((3, 40, LANES), f32),
        ],
        merged, electric, below, above, normals, face_scale, face_nbr, lift_matrix,
    )
    return out


def solution(mesh):
    return jax.shard_map(
        per_device,
        mesh=mesh,
        in_specs=(
            P(None, None, ("dom", "sub")),
            P(None, ("dom", "sub")),
            P(None, None, ("dom", "sub")),
            P(None, ("dom", "sub")),
            P(),
            P(),
            P(None, ("dom", "sub")),
            P(("dom", "sub")),
            P(("dom", "sub")),
            P(None, ("dom", "sub")),
            P(None, ("dom", "sub")),
        ),
        out_specs=P(None, None, ("dom", "sub")),
        check_vma=False,
    )
```

```python
import functools

import jax
import jax.numpy as jnp
import numpy as np
from jax import lax
from jax.experimental import pallas as pl
from jax.experimental.pallas import tpu as pltpu
from jax.sharding import PartitionSpec as P

SUBSTEPS = 4
COARSE_STEP = 0.2
FINE_STEP = COARSE_STEP / SUBSTEPS
LANES = 128
VMEM_BYTES = 40 * 2**20
PACK_VMEM_BYTES = 60 * 2**20
RING = ("dom", "sub")
REACH = 4
highest = lax.Precision.HIGHEST


def face_table():
    places = [
        (along_r, along_s, along_t)
        for along_t in range(4)
        for along_s in range(4 - along_t)
        for along_r in range(4 - along_t - along_s)
    ]
    bottom = [i for i, at in enumerate(places) if at[2] == 0]
    front = [i for i, at in enumerate(places) if at[1] == 0]
    slanted = [i for i, at in enumerate(places) if sum(at) == 3]
    beside = [i for i, at in enumerate(places) if at[0] == 0]
    return [bottom, front, slanted, beside]


def runs_of(nodes):
    runs = []
    for place, node in enumerate(nodes):
        if runs and runs[-1][1] + runs[-1][2] == node:
            runs[-1][2] += 1
        else:
            runs.append([place, node, 1])
    return runs


RUNS = [runs_of(nodes) for nodes in face_table()]


def seat(block, rows, columns):
    chip, core = block // 2, block % 2
    y, z = chip // columns, chip % columns
    if y % 2:
        z, core = columns - 1 - z, 1 - core
    return (y * columns + z) * 2 + core


def seats(count):
    chips = count // 2
    rows = max(r for r in range(1, chips + 1) if chips % r == 0 and r * r <= chips)
    return np.array([seat(block, rows, chips // rows) for block in range(count)], np.int32)


def slot_order(count, cap):
    block_at = np.argsort(seats(count))
    return (block_at[:, None] * cap + np.arange(cap)[None, :]).reshape(-1).astype(np.int32)


def take(block, lane):
    return jnp.take_along_axis(block, lane, axis=1, mode="promise_in_bounds")


def rows8(row):
    return jnp.broadcast_to(row, (8, LANES))


def lanes_at(block):
    if isinstance(block, int):
        return slice(block * LANES, (block + 1) * LANES)
    return pl.ds(pl.multiple_of(block * LANES, LANES), LANES)


def gather32(sources, which, lane, start):
    groups = list(start)
    for number, source in enumerate(sources):
        hit = which == number
        for group in range(4):
            groups[group] = jnp.where(hit, take(source(group), lane), groups[group])
    return groups


def spread_normals(normal_rows, out_ref):
    for c in range(3):
        for f in range(4):
            out_ref[c, f * 10 : f * 10 + 10, :] = jnp.broadcast_to(normal_rows(c, f), (10, LANES))


def regroup(jump_ref, sorted_ref):
    for f in range(4):
        for c in range(3):
            sorted_ref[c, f * 10 : f * 10 + 10, :] = jump_ref[f, c * 10 : c * 10 + 10, :]


def crossed(normals, jumps):
    def part(c):
        a, b = (c + 1) % 3, (c + 2) % 3
        return normals[a] * jumps[b] - normals[b] * jumps[a]

    return [part(c) for c in range(3)]


def curl_part(c, factor, grad):
    m, n = (c + 1) % 3, (c + 2) % 3
    total = factor(m, 0) * grad(0, n) - factor(n, 0) * grad(0, m)
    for a in (1, 2):
        total += factor(m, a) * grad(a, n) - factor(n, a) * grad(a, m)
    return total


def stack_derivatives(derivatives_ref, out_ref):
    out_ref[...] = jnp.zeros_like(out_ref)
    for a in range(3):
        out_ref[a * 24 : a * 24 + 20, :] = derivatives_ref[a]


def dot(a, b):
    return jnp.dot(a, b, precision=highest, preferred_element_type=jnp.float32)


def inverse_of(row_of, count, width, none):
    columns = [
        jnp.transpose(jnp.broadcast_to(row_of(b), (LANES, LANES))) for b in range(count)
    ]
    lane = lax.broadcasted_iota(jnp.int32, (LANES, LANES), 1)
    number = lax.broadcasted_iota(jnp.int32, (LANES, LANES), 0)
    out = []
    for w in range(width):
        best = jnp.full((LANES, LANES), none, jnp.int32)
        for b in range(count):
            best = jnp.maximum(
                best, jnp.where(columns[b] == lane + w * LANES, number + b * LANES, none)
            )
        out.append(jnp.max(best, axis=0, keepdims=True))
    return out


def pack_kernel(
    plain_send_hbm, order_hbm, fields_hbm, nbr_hbm, geometry_hbm, normals_hbm, scale_hbm,
    out_ref, ends_ref, home_ref, slot_ref, before_ref,
    plain_send_ref, order_ref, fields_ref, nbr_ref, geometry_ref, normals_ref, scale_ref,
    send_ref, rank_ref, row_ref, flat_ref, nb_ref, pool_ref, dense_ref, feature_ref,
    *sems,
):
    pairs = [
        (plain_send_hbm, plain_send_ref), (order_hbm, order_ref), (fields_hbm, fields_ref),
        (nbr_hbm, nbr_ref), (geometry_hbm, geometry_ref), (normals_hbm, normals_ref),
        (scale_hbm, scale_ref),
    ]
    copies = [pltpu.make_async_copy(a, b, sem) for (a, b), sem in zip(pairs, sems)]
    for copy in copies:
        copy.start()
    copies[0].wait()
    copies[1].wait()
    own = fields_ref.shape[2]
    blocks = own // LANES
    send_blocks = plain_send_ref.shape[0]
    dense_blocks = dense_ref.shape[1] // LANES
    for sb in range(send_blocks):
        order = rows8(order_ref[sb : sb + 1, :])
        row = jnp.zeros((8, LANES), jnp.int32)
        for b in range(send_blocks):
            block = take(rows8(plain_send_ref[b : b + 1, :]), order & (LANES - 1))
            row = jnp.where((order >> 7) == b, block, row)
        send_ref[sb : sb + 1, :] = row[0:1, :]
    upper = lax.broadcasted_iota(jnp.int32, (LANES, LANES), 0) <= lax.broadcasted_iota(
        jnp.int32, (LANES, LANES), 1
    )
    upper = jnp.where(upper, 1.0, 0.0)
    total = jnp.full((8, LANES), -1.0, jnp.float32)
    for sb in range(send_blocks):
        filled = rows8(send_ref[sb : sb + 1, :]) < own
        counts = jnp.where(filled, 1.0, 0.0)
        rank = total + dot(counts, upper)
        total += jnp.sum(counts, axis=1, keepdims=True)
        rank = jnp.where(filled, rank.astype(jnp.int32), LANES * LANES)
        rank_ref[sb : sb + 1, :] = rank[0:1, :]
    slots = inverse_of(lambda b: rank_ref[b : b + 1, :], send_blocks, dense_blocks, -1)
    for b in range(dense_blocks):
        slot_ref[b : b + 1, :] = slots[b]
        slot = rows8(slots[b])
        row = jnp.full((8, LANES), LANES * LANES, jnp.int32)
        for sb in range(send_blocks):
            block = take(rows8(send_ref[sb : sb + 1, :]), slot & (LANES - 1))
            row = jnp.where((slot >> 7) == sb, block, row)
        row_ref[b : b + 1, :] = row[0:1, :]
    homes = inverse_of(lambda b: row_ref[b : b + 1, :], dense_blocks, blocks, -1)
    for b in range(blocks):
        home_ref[b : b + 1, :] = homes[b]
    for copy in copies[2:]:
        copy.wait()
    for c in range(6):
        flat_ref[c * 20 : c * 20 + 20, :] = fields_ref[c]
    flat_ref[120:129, :] = geometry_ref[...]
    for c in range(3):
        flat_ref[129 + 4 * c : 133 + 4 * c, :] = normals_ref[c] * scale_ref[...]
    flat_ref[141:144, :] = jnp.zeros((3, own), jnp.float32)
    nb_ref[0:4, :] = nbr_ref[...]
    nb_ref[4:8, :] = nbr_ref[...]
    low_half = lax.broadcasted_iota(jnp.int32, (20, LANES), 1) < LANES // 2
    for c in range(3):
        ends_ref[c * 20 : c * 20 + 20, :] = jnp.where(
            low_half, fields_ref[c, :, 0:LANES], fields_ref[c, :, own - LANES : own]
        )
    ends_ref[60:64, :] = jnp.zeros((4, LANES), jnp.float32)
    for eh in range(2):
        for f in range(4):
            for c in range(3):
                for place, node, length in RUNS[f]:
                    pool_ref[eh, f, c * 10 + place : c * 10 + place + length, :] = fields_ref[
                        eh * 3 + c, node : node + length, :
                    ]
            pool_ref[eh, f, 30:32, :] = jnp.zeros((2, own), jnp.float32)
    sublane = lax.broadcasted_iota(jnp.int32, (8, LANES), 0)

    def pick(db, carry):
        row = rows8(jnp.minimum(row_ref[pl.ds(db, 1), :], own - 1))
        lane, which = row & (LANES - 1), row >> 7
        hits = [which == b for b in range(blocks)]
        for group in range(18):
            rows = slice(group * 8, group * 8 + 8)
            value = take(flat_ref[rows, 0:LANES], lane)
            for b in range(1, blocks):
                value = jnp.where(hits[b], take(flat_ref[rows, lanes_at(b)], lane), value)
            dense_ref[rows, lanes_at(db)] = value
        nbr = take(nb_ref[:, 0:LANES], lane)
        for b in range(1, blocks):
            nbr = jnp.where(hits[b], take(nb_ref[:, lanes_at(b)], lane), nbr)
        wall = jnp.where(nbr == 4 * row + sublane, -1.0, 1.0)
        for f in range(4):
            code = rows8(nbr[f : f + 1, :])
            sign = rows8(wall[f : f + 1, :])
            lane_f = (code >> 2) & (LANES - 1)
            which_f = (code & 3) * blocks + (code >> 9)
            groups = [jnp.zeros((8, LANES), jnp.float32)] * 8
            for number in range(4 * blocks):
                hit = which_f == number
                for group in range(8):
                    block = pool_ref[
                        group // 4,
                        number // blocks,
                        group % 4 * 8 : group % 4 * 8 + 8,
                        lanes_at(number % blocks),
                    ]
                    groups[group] = jnp.where(hit, take(block, lane_f), groups[group])
            for group in range(8):
                value = groups[group] * sign if group < 4 else groups[group]
                length = 8 if group % 4 < 3 else 6
                at = 144 + (group // 4 * 4 + f) * 30 + group % 4 * 8
                dense_ref[at : at + length, lanes_at(db)] = value[:length]
        return carry

    lax.fori_loop(0, dense_blocks, pick, 0)
    before_ref[...] = dense_ref[0:64, :]
    chunks = LANES * out_ref.shape[0] // (send_blocks * LANES)
    for sb in range(send_blocks):
        rank = rows8(rank_ref[sb : sb + 1, :])
        lane = rank & (LANES - 1)
        hits = [(rank >> 7) == b for b in range(dense_blocks)]
        for group in range(dense_ref.shape[0] // 8):
            rows = slice(group * 8, group * 8 + 8)
            value = jnp.zeros((8, LANES), jnp.float32)
            for b in range(dense_blocks):
                value = jnp.where(hits[b], take(dense_ref[rows, lanes_at(b)], lane), value)
            feature_ref[rows, :] = value
        out_ref[sb * chunks : (sb + 1) * chunks] = jnp.transpose(feature_ref[...]).reshape(
            chunks, LANES // chunks, feature_ref.shape[0]
        )


def unpack_kernel(
    width, received_ref, table_ref, lift_ref,
    out_ref, back_ref,
    feature_ref, picked_ref, held_ref, sorted_ref, normal_ref, flux_ref,
):
    nbr_ref, slots_ref = table_ref.at[0:4], table_ref.at[4:5]
    slot_blocks = received_ref.shape[0] // LANES
    feature_ref[...] = jnp.transpose(received_ref[...])
    slot = rows8(slots_ref[...])
    lane, which = slot & (LANES - 1), slot >> 7
    hits = [which == b for b in range(slot_blocks)]
    for group in range(feature_ref.shape[0] // 8):
        at = slice(group * 8, group * 8 + 8)
        value = take(feature_ref[at, 0:LANES], lane)
        for b in range(1, slot_blocks):
            value = jnp.where(hits[b], take(feature_ref[at, lanes_at(b)], lane), value)
        picked_ref[at, :] = value
    spread_normals(lambda c, f: picked_ref[129 + 4 * c + f : 130 + 4 * c + f, :], normal_ref)
    frozen_code = 4 * LANES + 4 * 2 * width
    for eh in range(2):
        for f in range(4):
            frozen = jnp.broadcast_to(nbr_ref[f : f + 1, :] == frozen_code, (30, LANES))
            at = 144 + (eh * 4 + f) * 30
            held_ref[f, 0:30, :] = jnp.where(frozen, picked_ref[at : at + 30, :], 0.0)
        regroup(held_ref, sorted_ref)
        flux = crossed([normal_ref[c] for c in range(3)], [sorted_ref[c] for c in range(3)])
        for c in range(3):
            flux_ref[:, lanes_at(eh * 3 + c)] = flux[c]
    lifted = dot(0.5 * lift_ref[...], flux_ref[...])
    place = lax.broadcasted_iota(jnp.int32, (8, LANES), 1)
    both = take(table_ref[...], (place >> 2) & (width - 1))
    lane = jnp.where(place < LANES // 2, rows8(both[6:7, :]), rows8(both[5:6, :]))
    picked_ref[144:264, :] = jnp.concatenate(
        [lifted[:, k * LANES : (k + 1) * LANES] for k in range(6)]
    )
    picked_ref[264:268, :] = nbr_ref[...].astype(jnp.float32)
    picked_ref[268:272, :] = lane[0:4, :].astype(jnp.float32)
    for k in range(out_ref.shape[0]):
        out_ref[k] = picked_ref[0:272, :]
    backs = inverse_of(lambda b: slots_ref[...], 1, slot_blocks, 0)
    for b in range(slot_blocks):
        back_ref[b : b + 1, :] = backs[b]


def window_state(spot_ref, aligned, shifted, rows, block_ref):
    half = 2 * REACH

    def fetch(w, carry):
        spot = spot_ref[w]

        @pl.when(spot < half)
        def _():
            block_ref[w, 0:rows, :] = aligned[spot, 0:rows, :]

        @pl.when(spot >= half)
        def _():
            block_ref[w, 0:rows, :] = shifted[spot - half, 0:rows, :]

        return carry

    lax.fori_loop(0, 2 * REACH + 1, fetch, 0)


def window_steps(
    derivatives_ref, lift_ref, block_ref, efield_ref, hfield_ref, pool_ref, export_ref, jump_ref,
    sorted_ref, spread_ref, flux_ref, grad_ref, lifted_ref, stack_ref,
):
    blocks = 2 * REACH + 1
    stack_derivatives(derivatives_ref, stack_ref)
    lift = 0.5 * lift_ref[...]
    half_lanes = lax.broadcasted_iota(jnp.int32, (8, LANES), 1) < LANES // 2
    face = lax.broadcasted_iota(jnp.int32, (8, LANES), 1) & 3
    zero = jnp.zeros((8, LANES), jnp.float32)

    def prepare(w, carry):
        for c in range(3):
            efield_ref[:, lanes_at(w * 3 + c)] = block_ref[w, c * 20 : c * 20 + 20, :]
            hfield_ref[:, lanes_at(w * 3 + c)] = block_ref[w, 60 + c * 20 : 80 + c * 20, :]
        spread_normals(
            lambda c, f: block_ref[w, 129 + 4 * c + f : 130 + 4 * c + f, :], spread_ref.at[w]
        )
        return carry

    lax.fori_loop(0, blocks, prepare, 0)
    for level in range(1, REACH + 1):
        magnetic = level % 2 == 1
        source_ref, target_ref = (efield_ref, hfield_ref) if magnetic else (hfield_ref, efield_ref)
        step = -FINE_STEP if magnetic else FINE_STEP
        held = 144 if magnetic else 204
        first, last = level, blocks - level

        def expose(w, carry, source_ref=source_ref):
            for f in range(4):
                for c in range(3):
                    for place, node, length in RUNS[f]:
                        pool_ref[w, f, c * 10 + place : c * 10 + place + length, :] = source_ref[
                            node : node + length, lanes_at(w * 3 + c)
                        ]
            lane = rows8(block_ref[w, 268:269, :]).astype(jnp.int32)
            groups = gather32(
                [lambda g, f=f: pool_ref[w, f, g * 8 : g * 8 + 8, :] for f in range(4)],
                face, lane, [zero] * 4,
            )
            for g in range(4):
                export_ref[w, g * 8 : g * 8 + 8, :] = groups[g]
            return carry

        lax.fori_loop(first - 1, last + 1, expose, 0)

        def gather(w, carry):
            sources = [
                lambda g, f=f: pool_ref[w, f, g * 8 : g * 8 + 8, :] for f in range(4)
            ]
            halo = [
                jnp.where(
                    half_lanes,
                    export_ref[w - 1, g * 8 : g * 8 + 8, :],
                    export_ref[w + 1, g * 8 : g * 8 + 8, :],
                )
                for g in range(4)
            ]
            sources.append(lambda g: halo[g])
            for f in range(4):
                code = rows8(block_ref[w, 264 + f : 265 + f, :]).astype(jnp.int32)
                local = code < 4 * LANES
                which = jnp.where(local, code & 3, code >> 7)
                lane = jnp.where(local, code >> 2, code) & (LANES - 1)
                groups = gather32(sources, which, lane, [zero] * 4)
                for g in range(4):
                    jump_ref[f, g * 8 : g * 8 + 8, :] = (
                        groups[g] - pool_ref[w, f, g * 8 : g * 8 + 8, :]
                    )
            regroup(jump_ref, sorted_ref)
            flux = crossed([spread_ref[w, c] for c in range(3)], [sorted_ref[c] for c in range(3)])
            for c in range(3):
                flux_ref[:, lanes_at(w * 3 + c)] = flux[c]
            return carry

        lax.fori_loop(first, last, gather, 0)
        span = slice(first * 3 * LANES, last * 3 * LANES)
        grad_ref[:, span] = dot(stack_ref[...], source_ref[:, span])
        lifted_ref[:, span] = dot(lift, flux_ref[:, span])

        def update(w, carry, target_ref=target_ref, step=step, held=held):
            def factor(m, a):
                return block_ref[w, 120 + 3 * m + a : 121 + 3 * m + a, :]

            def grad(a, c):
                return grad_ref[a * 24 : a * 24 + 20, lanes_at(w * 3 + c)]

            for c in range(3):
                at = lanes_at(w * 3 + c)
                rate = (
                    curl_part(c, factor, grad)
                    + lifted_ref[:, at]
                    + block_ref[w, held + c * 20 : held + c * 20 + 20, :]
                )
                target_ref[:, at] = target_ref[:, at] + step * rate
            return carry

        lax.fori_loop(first, last, update, 0)


def first_window_kernel(
    spot_ref, aligned_ref, shifted_ref, derivatives_ref, lift_ref,
    out_ref,
    block_ref, efield_ref, hfield_ref, *scratch,
):
    window_state(spot_ref, aligned_ref, shifted_ref, 272, block_ref)
    window_steps(derivatives_ref, lift_ref, block_ref, efield_ref, hfield_ref, *scratch)
    for c in range(3):
        electric = efield_ref[:, lanes_at(REACH * 3 + c)]
        magnetic = hfield_ref[:, lanes_at(REACH * 3 + c)]
        for k in range(out_ref.shape[0]):
            out_ref[k, c * 20 : c * 20 + 20, :] = electric
            out_ref[k, 60 + c * 20 : 80 + c * 20, :] = magnetic


def last_window_kernel(
    spot_ref, aligned_ref, shifted_ref, aligned_state_ref, shifted_state_ref, back_ref,
    derivatives_ref, lift_ref,
    out_ref,
    result_ref, feature_ref, block_ref, efield_ref, hfield_ref, *scratch,
):
    window_state(spot_ref, aligned_ref, shifted_ref, 272, block_ref)
    window_state(spot_ref, aligned_state_ref, shifted_state_ref, 120, block_ref)
    window_steps(derivatives_ref, lift_ref, block_ref, efield_ref, hfield_ref, *scratch)
    for c in range(3):
        result_ref[c * 20 : c * 20 + 20, :] = efield_ref[:, lanes_at(REACH * 3 + c)]
        result_ref[60 + c * 20 : 80 + c * 20, :] = hfield_ref[:, lanes_at(REACH * 3 + c)]
    result_ref[120:128, :] = jnp.zeros((8, LANES), jnp.float32)
    for b in range(back_ref.shape[0]):
        lane = rows8(back_ref[b : b + 1, :])
        for g in range(16):
            feature_ref[g * 8 : g * 8 + 8, lanes_at(b)] = take(
                result_ref[g * 8 : g * 8 + 8, :], lane
            )
    out_ref[...] = jnp.transpose(feature_ref[...])


def coarse_pool(field_ref, first, pool_ref):
    own = field_ref.shape[2]
    for f in range(4):
        for c in range(3):
            for place, node, length in RUNS[f]:
                pool_ref[f, c * 10 + place : c * 10 + place + length, 0:own] = field_ref[
                    first + c, node : node + length, :
                ]


def halo_rows(below, above):
    half = lax.broadcasted_iota(jnp.int32, below.shape, 1) >= LANES // 2
    return pltpu.roll(jnp.where(half, below, above), LANES // 2, 1)


def coarse_halo(halo, store):
    for f in range(4):
        for c in range(3):
            for place, node, length in RUNS[f]:
                store(f, c * 10 + place, length, halo[c * 20 + node : c * 20 + node + length, :])


def coarse_flux(
    sources, number_of, mirror, nbr_ref, normals_ref, scale_ref, own_ref, flux_ref, jump_ref,
    sorted_ref, spread_ref, ends=None,
):
    own_blocks = flux_ref.shape[2] // LANES
    lane_number = lax.broadcasted_iota(jnp.int32, (8, LANES), 1)
    zero = jnp.zeros((8, LANES), jnp.float32)

    def one(eb, outer):
        at = lanes_at(eb)
        for f in range(4):
            code = rows8(nbr_ref[f : f + 1, at])
            which, lane = number_of(f, at, code)
            groups = gather32(sources, which, lane, [zero] * 4)
            if mirror:
                wall = code == 4 * (lane_number + eb * LANES) + f
                sign = jnp.where(wall, -1.0, 1.0)
                groups = [group * sign for group in groups]
            if outer:
                face = jnp.where(code >= 4 * own_blocks * LANES, code & 3, 4)
                groups = gather32(ends, face, (code >> 2) & (LANES - 1), groups)
            for g in range(4):
                jump_ref[f, g * 8 : g * 8 + 8, :] = (
                    groups[g] - own_ref[f, g * 8 : g * 8 + 8, at]
                )
        regroup(jump_ref, sorted_ref)
        scale = scale_ref[:, at]
        scaled = [normals_ref[c, :, at] * scale for c in range(3)]
        spread_normals(lambda c, f: scaled[c][f : f + 1, :], spread_ref)
        flux = crossed([spread_ref[c] for c in range(3)], [sorted_ref[c] for c in range(3)])
        for c in range(3):
            flux_ref[c, :, at] = flux[c]

    def inner(eb, carry):
        one(eb, False)
        return carry

    if ends is None:
        lax.fori_loop(0, own_blocks, inner, 0)
    else:
        one(0, True)
        lax.fori_loop(1, own_blocks - 1, inner, 0)
        one(own_blocks - 1, True)


def own_faces(pool_ref, own):
    blocks = own // LANES
    sources = [
        lambda g, n=n: pool_ref[n // blocks, g * 8 : g * 8 + 8, lanes_at(n % blocks)]
        for n in range(4 * blocks)
    ]

    def number_of(f, at, code):
        block = code >> 9
        which = jnp.where(block < blocks, (code & 3) * blocks + block, 4 * blocks)
        return which, (code >> 2) & (LANES - 1)

    return sources, number_of


def coarse_update(
    step, source, target, out, geometry_ref, derivatives_ref, lift_ref, stack_ref, flux_ref,
    grad_ref, lifted_ref,
):
    own_blocks = flux_ref.shape[2] // LANES
    stack_derivatives(derivatives_ref, stack_ref)
    lift = 0.5 * lift_ref[...]
    for c in range(3):
        grad_ref[c] = dot(stack_ref[...], source(c))
        lifted_ref[c] = dot(lift, flux_ref[c])

    def one(eb, carry):
        at = lanes_at(eb)

        def factor(m, a):
            return geometry_ref[3 * m + a : 3 * m + a + 1, at]

        def grad(a, c):
            return grad_ref[c, a * 24 : a * 24 + 20, at]

        for c in range(3):
            out(c, at, target(c, at) + step * (curl_part(c, factor, grad) + lifted_ref[c, :, at]))
        return carry

    lax.fori_loop(0, own_blocks, one, 0)


def early_kernel(
    fields_ref, home_ref, geometry_ref, normals_ref, scale_ref, nbr_ref, derivatives_ref, lift_ref,
    magnetic_ref, code_ref,
    pool_ref, flux_ref, jump_ref, sorted_ref, spread_ref, stack_ref, grad_ref, lifted_ref,
):
    own = fields_ref.shape[2]
    blocks = own // LANES
    coarse_pool(fields_ref, 0, pool_ref)
    sources, number_of = own_faces(pool_ref, own)
    coarse_flux(
        sources, number_of, True, nbr_ref, normals_ref, scale_ref, pool_ref, flux_ref, jump_ref,
        sorted_ref, spread_ref,
    )

    def out(c, at, value):
        magnetic_ref[c, :, at] = value

    coarse_update(
        -COARSE_STEP, lambda c: fields_ref[c], lambda c, at: fields_ref[3 + c, :, at], out,
        geometry_ref, derivatives_ref, lift_ref, stack_ref, flux_ref, grad_ref, lifted_ref,
    )
    width = jump_ref.shape[2] * 2

    def locate(eb, carry):
        at = lanes_at(eb)
        for f in range(4):
            code = rows8(nbr_ref[f : f + 1, at])
            home = jnp.full((8, LANES), -1, jnp.int32)
            for b in range(blocks):
                block = take(rows8(home_ref[b : b + 1, :]), (code >> 2) & (LANES - 1))
                home = jnp.where((code >> 9) == b, block, home)
            code_ref[f : f + 1, at] = jnp.where(home < 0, -1, (code & 3) * width + home)[0:1, :]
        return carry

    lax.fori_loop(0, blocks, locate, 0)


def merge_kernel(
    returned_ref, home_ref, slot_ref, before_ref, code_ref, magnetic_ref, fields_ref, below_ref,
    above_ref, geometry_ref, normals_ref, scale_ref, nbr_ref, derivatives_ref, lift_ref,
    merged_ref, ends_ref,
    flat_ref, back_ref, dense_ref, change_ref, fine_pool_ref, end_pool_ref,
    pool_ref, flux_ref, jump_ref, sorted_ref, spread_ref, stack_ref, grad_ref, lifted_ref,
):
    own = fields_ref.shape[2]
    slot_blocks = returned_ref.shape[0] // LANES
    dense_blocks = dense_ref.shape[1] // LANES
    back_ref[...] = jnp.transpose(returned_ref[...])
    for db in range(dense_blocks):
        slot = rows8(slot_ref[db : db + 1, :])
        lane = slot & (LANES - 1)
        hits = [(slot >> 7) == b for b in range(slot_blocks)]
        for group in range(15):
            rows = slice(group * 8, group * 8 + 8)
            value = jnp.zeros((8, LANES), jnp.float32)
            for b in range(slot_blocks):
                value = jnp.where(hits[b], take(back_ref[rows, lanes_at(b)], lane), value)
            dense_ref[rows, lanes_at(db)] = value
    for c in range(6):
        flat_ref[c * 20 : c * 20 + 20, :] = fields_ref[c]

    def merge(eb, carry):
        at = lanes_at(eb)
        home = rows8(home_ref[pl.ds(eb, 1), :])
        lane = home & (LANES - 1)
        hits = [(home >> 7) == b for b in range(dense_blocks)]
        for group in range(15):
            rows = slice(group * 8, group * 8 + 8)
            value = flat_ref[rows, at]
            for b in range(dense_blocks):
                value = jnp.where(hits[b], take(dense_ref[rows, lanes_at(b)], lane), value)
            flat_ref[rows, at] = value
        return carry

    lax.fori_loop(0, own // LANES, merge, 0)
    for c in range(6):
        merged_ref[c] = flat_ref[c * 20 : c * 20 + 20, :]
    for c in range(3):
        change_ref[c] = merged_ref[c] - fields_ref[c]
    coarse_pool(change_ref, 0, pool_ref)
    dense_ref[0:64, :] = dense_ref[0:64, :] - before_ref[...]
    for f in range(4):
        for c in range(3):
            for place, node, length in RUNS[f]:
                rows = slice(c * 10 + place, c * 10 + place + length)
                first = c * 20 + node
                fine_pool_ref[f, rows, :] = dense_ref[first : first + length, :]
    halo = halo_rows(below_ref[...], above_ref[...])

    def store(f, place, length, value):
        end_pool_ref[f, place : place + length, :] = value

    coarse_halo(halo, store)
    sources = [
        lambda g, n=n: fine_pool_ref[
            n // dense_blocks, g * 8 : g * 8 + 8, lanes_at(n % dense_blocks)
        ]
        for n in range(4 * dense_blocks)
    ]
    ends = [lambda g, f=f: end_pool_ref[f, g * 8 : g * 8 + 8, :] for f in range(4)]

    def number_of(f, at, code):
        fine = rows8(code_ref[f : f + 1, at])
        return fine >> 7, fine & (LANES - 1)

    coarse_flux(
        sources, number_of, True, nbr_ref, normals_ref, scale_ref, pool_ref, flux_ref, jump_ref,
        sorted_ref, spread_ref, ends,
    )

    def target(c, at):
        return magnetic_ref[c, :, at] + (merged_ref[3 + c, :, at] - fields_ref[3 + c, :, at])

    def out(c, at, value):
        merged_ref[3 + c, :, at] = value

    coarse_update(
        -COARSE_STEP, lambda c: change_ref[c], target, out,
        geometry_ref, derivatives_ref, lift_ref, stack_ref, flux_ref, grad_ref, lifted_ref,
    )
    low_half = lax.broadcasted_iota(jnp.int32, (20, LANES), 1) < LANES // 2
    for c in range(3):
        ends_ref[c * 20 : c * 20 + 20, :] = jnp.where(
            low_half, merged_ref[3 + c, :, 0:LANES], merged_ref[3 + c, :, own - LANES : own]
        )
    ends_ref[60:64, :] = jnp.zeros((4, LANES), jnp.float32)


def coarse_electric_kernel(
    merged_ref, geometry_ref, normals_ref, scale_ref, nbr_ref, derivatives_ref, lift_ref,
    out_ref,
    pool_ref, flux_ref, jump_ref, sorted_ref, spread_ref, stack_ref, grad_ref, lifted_ref,
):
    own = merged_ref.shape[2]
    coarse_pool(merged_ref, 3, pool_ref)
    sources, number_of = own_faces(pool_ref, own)
    coarse_flux(
        sources, number_of, False, nbr_ref, normals_ref, scale_ref, pool_ref, flux_ref, jump_ref,
        sorted_ref, spread_ref,
    )

    def out(c, at, value):
        out_ref[c, :, at] = value

    coarse_update(
        COARSE_STEP, lambda c: merged_ref[3 + c], lambda c, at: merged_ref[c, :, at], out,
        geometry_ref, derivatives_ref, lift_ref, stack_ref, flux_ref, grad_ref, lifted_ref,
    )


def finish_kernel(
    merged_ref, electric_ref, below_ref, above_ref, normals_ref, scale_ref, nbr_ref, lift_ref,
    out_ref,
    pool_ref, flux_ref, jump_ref, sorted_ref, spread_ref,
):
    own = merged_ref.shape[2]
    halo = halo_rows(below_ref[...], above_ref[...])

    def store(f, place, length, value):
        pool_ref[f, place : place + length, :] = value

    coarse_halo(halo, store)
    zero = jnp.zeros((8, LANES), jnp.float32)
    sources = [lambda g, f=f: pool_ref[f, g * 8 : g * 8 + 8, :] for f in range(4)]
    ends = (0, own // LANES - 1)
    for number, eb in enumerate(ends):
        at = lanes_at(eb)
        for f in range(4):
            code = rows8(nbr_ref[f : f + 1, at])
            which = jnp.where(code >= 4 * own, code & 3, 4)
            groups = gather32(sources, which, (code >> 2) & (LANES - 1), [zero] * 4)
            for g in range(4):
                jump_ref[f, g * 8 : g * 8 + 8, :] = groups[g]
        regroup(jump_ref, sorted_ref)
        scale = scale_ref[:, at]
        scaled = [normals_ref[c, :, at] * scale for c in range(3)]
        spread_normals(lambda c, f: scaled[c][f : f + 1, :], spread_ref)
        flux = crossed([spread_ref[c] for c in range(3)], [sorted_ref[c] for c in range(3)])
        for c in range(3):
            flux_ref[:, lanes_at(number * 3 + c)] = flux[c]
    lifted = dot(0.5 * lift_ref[...], flux_ref[...])
    for c in range(3):
        out_ref[c, :, LANES : own - LANES] = electric_ref[c, :, LANES : own - LANES]
        for number, eb in enumerate(ends):
            at = (number * 3 + c) * LANES
            out_ref[c, :, lanes_at(eb)] = (
                electric_ref[c, :, lanes_at(eb)] + COARSE_STEP * lifted[:, at : at + LANES]
            )
        out_ref[3 + c] = merged_ref[3 + c]


def call(kernel, outs, scratch, *args, hbm=(), smem=(), vmem=VMEM_BYTES):
    whole = pl.BlockSpec(memory_space=pltpu.VMEM)
    specs = [
        pl.BlockSpec(memory_space=pltpu.HBM if number in hbm else pltpu.SMEM if number in smem
                     else pltpu.VMEM)
        for number in range(len(args))
    ]
    return pl.pallas_call(
        kernel,
        out_shape=[jax.ShapeDtypeStruct(shape, dtype) for shape, dtype in outs],
        in_specs=specs,
        out_specs=[whole] * len(outs),
        scratch_shapes=[pltpu.VMEM(shape, dtype) for shape, dtype in scratch]
        + [pltpu.SemaphoreType.DMA(())] * len(hbm),
        compiler_params=pltpu.CompilerParams(vmem_limit_bytes=vmem),
    )(*args)


def device_of(block):
    sub = lax.axis_size("sub")
    return int(seats(lax.axis_size("dom"))[block // sub]) * sub + block % sub


def exchange(block):
    count = lax.axis_size(RING)
    up = [(i, (i + 1) % count) for i in range(count)]
    down = [(target, source) for source, target in up]
    return lax.ppermute(block, RING, up), lax.ppermute(block, RING, down)


def share(copies):
    count, size = lax.axis_size(RING), copies.shape[0]

    def within(start):
        groups = [
            [device_of((first + i + start) % count) for i in range(size)]
            for first in range(0, count, size)
        ]
        return lax.all_to_all(copies, RING, 0, 0, axis_index_groups=groups, tiled=True)

    return within(0), within(size // 2)


def spots(count, size):
    table = np.zeros((count, 16), np.int32)
    for block in range(count):
        for w in range(2 * REACH + 1):
            at = block % size + w - REACH
            if not 0 <= at < size:
                at = (block + size // 2) % size + w - REACH + size
            table[device_of(block), w] = at
    return table


def swap_slots(rows):
    width = rows.shape[-1]
    chunks = rows.reshape(lax.axis_size("dom"), -1, width)
    return lax.all_to_all(chunks, "dom", split_axis=0, concat_axis=0, tiled=True).reshape(-1, width)


def per_device(
    fields, geometry, normals, face_scale, derivatives, lift_matrix, face_nbr, send_rows,
    fine_slots, export_rows, fine_nbr,
):
    f32, i32 = jnp.float32, jnp.int32
    own = fields.shape[2]
    slots = send_rows.shape[0]
    fine = fine_slots.shape[0]
    width = export_rows.shape[1]
    table = jnp.concatenate(
        [
            fine_nbr,
            fine_slots.reshape(1, fine),
            jnp.pad(export_rows, ((0, 0), (0, fine - width))),
            jnp.zeros((1, fine), i32),
        ]
    )
    count = lax.axis_size(RING)
    table = lax.ppermute(table, RING, [(i, device_of(i)) for i in range(count)])
    me = lax.axis_index(RING)
    spot = lax.dynamic_index_in_dim(
        jnp.asarray(spots(count, 2 * REACH)), me, keepdims=False
    )
    traces = ((4, 32, fine), f32)
    send = send_rows.reshape(slots // LANES, LANES)
    order = slot_order(lax.axis_size("dom"), slots // lax.axis_size("dom"))
    dense = 2 * fine
    packed, ends, home, dense_slots, before = call(
        pack_kernel,
        [
            ((lax.axis_size("dom"), slots // lax.axis_size("dom"), 384), f32), ((64, LANES), f32),
            ((own // LANES, LANES), i32), ((dense // LANES, LANES), i32), ((64, dense), f32),
        ],
        [
            (send.shape, i32), (send.shape, i32), (fields.shape, f32), (face_nbr.shape, i32),
            (geometry.shape, f32), (normals.shape, f32), (face_scale.shape, f32),
            (send.shape, i32), (send.shape, i32), ((dense // LANES, LANES), i32),
            ((144, own), f32), ((8, own), i32), ((2, 4, 32, own), f32), ((384, dense), f32),
            ((384, LANES), f32),
        ],
        send, jnp.asarray(order.reshape(send.shape)), fields, face_nbr, geometry, normals,
        face_scale,
        hbm=range(7),
        vmem=PACK_VMEM_BYTES,
    )
    received = swap_slots(packed)
    ends_below, ends_above = exchange(ends)
    work = [
        ((3, 40, own), f32), ((4, 32, LANES), f32), ((3, 40, LANES), f32), ((3, 40, LANES), f32),
        ((72, 20), f32), ((3, 72, own), f32), ((3, 20, own), f32),
    ]
    early, fine_code = call(
        early_kernel,
        [((3, 20, own), f32), (face_nbr.shape, i32)],
        [((4, 32, own), f32)] + work,
        fields, home, geometry, normals, face_scale, face_nbr, derivatives, lift_matrix,
    )
    received, table, ends_below, ends_above, early, fine_code, spot = lax.optimization_barrier(
        (received, table, ends_below, ends_above, early, fine_code, spot)
    )
    group = 2 * REACH
    blocks = group + 1
    copies, back = call(
        functools.partial(unpack_kernel, width),
        [((group, 272, fine), f32), ((slots // LANES, LANES), i32)],
        [
            ((384, slots), f32), ((384, fine), f32), traces, ((3, 40, fine), f32),
            ((3, 40, fine), f32), ((40, 6 * fine), f32),
        ],
        received, table, lift_matrix,
    )
    window = [
        ((blocks, 272, fine), f32), ((20, blocks * 3 * fine), f32), ((20, blocks * 3 * fine), f32),
        ((blocks, 4, 32, fine), f32), ((blocks, 32, fine), f32), traces, ((3, 40, fine), f32),
        ((blocks, 3, 40, fine), f32), ((40, blocks * 3 * fine), f32),
        ((72, blocks * 3 * fine), f32), ((20, blocks * 3 * fine), f32), ((72, 20), f32),
    ]
    aligned, offset = share(copies)
    (copies,) = call(
        first_window_kernel,
        [((group, 120, fine), f32)],
        window,
        spot, aligned, offset, derivatives, lift_matrix,
        smem=(0,),
    )
    aligned_state, offset_state = share(copies)
    (outgoing,) = call(
        last_window_kernel,
        [((slots, LANES), f32)],
        [((128, fine), f32), ((128, slots), f32)] + window,
        spot, aligned, offset, aligned_state, offset_state, back, derivatives, lift_matrix,
        smem=(0,),
    )
    returned = swap_slots(outgoing)
    merged, ends = call(
        merge_kernel,
        [((6, 20, own), f32), ((64, LANES), f32)],
        [
            ((120, own), f32), ((128, slots), f32), ((120, dense), f32), ((3, 20, own), f32),
            ((4, 32, dense), f32), traces, ((4, 32, own), f32),
        ] + work,
        returned, home, dense_slots, before, fine_code, early, fields, ends_below, ends_above,
        geometry, normals, face_scale, face_nbr, derivatives, lift_matrix,
    )
    below, above = exchange(ends)
    (electric,) = call(
        coarse_electric_kernel,
        [((3, 20, own), f32)],
        [((4, 32, own), f32)] + work,
        merged, geometry, normals, face_scale, face_nbr, derivatives, lift_matrix,
    )
    (out,) = call(
        finish_kernel,
        [((6, 20, own), f32)],
        [
            traces, ((40, 6 * LANES), f32), ((4, 32, LANES), f32), ((3, 40, LANES), f32),
            ((3, 40, LANES), f32),
        ],
        merged, electric, below, above, normals, face_scale, face_nbr, lift_matrix,
    )
    return out


def solution(mesh):
    return jax.shard_map(
        per_device,
        mesh=mesh,
        in_specs=(
            P(None, None, ("dom", "sub")),
            P(None, ("dom", "sub")),
            P(None, None, ("dom", "sub")),
            P(None, ("dom", "sub")),
            P(),
            P(),
            P(None, ("dom", "sub")),
            P(("dom", "sub")),
            P(("dom", "sub")),
            P(None, ("dom", "sub")),
            P(None, ("dom", "sub")),
        ),
        out_specs=P(None, None, ("dom", "sub")),
        check_vma=False,
    )
```

```python
import functools

import jax
import jax.numpy as jnp
import numpy as np
from jax import lax
from jax.experimental import pallas as pl
from jax.experimental.pallas import tpu as pltpu
from jax.sharding import PartitionSpec as P

SUBSTEPS = 4
COARSE_STEP = 0.2
FINE_STEP = COARSE_STEP / SUBSTEPS
LANES = 128
VMEM_BYTES = 40 * 2**20
PACK_VMEM_BYTES = 60 * 2**20
RING = ("dom", "sub")
REACH = 4
highest = lax.Precision.HIGHEST


def face_table():
    places = [
        (along_r, along_s, along_t)
        for along_t in range(4)
        for along_s in range(4 - along_t)
        for along_r in range(4 - along_t - along_s)
    ]
    bottom = [i for i, at in enumerate(places) if at[2] == 0]
    front = [i for i, at in enumerate(places) if at[1] == 0]
    slanted = [i for i, at in enumerate(places) if sum(at) == 3]
    beside = [i for i, at in enumerate(places) if at[0] == 0]
    return [bottom, front, slanted, beside]


def runs_of(nodes):
    runs = []
    for place, node in enumerate(nodes):
        if runs and runs[-1][1] + runs[-1][2] == node:
            runs[-1][2] += 1
        else:
            runs.append([place, node, 1])
    return runs


RUNS = [runs_of(nodes) for nodes in face_table()]


def seat(block, rows, columns):
    chip, core = block // 2, block % 2
    y, z = chip // columns, chip % columns
    if y % 2:
        z, core = columns - 1 - z, 1 - core
    return (y * columns + z) * 2 + core


def seats(count):
    chips = count // 2
    rows = max(r for r in range(1, chips + 1) if chips % r == 0 and r * r <= chips)
    return np.array([seat(block, rows, chips // rows) for block in range(count)], np.int32)


def slot_order(count, cap):
    block_at = np.argsort(seats(count))
    return (block_at[:, None] * cap + np.arange(cap)[None, :]).reshape(-1).astype(np.int32)


def take(block, lane):
    return jnp.take_along_axis(block, lane, axis=1, mode="promise_in_bounds")


def rows8(row):
    return jnp.broadcast_to(row, (8, LANES))


def lanes_at(block):
    if isinstance(block, int):
        return slice(block * LANES, (block + 1) * LANES)
    return pl.ds(pl.multiple_of(block * LANES, LANES), LANES)


def gather32(sources, which, lane, start):
    groups = list(start)
    for number, source in enumerate(sources):
        hit = which == number
        for group in range(4):
            groups[group] = jnp.where(hit, take(source(group), lane), groups[group])
    return groups


def spread_normals(normal_rows, out_ref):
    for c in range(3):
        for f in range(4):
            out_ref[c, f * 10 : f * 10 + 10, :] = jnp.broadcast_to(normal_rows(c, f), (10, LANES))


def regroup(jump_ref, sorted_ref):
    for f in range(4):
        for c in range(3):
            sorted_ref[c, f * 10 : f * 10 + 10, :] = jump_ref[f, c * 10 : c * 10 + 10, :]


def crossed(normals, jumps):
    def part(c):
        a, b = (c + 1) % 3, (c + 2) % 3
        return normals[a] * jumps[b] - normals[b] * jumps[a]

    return [part(c) for c in range(3)]


def curl_part(c, factor, grad):
    m, n = (c + 1) % 3, (c + 2) % 3
    total = factor(m, 0) * grad(0, n) - factor(n, 0) * grad(0, m)
    for a in (1, 2):
        total += factor(m, a) * grad(a, n) - factor(n, a) * grad(a, m)
    return total


def stack_derivatives(derivatives_ref, out_ref):
    out_ref[...] = jnp.zeros_like(out_ref)
    for a in range(3):
        out_ref[a * 24 : a * 24 + 20, :] = derivatives_ref[a]


def dot(a, b):
    return jnp.dot(a, b, precision=highest, preferred_element_type=jnp.float32)


def inverse_of(row_of, count, width, none):
    columns = [
        jnp.transpose(jnp.broadcast_to(row_of(b), (LANES, LANES))) for b in range(count)
    ]
    lane = lax.broadcasted_iota(jnp.int32, (LANES, LANES), 1)
    number = lax.broadcasted_iota(jnp.int32, (LANES, LANES), 0)
    out = []
    for w in range(width):
        best = jnp.full((LANES, LANES), none, jnp.int32)
        for b in range(count):
            best = jnp.maximum(
                best, jnp.where(columns[b] == lane + w * LANES, number + b * LANES, none)
            )
        out.append(jnp.max(best, axis=0, keepdims=True))
    return out


def pack_kernel(
    plain_send_hbm, order_hbm, fields_hbm, nbr_hbm, geometry_hbm, normals_hbm, scale_hbm,
    out_ref, ends_ref, home_ref, slot_ref, before_ref,
    plain_send_ref, order_ref, fields_ref, nbr_ref, geometry_ref, normals_ref, scale_ref,
    send_ref, rank_ref, row_ref, flat_ref, nb_ref, pool_ref, dense_ref, feature_ref,
    *sems,
):
    pairs = [
        (plain_send_hbm, plain_send_ref), (order_hbm, order_ref), (fields_hbm, fields_ref),
        (nbr_hbm, nbr_ref), (geometry_hbm, geometry_ref), (normals_hbm, normals_ref),
        (scale_hbm, scale_ref),
    ]
    copies = [pltpu.make_async_copy(a, b, sem) for (a, b), sem in zip(pairs, sems)]
    for copy in copies:
        copy.start()
    copies[0].wait()
    copies[1].wait()
    own = fields_ref.shape[2]
    blocks = own // LANES
    send_blocks = plain_send_ref.shape[0]
    dense_blocks = dense_ref.shape[1] // LANES
    for sb in range(send_blocks):
        order = rows8(order_ref[sb : sb + 1, :])
        row = jnp.zeros((8, LANES), jnp.int32)
        for b in range(send_blocks):
            block = take(rows8(plain_send_ref[b : b + 1, :]), order & (LANES - 1))
            row = jnp.where((order >> 7) == b, block, row)
        send_ref[sb : sb + 1, :] = row[0:1, :]
    upper = lax.broadcasted_iota(jnp.int32, (LANES, LANES), 0) <= lax.broadcasted_iota(
        jnp.int32, (LANES, LANES), 1
    )
    upper = jnp.where(upper, 1.0, 0.0)
    total = jnp.full((8, LANES), -1.0, jnp.float32)
    for sb in range(send_blocks):
        filled = rows8(send_ref[sb : sb + 1, :]) < own
        counts = jnp.where(filled, 1.0, 0.0)
        rank = total + dot(counts, upper)
        total += jnp.sum(counts, axis=1, keepdims=True)
        rank = jnp.where(filled, rank.astype(jnp.int32), LANES * LANES)
        rank_ref[sb : sb + 1, :] = rank[0:1, :]
    slots = inverse_of(lambda b: rank_ref[b : b + 1, :], send_blocks, dense_blocks, -1)
    for b in range(dense_blocks):
        slot_ref[b : b + 1, :] = slots[b]
        slot = rows8(slots[b])
        row = jnp.full((8, LANES), LANES * LANES, jnp.int32)
        for sb in range(send_blocks):
            block = take(rows8(send_ref[sb : sb + 1, :]), slot & (LANES - 1))
            row = jnp.where((slot >> 7) == sb, block, row)
        row_ref[b : b + 1, :] = row[0:1, :]
    homes = inverse_of(lambda b: row_ref[b : b + 1, :], dense_blocks, blocks, -1)
    for b in range(blocks):
        home_ref[b : b + 1, :] = homes[b]
    for copy in copies[2:]:
        copy.wait()
    for c in range(6):
        flat_ref[c * 20 : c * 20 + 20, :] = fields_ref[c]
    flat_ref[120:129, :] = geometry_ref[...]
    for c in range(3):
        flat_ref[129 + 4 * c : 133 + 4 * c, :] = normals_ref[c] * scale_ref[...]
    flat_ref[141:144, :] = jnp.zeros((3, own), jnp.float32)
    nb_ref[0:4, :] = nbr_ref[...]
    nb_ref[4:8, :] = nbr_ref[...]
    low_half = lax.broadcasted_iota(jnp.int32, (20, LANES), 1) < LANES // 2
    for c in range(3):
        ends_ref[c * 20 : c * 20 + 20, :] = jnp.where(
            low_half, fields_ref[c, :, 0:LANES], fields_ref[c, :, own - LANES : own]
        )
    ends_ref[60:64, :] = jnp.zeros((4, LANES), jnp.float32)
    for eh in range(2):
        for f in range(4):
            for c in range(3):
                for place, node, length in RUNS[f]:
                    pool_ref[eh, f, c * 10 + place : c * 10 + place + length, :] = fields_ref[
                        eh * 3 + c, node : node + length, :
                    ]
            pool_ref[eh, f, 30:32, :] = jnp.zeros((2, own), jnp.float32)
    sublane = lax.broadcasted_iota(jnp.int32, (8, LANES), 0)

    def pick(db, carry):
        row = rows8(jnp.minimum(row_ref[pl.ds(db, 1), :], own - 1))
        lane, which = row & (LANES - 1), row >> 7
        hits = [which == b for b in range(blocks)]
        for group in range(18):
            rows = slice(group * 8, group * 8 + 8)
            value = take(flat_ref[rows, 0:LANES], lane)
            for b in range(1, blocks):
                value = jnp.where(hits[b], take(flat_ref[rows, lanes_at(b)], lane), value)
            dense_ref[rows, lanes_at(db)] = value
        nbr = take(nb_ref[:, 0:LANES], lane)
        for b in range(1, blocks):
            nbr = jnp.where(hits[b], take(nb_ref[:, lanes_at(b)], lane), nbr)
        wall = jnp.where(nbr == 4 * row + sublane, -1.0, 1.0)
        for f in range(4):
            code = rows8(nbr[f : f + 1, :])
            sign = rows8(wall[f : f + 1, :])
            lane_f = (code >> 2) & (LANES - 1)
            which_f = (code & 3) * blocks + (code >> 9)
            groups = [jnp.zeros((8, LANES), jnp.float32)] * 8
            for number in range(4 * blocks):
                hit = which_f == number
                for group in range(8):
                    block = pool_ref[
                        group // 4,
                        number // blocks,
                        group % 4 * 8 : group % 4 * 8 + 8,
                        lanes_at(number % blocks),
                    ]
                    groups[group] = jnp.where(hit, take(block, lane_f), groups[group])
            for group in range(8):
                value = groups[group] * sign if group < 4 else groups[group]
                length = 8 if group % 4 < 3 else 6
                at = 144 + (group // 4 * 4 + f) * 30 + group % 4 * 8
                dense_ref[at : at + length, lanes_at(db)] = value[:length]
        return carry

    lax.fori_loop(0, dense_blocks, pick, 0)
    before_ref[...] = dense_ref[0:64, :]
    chunks = LANES * out_ref.shape[0] // (send_blocks * LANES)
    for sb in range(send_blocks):
        rank = rows8(rank_ref[sb : sb + 1, :])
        lane = rank & (LANES - 1)
        hits = [(rank >> 7) == b for b in range(dense_blocks)]
        for group in range(dense_ref.shape[0] // 8):
            rows = slice(group * 8, group * 8 + 8)
            value = jnp.zeros((8, LANES), jnp.float32)
            for b in range(dense_blocks):
                value = jnp.where(hits[b], take(dense_ref[rows, lanes_at(b)], lane), value)
            feature_ref[rows, :] = value
        out_ref[sb * chunks : (sb + 1) * chunks] = jnp.transpose(feature_ref[...]).reshape(
            chunks, LANES // chunks, feature_ref.shape[0]
        )


def unpack_kernel(
    width, received_ref, table_ref, lift_ref,
    out_ref, back_ref,
    feature_ref, picked_ref, held_ref, sorted_ref, normal_ref, flux_ref,
):
    nbr_ref, slots_ref = table_ref.at[0:4], table_ref.at[4:5]
    slot_blocks = received_ref.shape[0] // LANES
    feature_ref[...] = jnp.transpose(received_ref[...])
    slot = rows8(slots_ref[...])
    lane, which = slot & (LANES - 1), slot >> 7
    hits = [which == b for b in range(slot_blocks)]
    for group in range(feature_ref.shape[0] // 8):
        at = slice(group * 8, group * 8 + 8)
        value = take(feature_ref[at, 0:LANES], lane)
        for b in range(1, slot_blocks):
            value = jnp.where(hits[b], take(feature_ref[at, lanes_at(b)], lane), value)
        picked_ref[at, :] = value
    spread_normals(lambda c, f: picked_ref[129 + 4 * c + f : 130 + 4 * c + f, :], normal_ref)
    frozen_code = 4 * LANES + 4 * 2 * width
    for eh in range(2):
        for f in range(4):
            frozen = jnp.broadcast_to(nbr_ref[f : f + 1, :] == frozen_code, (30, LANES))
            at = 144 + (eh * 4 + f) * 30
            held_ref[f, 0:30, :] = jnp.where(frozen, picked_ref[at : at + 30, :], 0.0)
        regroup(held_ref, sorted_ref)
        flux = crossed([normal_ref[c] for c in range(3)], [sorted_ref[c] for c in range(3)])
        for c in range(3):
            flux_ref[:, lanes_at(eh * 3 + c)] = flux[c]
    lifted = dot(0.5 * lift_ref[...], flux_ref[...])
    place = lax.broadcasted_iota(jnp.int32, (8, LANES), 1)
    both = take(table_ref[...], (place >> 2) & (width - 1))
    lane = jnp.where(place < LANES // 2, rows8(both[6:7, :]), rows8(both[5:6, :]))
    picked_ref[144:264, :] = jnp.concatenate(
        [lifted[:, k * LANES : (k + 1) * LANES] for k in range(6)]
    )
    picked_ref[264:268, :] = nbr_ref[...].astype(jnp.float32)
    picked_ref[268:272, :] = lane[0:4, :].astype(jnp.float32)
    for k in range(out_ref.shape[0]):
        out_ref[k] = picked_ref[0:272, :]
    backs = inverse_of(lambda b: slots_ref[...], 1, slot_blocks, 0)
    for b in range(slot_blocks):
        back_ref[b : b + 1, :] = backs[b]


def window_state(spot_ref, parts, rows, block_ref):
    size = parts[0].shape[0]

    def fetch(w, carry):
        spot = spot_ref[w]
        for number, part in enumerate(parts):

            @pl.when((spot >= number * size) & (spot < number * size + size))
            def _(number=number, part=part):
                block_ref[w, 0:rows, :] = part[spot - number * size, 0:rows, :]

        return carry

    lax.fori_loop(0, 2 * REACH + 1, fetch, 0)


def window_steps(
    derivatives_ref, lift_ref, block_ref, efield_ref, hfield_ref, pool_ref, export_ref, jump_ref,
    sorted_ref, spread_ref, flux_ref, grad_ref, lifted_ref, stack_ref,
):
    blocks = 2 * REACH + 1
    stack_derivatives(derivatives_ref, stack_ref)
    lift = 0.5 * lift_ref[...]
    half_lanes = lax.broadcasted_iota(jnp.int32, (8, LANES), 1) < LANES // 2
    face = lax.broadcasted_iota(jnp.int32, (8, LANES), 1) & 3
    zero = jnp.zeros((8, LANES), jnp.float32)

    def prepare(w, carry):
        for c in range(3):
            efield_ref[:, lanes_at(w * 3 + c)] = block_ref[w, c * 20 : c * 20 + 20, :]
            hfield_ref[:, lanes_at(w * 3 + c)] = block_ref[w, 60 + c * 20 : 80 + c * 20, :]
        spread_normals(
            lambda c, f: block_ref[w, 129 + 4 * c + f : 130 + 4 * c + f, :], spread_ref.at[w]
        )
        return carry

    lax.fori_loop(0, blocks, prepare, 0)
    for level in range(1, REACH + 1):
        magnetic = level % 2 == 1
        source_ref, target_ref = (efield_ref, hfield_ref) if magnetic else (hfield_ref, efield_ref)
        step = -FINE_STEP if magnetic else FINE_STEP
        held = 144 if magnetic else 204
        first, last = level, blocks - level

        def expose(w, carry, source_ref=source_ref):
            for f in range(4):
                for c in range(3):
                    for place, node, length in RUNS[f]:
                        pool_ref[w, f, c * 10 + place : c * 10 + place + length, :] = source_ref[
                            node : node + length, lanes_at(w * 3 + c)
                        ]
            lane = rows8(block_ref[w, 268:269, :]).astype(jnp.int32)
            groups = gather32(
                [lambda g, f=f: pool_ref[w, f, g * 8 : g * 8 + 8, :] for f in range(4)],
                face, lane, [zero] * 4,
            )
            for g in range(4):
                export_ref[w, g * 8 : g * 8 + 8, :] = groups[g]
            return carry

        lax.fori_loop(first - 1, last + 1, expose, 0)

        def gather(w, carry):
            sources = [
                lambda g, f=f: pool_ref[w, f, g * 8 : g * 8 + 8, :] for f in range(4)
            ]
            halo = [
                jnp.where(
                    half_lanes,
                    export_ref[w - 1, g * 8 : g * 8 + 8, :],
                    export_ref[w + 1, g * 8 : g * 8 + 8, :],
                )
                for g in range(4)
            ]
            sources.append(lambda g: halo[g])
            for f in range(4):
                code = rows8(block_ref[w, 264 + f : 265 + f, :]).astype(jnp.int32)
                local = code < 4 * LANES
                which = jnp.where(local, code & 3, code >> 7)
                lane = jnp.where(local, code >> 2, code) & (LANES - 1)
                groups = gather32(sources, which, lane, [zero] * 4)
                for g in range(4):
                    jump_ref[f, g * 8 : g * 8 + 8, :] = (
                        groups[g] - pool_ref[w, f, g * 8 : g * 8 + 8, :]
                    )
            regroup(jump_ref, sorted_ref)
            flux = crossed([spread_ref[w, c] for c in range(3)], [sorted_ref[c] for c in range(3)])
            for c in range(3):
                flux_ref[:, lanes_at(w * 3 + c)] = flux[c]
            return carry

        lax.fori_loop(first, last, gather, 0)
        span = slice(first * 3 * LANES, last * 3 * LANES)
        grad_ref[:, span] = dot(stack_ref[...], source_ref[:, span])
        lifted_ref[:, span] = dot(lift, flux_ref[:, span])

        def update(w, carry, target_ref=target_ref, step=step, held=held):
            def factor(m, a):
                return block_ref[w, 120 + 3 * m + a : 121 + 3 * m + a, :]

            def grad(a, c):
                return grad_ref[a * 24 : a * 24 + 20, lanes_at(w * 3 + c)]

            for c in range(3):
                at = lanes_at(w * 3 + c)
                rate = (
                    curl_part(c, factor, grad)
                    + lifted_ref[:, at]
                    + block_ref[w, held + c * 20 : held + c * 20 + 20, :]
                )
                target_ref[:, at] = target_ref[:, at] + step * rate
            return carry

        lax.fori_loop(first, last, update, 0)


def first_window_kernel(
    spot_ref, row_ref, next_ref, twin_ref, derivatives_ref, lift_ref,
    out_ref,
    block_ref, efield_ref, hfield_ref, *scratch,
):
    window_state(spot_ref, (row_ref, next_ref, twin_ref), 272, block_ref)
    window_steps(derivatives_ref, lift_ref, block_ref, efield_ref, hfield_ref, *scratch)
    for c in range(3):
        electric = efield_ref[:, lanes_at(REACH * 3 + c)]
        magnetic = hfield_ref[:, lanes_at(REACH * 3 + c)]
        for k in range(out_ref.shape[0]):
            out_ref[k, c * 20 : c * 20 + 20, :] = electric
            out_ref[k, 60 + c * 20 : 80 + c * 20, :] = magnetic


def last_window_kernel(
    spot_ref, row_ref, next_ref, twin_ref, row_state_ref, next_state_ref, twin_state_ref,
    back_ref, derivatives_ref, lift_ref,
    out_ref,
    result_ref, feature_ref, block_ref, efield_ref, hfield_ref, *scratch,
):
    window_state(spot_ref, (row_ref, next_ref, twin_ref), 272, block_ref)
    window_state(spot_ref, (row_state_ref, next_state_ref, twin_state_ref), 120, block_ref)
    window_steps(derivatives_ref, lift_ref, block_ref, efield_ref, hfield_ref, *scratch)
    for c in range(3):
        result_ref[c * 20 : c * 20 + 20, :] = efield_ref[:, lanes_at(REACH * 3 + c)]
        result_ref[60 + c * 20 : 80 + c * 20, :] = hfield_ref[:, lanes_at(REACH * 3 + c)]
    result_ref[120:128, :] = jnp.zeros((8, LANES), jnp.float32)
    for b in range(back_ref.shape[0]):
        lane = rows8(back_ref[b : b + 1, :])
        for g in range(16):
            feature_ref[g * 8 : g * 8 + 8, lanes_at(b)] = take(
                result_ref[g * 8 : g * 8 + 8, :], lane
            )
    out_ref[...] = jnp.transpose(feature_ref[...])


def coarse_pool(field_ref, first, pool_ref):
    own = field_ref.shape[2]
    for f in range(4):
        for c in range(3):
            for place, node, length in RUNS[f]:
                pool_ref[f, c * 10 + place : c * 10 + place + length, 0:own] = field_ref[
                    first + c, node : node + length, :
                ]


def halo_rows(below, above):
    half = lax.broadcasted_iota(jnp.int32, below.shape, 1) >= LANES // 2
    return pltpu.roll(jnp.where(half, below, above), LANES // 2, 1)


def coarse_halo(halo, store):
    for f in range(4):
        for c in range(3):
            for place, node, length in RUNS[f]:
                store(f, c * 10 + place, length, halo[c * 20 + node : c * 20 + node + length, :])


def coarse_flux(
    sources, number_of, mirror, nbr_ref, normals_ref, scale_ref, own_ref, flux_ref, jump_ref,
    sorted_ref, spread_ref, ends=None,
):
    own_blocks = flux_ref.shape[2] // LANES
    lane_number = lax.broadcasted_iota(jnp.int32, (8, LANES), 1)
    zero = jnp.zeros((8, LANES), jnp.float32)

    def one(eb, outer):
        at = lanes_at(eb)
        for f in range(4):
            code = rows8(nbr_ref[f : f + 1, at])
            which, lane = number_of(f, at, code)
            groups = gather32(sources, which, lane, [zero] * 4)
            if mirror:
                wall = code == 4 * (lane_number + eb * LANES) + f
                sign = jnp.where(wall, -1.0, 1.0)
                groups = [group * sign for group in groups]
            if outer:
                face = jnp.where(code >= 4 * own_blocks * LANES, code & 3, 4)
                groups = gather32(ends, face, (code >> 2) & (LANES - 1), groups)
            for g in range(4):
                jump_ref[f, g * 8 : g * 8 + 8, :] = (
                    groups[g] - own_ref[f, g * 8 : g * 8 + 8, at]
                )
        regroup(jump_ref, sorted_ref)
        scale = scale_ref[:, at]
        scaled = [normals_ref[c, :, at] * scale for c in range(3)]
        spread_normals(lambda c, f: scaled[c][f : f + 1, :], spread_ref)
        flux = crossed([spread_ref[c] for c in range(3)], [sorted_ref[c] for c in range(3)])
        for c in range(3):
            flux_ref[c, :, at] = flux[c]

    def inner(eb, carry):
        one(eb, False)
        return carry

    if ends is None:
        lax.fori_loop(0, own_blocks, inner, 0)
    else:
        one(0, True)
        lax.fori_loop(1, own_blocks - 1, inner, 0)
        one(own_blocks - 1, True)


def own_faces(pool_ref, own):
    blocks = own // LANES
    sources = [
        lambda g, n=n: pool_ref[n // blocks, g * 8 : g * 8 + 8, lanes_at(n % blocks)]
        for n in range(4 * blocks)
    ]

    def number_of(f, at, code):
        block = code >> 9
        which = jnp.where(block < blocks, (code & 3) * blocks + block, 4 * blocks)
        return which, (code >> 2) & (LANES - 1)

    return sources, number_of


def coarse_update(
    step, source, target, out, geometry_ref, derivatives_ref, lift_ref, stack_ref, flux_ref,
    grad_ref, lifted_ref,
):
    own_blocks = flux_ref.shape[2] // LANES
    stack_derivatives(derivatives_ref, stack_ref)
    lift = 0.5 * lift_ref[...]
    for c in range(3):
        grad_ref[c] = dot(stack_ref[...], source(c))
        lifted_ref[c] = dot(lift, flux_ref[c])

    def one(eb, carry):
        at = lanes_at(eb)

        def factor(m, a):
            return geometry_ref[3 * m + a : 3 * m + a + 1, at]

        def grad(a, c):
            return grad_ref[c, a * 24 : a * 24 + 20, at]

        for c in range(3):
            out(c, at, target(c, at) + step * (curl_part(c, factor, grad) + lifted_ref[c, :, at]))
        return carry

    lax.fori_loop(0, own_blocks, one, 0)


def early_kernel(
    fields_ref, home_ref, geometry_ref, normals_ref, scale_ref, nbr_ref, derivatives_ref, lift_ref,
    magnetic_ref, code_ref,
    pool_ref, flux_ref, jump_ref, sorted_ref, spread_ref, stack_ref, grad_ref, lifted_ref,
):
    own = fields_ref.shape[2]
    blocks = own // LANES
    coarse_pool(fields_ref, 0, pool_ref)
    sources, number_of = own_faces(pool_ref, own)
    coarse_flux(
        sources, number_of, True, nbr_ref, normals_ref, scale_ref, pool_ref, flux_ref, jump_ref,
        sorted_ref, spread_ref,
    )

    def out(c, at, value):
        magnetic_ref[c, :, at] = value

    coarse_update(
        -COARSE_STEP, lambda c: fields_ref[c], lambda c, at: fields_ref[3 + c, :, at], out,
        geometry_ref, derivatives_ref, lift_ref, stack_ref, flux_ref, grad_ref, lifted_ref,
    )
    width = jump_ref.shape[2] * 2

    def locate(eb, carry):
        at = lanes_at(eb)
        for f in range(4):
            code = rows8(nbr_ref[f : f + 1, at])
            home = jnp.full((8, LANES), -1, jnp.int32)
            for b in range(blocks):
                block = take(rows8(home_ref[b : b + 1, :]), (code >> 2) & (LANES - 1))
                home = jnp.where((code >> 9) == b, block, home)
            code_ref[f : f + 1, at] = jnp.where(home < 0, -1, (code & 3) * width + home)[0:1, :]
        return carry

    lax.fori_loop(0, blocks, locate, 0)


def merge_kernel(
    returned_ref, home_ref, slot_ref, before_ref, code_ref, magnetic_ref, fields_ref, below_ref,
    above_ref, geometry_ref, normals_ref, scale_ref, nbr_ref, derivatives_ref, lift_ref,
    merged_ref, ends_ref,
    flat_ref, back_ref, dense_ref, change_ref, fine_pool_ref, end_pool_ref,
    pool_ref, flux_ref, jump_ref, sorted_ref, spread_ref, stack_ref, grad_ref, lifted_ref,
):
    own = fields_ref.shape[2]
    slot_blocks = returned_ref.shape[0] // LANES
    dense_blocks = dense_ref.shape[1] // LANES
    back_ref[...] = jnp.transpose(returned_ref[...])
    for db in range(dense_blocks):
        slot = rows8(slot_ref[db : db + 1, :])
        lane = slot & (LANES - 1)
        hits = [(slot >> 7) == b for b in range(slot_blocks)]
        for group in range(15):
            rows = slice(group * 8, group * 8 + 8)
            value = jnp.zeros((8, LANES), jnp.float32)
            for b in range(slot_blocks):
                value = jnp.where(hits[b], take(back_ref[rows, lanes_at(b)], lane), value)
            dense_ref[rows, lanes_at(db)] = value
    for c in range(6):
        flat_ref[c * 20 : c * 20 + 20, :] = fields_ref[c]

    def merge(eb, carry):
        at = lanes_at(eb)
        home = rows8(home_ref[pl.ds(eb, 1), :])
        lane = home & (LANES - 1)
        hits = [(home >> 7) == b for b in range(dense_blocks)]
        for group in range(15):
            rows = slice(group * 8, group * 8 + 8)
            value = flat_ref[rows, at]
            for b in range(dense_blocks):
                value = jnp.where(hits[b], take(dense_ref[rows, lanes_at(b)], lane), value)
            flat_ref[rows, at] = value
        return carry

    lax.fori_loop(0, own // LANES, merge, 0)
    for c in range(6):
        merged_ref[c] = flat_ref[c * 20 : c * 20 + 20, :]
    for c in range(3):
        change_ref[c] = merged_ref[c] - fields_ref[c]
    coarse_pool(change_ref, 0, pool_ref)
    dense_ref[0:64, :] = dense_ref[0:64, :] - before_ref[...]
    for f in range(4):
        for c in range(3):
            for place, node, length in RUNS[f]:
                rows = slice(c * 10 + place, c * 10 + place + length)
                first = c * 20 + node
                fine_pool_ref[f, rows, :] = dense_ref[first : first + length, :]
    halo = halo_rows(below_ref[...], above_ref[...])

    def store(f, place, length, value):
        end_pool_ref[f, place : place + length, :] = value

    coarse_halo(halo, store)
    sources = [
        lambda g, n=n: fine_pool_ref[
            n // dense_blocks, g * 8 : g * 8 + 8, lanes_at(n % dense_blocks)
        ]
        for n in range(4 * dense_blocks)
    ]
    ends = [lambda g, f=f: end_pool_ref[f, g * 8 : g * 8 + 8, :] for f in range(4)]

    def number_of(f, at, code):
        fine = rows8(code_ref[f : f + 1, at])
        return fine >> 7, fine & (LANES - 1)

    coarse_flux(
        sources, number_of, True, nbr_ref, normals_ref, scale_ref, pool_ref, flux_ref, jump_ref,
        sorted_ref, spread_ref, ends,
    )

    def target(c, at):
        return magnetic_ref[c, :, at] + (merged_ref[3 + c, :, at] - fields_ref[3 + c, :, at])

    def out(c, at, value):
        merged_ref[3 + c, :, at] = value

    coarse_update(
        -COARSE_STEP, lambda c: change_ref[c], target, out,
        geometry_ref, derivatives_ref, lift_ref, stack_ref, flux_ref, grad_ref, lifted_ref,
    )
    low_half = lax.broadcasted_iota(jnp.int32, (20, LANES), 1) < LANES // 2
    for c in range(3):
        ends_ref[c * 20 : c * 20 + 20, :] = jnp.where(
            low_half, merged_ref[3 + c, :, 0:LANES], merged_ref[3 + c, :, own - LANES : own]
        )
    ends_ref[60:64, :] = jnp.zeros((4, LANES), jnp.float32)


def coarse_electric_kernel(
    merged_ref, geometry_ref, normals_ref, scale_ref, nbr_ref, derivatives_ref, lift_ref,
    out_ref,
    pool_ref, flux_ref, jump_ref, sorted_ref, spread_ref, stack_ref, grad_ref, lifted_ref,
):
    own = merged_ref.shape[2]
    coarse_pool(merged_ref, 3, pool_ref)
    sources, number_of = own_faces(pool_ref, own)
    coarse_flux(
        sources, number_of, False, nbr_ref, normals_ref, scale_ref, pool_ref, flux_ref, jump_ref,
        sorted_ref, spread_ref,
    )

    def out(c, at, value):
        out_ref[c, :, at] = value

    coarse_update(
        COARSE_STEP, lambda c: merged_ref[3 + c], lambda c, at: merged_ref[c, :, at], out,
        geometry_ref, derivatives_ref, lift_ref, stack_ref, flux_ref, grad_ref, lifted_ref,
    )


def finish_kernel(
    merged_ref, electric_ref, below_ref, above_ref, normals_ref, scale_ref, nbr_ref, lift_ref,
    out_ref,
    pool_ref, flux_ref, jump_ref, sorted_ref, spread_ref,
):
    own = merged_ref.shape[2]
    halo = halo_rows(below_ref[...], above_ref[...])

    def store(f, place, length, value):
        pool_ref[f, place : place + length, :] = value

    coarse_halo(halo, store)
    zero = jnp.zeros((8, LANES), jnp.float32)
    sources = [lambda g, f=f: pool_ref[f, g * 8 : g * 8 + 8, :] for f in range(4)]
    ends = (0, own // LANES - 1)
    for number, eb in enumerate(ends):
        at = lanes_at(eb)
        for f in range(4):
            code = rows8(nbr_ref[f : f + 1, at])
            which = jnp.where(code >= 4 * own, code & 3, 4)
            groups = gather32(sources, which, (code >> 2) & (LANES - 1), [zero] * 4)
            for g in range(4):
                jump_ref[f, g * 8 : g * 8 + 8, :] = groups[g]
        regroup(jump_ref, sorted_ref)
        scale = scale_ref[:, at]
        scaled = [normals_ref[c, :, at] * scale for c in range(3)]
        spread_normals(lambda c, f: scaled[c][f : f + 1, :], spread_ref)
        flux = crossed([spread_ref[c] for c in range(3)], [sorted_ref[c] for c in range(3)])
        for c in range(3):
            flux_ref[:, lanes_at(number * 3 + c)] = flux[c]
    lifted = dot(0.5 * lift_ref[...], flux_ref[...])
    for c in range(3):
        out_ref[c, :, LANES : own - LANES] = electric_ref[c, :, LANES : own - LANES]
        for number, eb in enumerate(ends):
            at = (number * 3 + c) * LANES
            out_ref[c, :, lanes_at(eb)] = (
                electric_ref[c, :, lanes_at(eb)] + COARSE_STEP * lifted[:, at : at + LANES]
            )
        out_ref[3 + c] = merged_ref[3 + c]


def call(kernel, outs, scratch, *args, hbm=(), smem=(), vmem=VMEM_BYTES):
    whole = pl.BlockSpec(memory_space=pltpu.VMEM)
    specs = [
        pl.BlockSpec(memory_space=pltpu.HBM if number in hbm else pltpu.SMEM if number in smem
                     else pltpu.VMEM)
        for number in range(len(args))
    ]
    return pl.pallas_call(
        kernel,
        out_shape=[jax.ShapeDtypeStruct(shape, dtype) for shape, dtype in outs],
        in_specs=specs,
        out_specs=[whole] * len(outs),
        scratch_shapes=[pltpu.VMEM(shape, dtype) for shape, dtype in scratch]
        + [pltpu.SemaphoreType.DMA(())] * len(hbm),
        compiler_params=pltpu.CompilerParams(vmem_limit_bytes=vmem),
    )(*args)


def device_of(block):
    sub = lax.axis_size("sub")
    return int(seats(lax.axis_size("dom"))[block // sub]) * sub + block % sub


def exchange(block):
    count = lax.axis_size(RING)
    up = [(i, (i + 1) % count) for i in range(count)]
    down = [(target, source) for source, target in up]
    return lax.ppermute(block, RING, up), lax.ppermute(block, RING, down)


def share(copies):
    row = lax.all_to_all(copies, "sub", 0, 0, tiled=True)
    count = lax.axis_size("dom")
    seat_of = seats(count)

    def swap(partner):
        pairs = [(int(seat_of[d]), int(seat_of[partner(d) % count])) for d in range(count)]
        return lax.ppermute(row, "dom", pairs)

    return row, swap(lambda d: d - 1 if d % 2 == 0 else d + 1), swap(lambda d: d ^ 1)


def spots(count, size):
    table = np.zeros((count, 16), np.int32)
    for block in range(count):
        d, s = divmod(block, size)
        for w in range(2 * REACH + 1):
            step, at = divmod(s + w - REACH, size)
            part = 0 if step == 0 else 2 if (d + step) % count == d ^ 1 else 1
            table[device_of(block), w] = part * size + at
    return table


def swap_slots(rows):
    width = rows.shape[-1]
    chunks = rows.reshape(lax.axis_size("dom"), -1, width)
    return lax.all_to_all(chunks, "dom", split_axis=0, concat_axis=0, tiled=True).reshape(-1, width)


def per_device(
    fields, geometry, normals, face_scale, derivatives, lift_matrix, face_nbr, send_rows,
    fine_slots, export_rows, fine_nbr,
):
    f32, i32 = jnp.float32, jnp.int32
    own = fields.shape[2]
    slots = send_rows.shape[0]
    fine = fine_slots.shape[0]
    width = export_rows.shape[1]
    table = jnp.concatenate(
        [
            fine_nbr,
            fine_slots.reshape(1, fine),
            jnp.pad(export_rows, ((0, 0), (0, fine - width))),
            jnp.zeros((1, fine), i32),
        ]
    )
    count = lax.axis_size(RING)
    table = lax.ppermute(table, RING, [(i, device_of(i)) for i in range(count)])
    me = lax.axis_index(RING)
    spot = lax.dynamic_index_in_dim(
        jnp.asarray(spots(count, lax.axis_size("sub"))), me, keepdims=False
    )
    traces = ((4, 32, fine), f32)
    send = send_rows.reshape(slots // LANES, LANES)
    order = slot_order(lax.axis_size("dom"), slots // lax.axis_size("dom"))
    dense = 2 * fine
    packed, ends, home, dense_slots, before = call(
        pack_kernel,
        [
            ((lax.axis_size("dom"), slots // lax.axis_size("dom"), 384), f32), ((64, LANES), f32),
            ((own // LANES, LANES), i32), ((dense // LANES, LANES), i32), ((64, dense), f32),
        ],
        [
            (send.shape, i32), (send.shape, i32), (fields.shape, f32), (face_nbr.shape, i32),
            (geometry.shape, f32), (normals.shape, f32), (face_scale.shape, f32),
            (send.shape, i32), (send.shape, i32), ((dense // LANES, LANES), i32),
            ((144, own), f32), ((8, own), i32), ((2, 4, 32, own), f32), ((384, dense), f32),
            ((384, LANES), f32),
        ],
        send, jnp.asarray(order.reshape(send.shape)), fields, face_nbr, geometry, normals,
        face_scale,
        hbm=range(7),
        vmem=PACK_VMEM_BYTES,
    )
    received = swap_slots(packed)
    ends_below, ends_above = exchange(ends)
    work = [
        ((3, 40, own), f32), ((4, 32, LANES), f32), ((3, 40, LANES), f32), ((3, 40, LANES), f32),
        ((72, 20), f32), ((3, 72, own), f32), ((3, 20, own), f32),
    ]
    early, fine_code = call(
        early_kernel,
        [((3, 20, own), f32), (face_nbr.shape, i32)],
        [((4, 32, own), f32)] + work,
        fields, home, geometry, normals, face_scale, face_nbr, derivatives, lift_matrix,
    )
    received, table, ends_below, ends_above, early, fine_code, spot = lax.optimization_barrier(
        (received, table, ends_below, ends_above, early, fine_code, spot)
    )
    group = lax.axis_size("sub")
    blocks = 2 * REACH + 1
    copies, back = call(
        functools.partial(unpack_kernel, width),
        [((group, 272, fine), f32), ((slots // LANES, LANES), i32)],
        [
            ((384, slots), f32), ((384, fine), f32), traces, ((3, 40, fine), f32),
            ((3, 40, fine), f32), ((40, 6 * fine), f32),
        ],
        received, table, lift_matrix,
    )
    window = [
        ((blocks, 272, fine), f32), ((20, blocks * 3 * fine), f32), ((20, blocks * 3 * fine), f32),
        ((blocks, 4, 32, fine), f32), ((blocks, 32, fine), f32), traces, ((3, 40, fine), f32),
        ((blocks, 3, 40, fine), f32), ((40, blocks * 3 * fine), f32),
        ((72, blocks * 3 * fine), f32), ((20, blocks * 3 * fine), f32), ((72, 20), f32),
    ]
    rows = share(copies)
    (copies,) = call(
        first_window_kernel,
        [((group, 120, fine), f32)],
        window,
        spot, *rows, derivatives, lift_matrix,
        smem=(0,),
    )
    states = share(copies)
    (outgoing,) = call(
        last_window_kernel,
        [((slots, LANES), f32)],
        [((128, fine), f32), ((128, slots), f32)] + window,
        spot, *rows, *states, back, derivatives, lift_matrix,
        smem=(0,),
    )
    returned = swap_slots(outgoing)
    merged, ends = call(
        merge_kernel,
        [((6, 20, own), f32), ((64, LANES), f32)],
        [
            ((120, own), f32), ((128, slots), f32), ((120, dense), f32), ((3, 20, own), f32),
            ((4, 32, dense), f32), traces, ((4, 32, own), f32),
        ] + work,
        returned, home, dense_slots, before, fine_code, early, fields, ends_below, ends_above,
        geometry, normals, face_scale, face_nbr, derivatives, lift_matrix,
    )
    below, above = exchange(ends)
    (electric,) = call(
        coarse_electric_kernel,
        [((3, 20, own), f32)],
        [((4, 32, own), f32)] + work,
        merged, geometry, normals, face_scale, face_nbr, derivatives, lift_matrix,
    )
    (out,) = call(
        finish_kernel,
        [((6, 20, own), f32)],
        [
            traces, ((40, 6 * LANES), f32), ((4, 32, LANES), f32), ((3, 40, LANES), f32),
            ((3, 40, LANES), f32),
        ],
        merged, electric, below, above, normals, face_scale, face_nbr, lift_matrix,
    )
    return out


def solution(mesh):
    return jax.shard_map(
        per_device,
        mesh=mesh,
        in_specs=(
            P(None, None, ("dom", "sub")),
            P(None, ("dom", "sub")),
            P(None, None, ("dom", "sub")),
            P(None, ("dom", "sub")),
            P(),
            P(),
            P(None, ("dom", "sub")),
            P(("dom", "sub")),
            P(("dom", "sub")),
            P(None, ("dom", "sub")),
            P(None, ("dom", "sub")),
        ),
        out_specs=P(None, None, ("dom", "sub")),
        check_vma=False,
    )
```

```python
import functools

import jax
import jax.numpy as jnp
import numpy as np
from jax import lax
from jax.experimental import pallas as pl
from jax.experimental.pallas import tpu as pltpu
from jax.sharding import PartitionSpec as P

SUBSTEPS = 4
COARSE_STEP = 0.2
FINE_STEP = COARSE_STEP / SUBSTEPS
LANES = 128
VMEM_BYTES = 40 * 2**20
PACK_VMEM_BYTES = 60 * 2**20
RING = ("dom", "sub")
REACH = 4
highest = lax.Precision.HIGHEST


def face_table():
    places = [
        (along_r, along_s, along_t)
        for along_t in range(4)
        for along_s in range(4 - along_t)
        for along_r in range(4 - along_t - along_s)
    ]
    bottom = [i for i, at in enumerate(places) if at[2] == 0]
    front = [i for i, at in enumerate(places) if at[1] == 0]
    slanted = [i for i, at in enumerate(places) if sum(at) == 3]
    beside = [i for i, at in enumerate(places) if at[0] == 0]
    return [bottom, front, slanted, beside]


def runs_of(nodes):
    runs = []
    for place, node in enumerate(nodes):
        if runs and runs[-1][1] + runs[-1][2] == node:
            runs[-1][2] += 1
        else:
            runs.append([place, node, 1])
    return runs


RUNS = [runs_of(nodes) for nodes in face_table()]


def seat(block, rows, columns):
    chip, core = block // 2, block % 2
    y, z = chip // columns, chip % columns
    if y % 2:
        z, core = columns - 1 - z, 1 - core
    return (y * columns + z) * 2 + core


def seats(count):
    chips = count // 2
    rows = max(r for r in range(1, chips + 1) if chips % r == 0 and r * r <= chips)
    return np.array([seat(block, rows, chips // rows) for block in range(count)], np.int32)


def slot_order(count, cap):
    block_at = np.argsort(seats(count))
    return (block_at[:, None] * cap + np.arange(cap)[None, :]).reshape(-1).astype(np.int32)


def take(block, lane):
    return jnp.take_along_axis(block, lane, axis=1, mode="promise_in_bounds")


def rows8(row):
    return jnp.broadcast_to(row, (8, LANES))


def lanes_at(block):
    if isinstance(block, int):
        return slice(block * LANES, (block + 1) * LANES)
    return pl.ds(pl.multiple_of(block * LANES, LANES), LANES)


def gather32(sources, which, lane, start):
    groups = list(start)
    for number, source in enumerate(sources):
        hit = which == number
        for group in range(4):
            groups[group] = jnp.where(hit, take(source(group), lane), groups[group])
    return groups


def spread_normals(normal_rows, out_ref):
    for c in range(3):
        for f in range(4):
            out_ref[c, f * 10 : f * 10 + 10, :] = jnp.broadcast_to(normal_rows(c, f), (10, LANES))


def regroup(jump_ref, sorted_ref):
    for f in range(4):
        for c in range(3):
            sorted_ref[c, f * 10 : f * 10 + 10, :] = jump_ref[f, c * 10 : c * 10 + 10, :]


def crossed(normals, jumps):
    def part(c):
        a, b = (c + 1) % 3, (c + 2) % 3
        return normals[a] * jumps[b] - normals[b] * jumps[a]

    return [part(c) for c in range(3)]


def curl_part(c, factor, grad):
    m, n = (c + 1) % 3, (c + 2) % 3
    total = factor(m, 0) * grad(0, n) - factor(n, 0) * grad(0, m)
    for a in (1, 2):
        total += factor(m, a) * grad(a, n) - factor(n, a) * grad(a, m)
    return total


def stack_derivatives(derivatives_ref, out_ref):
    out_ref[...] = jnp.zeros_like(out_ref)
    for a in range(3):
        out_ref[a * 24 : a * 24 + 20, :] = derivatives_ref[a]


def dot(a, b):
    return jnp.dot(a, b, precision=highest, preferred_element_type=jnp.float32)


def inverse_of(row_of, count, width, none):
    columns = [
        jnp.transpose(jnp.broadcast_to(row_of(b), (LANES, LANES))) for b in range(count)
    ]
    lane = lax.broadcasted_iota(jnp.int32, (LANES, LANES), 1)
    number = lax.broadcasted_iota(jnp.int32, (LANES, LANES), 0)
    out = []
    for w in range(width):
        best = jnp.full((LANES, LANES), none, jnp.int32)
        for b in range(count):
            best = jnp.maximum(
                best, jnp.where(columns[b] == lane + w * LANES, number + b * LANES, none)
            )
        out.append(jnp.max(best, axis=0, keepdims=True))
    return out


def pack_kernel(
    plain_send_hbm, order_hbm, fields_hbm, nbr_hbm, geometry_hbm, normals_hbm, scale_hbm,
    out_ref, ends_ref, home_ref, slot_ref, before_ref,
    plain_send_ref, order_ref, fields_ref, nbr_ref, geometry_ref, normals_ref, scale_ref,
    send_ref, rank_ref, row_ref, flat_ref, nb_ref, pool_ref, dense_ref, feature_ref,
    *sems,
):
    pairs = [
        (plain_send_hbm, plain_send_ref), (order_hbm, order_ref), (fields_hbm, fields_ref),
        (nbr_hbm, nbr_ref), (geometry_hbm, geometry_ref), (normals_hbm, normals_ref),
        (scale_hbm, scale_ref),
    ]
    copies = [pltpu.make_async_copy(a, b, sem) for (a, b), sem in zip(pairs, sems)]
    for copy in copies:
        copy.start()
    copies[0].wait()
    copies[1].wait()
    own = fields_ref.shape[2]
    blocks = own // LANES
    send_blocks = plain_send_ref.shape[0]
    dense_blocks = dense_ref.shape[1] // LANES
    for sb in range(send_blocks):
        order = rows8(order_ref[sb : sb + 1, :])
        row = jnp.zeros((8, LANES), jnp.int32)
        for b in range(send_blocks):
            block = take(rows8(plain_send_ref[b : b + 1, :]), order & (LANES - 1))
            row = jnp.where((order >> 7) == b, block, row)
        send_ref[sb : sb + 1, :] = row[0:1, :]
    upper = lax.broadcasted_iota(jnp.int32, (LANES, LANES), 0) <= lax.broadcasted_iota(
        jnp.int32, (LANES, LANES), 1
    )
    upper = jnp.where(upper, 1.0, 0.0)
    total = jnp.full((8, LANES), -1.0, jnp.float32)
    for sb in range(send_blocks):
        filled = rows8(send_ref[sb : sb + 1, :]) < own
        counts = jnp.where(filled, 1.0, 0.0)
        rank = total + dot(counts, upper)
        total += jnp.sum(counts, axis=1, keepdims=True)
        rank = jnp.where(filled, rank.astype(jnp.int32), LANES * LANES)
        rank_ref[sb : sb + 1, :] = rank[0:1, :]
    slots = inverse_of(lambda b: rank_ref[b : b + 1, :], send_blocks, dense_blocks, -1)
    for b in range(dense_blocks):
        slot_ref[b : b + 1, :] = slots[b]
        slot = rows8(slots[b])
        row = jnp.full((8, LANES), LANES * LANES, jnp.int32)
        for sb in range(send_blocks):
            block = take(rows8(send_ref[sb : sb + 1, :]), slot & (LANES - 1))
            row = jnp.where((slot >> 7) == sb, block, row)
        row_ref[b : b + 1, :] = row[0:1, :]
    homes = inverse_of(lambda b: row_ref[b : b + 1, :], dense_blocks, blocks, -1)
    for b in range(blocks):
        home_ref[b : b + 1, :] = homes[b]
    for copy in copies[2:]:
        copy.wait()
    for c in range(6):
        flat_ref[c * 20 : c * 20 + 20, :] = fields_ref[c]
    flat_ref[120:129, :] = geometry_ref[...]
    for c in range(3):
        flat_ref[129 + 4 * c : 133 + 4 * c, :] = normals_ref[c] * scale_ref[...]
    flat_ref[141:144, :] = jnp.zeros((3, own), jnp.float32)
    nb_ref[0:4, :] = nbr_ref[...]
    nb_ref[4:8, :] = nbr_ref[...]
    low_half = lax.broadcasted_iota(jnp.int32, (20, LANES), 1) < LANES // 2
    for c in range(3):
        ends_ref[c * 20 : c * 20 + 20, :] = jnp.where(
            low_half, fields_ref[c, :, 0:LANES], fields_ref[c, :, own - LANES : own]
        )
    ends_ref[60:64, :] = jnp.zeros((4, LANES), jnp.float32)
    for eh in range(2):
        for f in range(4):
            for c in range(3):
                for place, node, length in RUNS[f]:
                    pool_ref[eh, f, c * 10 + place : c * 10 + place + length, :] = fields_ref[
                        eh * 3 + c, node : node + length, :
                    ]
            pool_ref[eh, f, 30:32, :] = jnp.zeros((2, own), jnp.float32)
    sublane = lax.broadcasted_iota(jnp.int32, (8, LANES), 0)

    def pick(db, carry):
        row = rows8(jnp.minimum(row_ref[db : db + 1, :], own - 1))
        lane, which = row & (LANES - 1), row >> 7
        hits = [which == b for b in range(blocks)]
        for group in range(18):
            rows = slice(group * 8, group * 8 + 8)
            value = take(flat_ref[rows, 0:LANES], lane)
            for b in range(1, blocks):
                value = jnp.where(hits[b], take(flat_ref[rows, lanes_at(b)], lane), value)
            dense_ref[rows, lanes_at(db)] = value
        nbr = take(nb_ref[:, 0:LANES], lane)
        for b in range(1, blocks):
            nbr = jnp.where(hits[b], take(nb_ref[:, lanes_at(b)], lane), nbr)
        wall = jnp.where(nbr == 4 * row + sublane, -1.0, 1.0)
        for f in range(4):
            code = rows8(nbr[f : f + 1, :])
            sign = rows8(wall[f : f + 1, :])
            lane_f = (code >> 2) & (LANES - 1)
            which_f = (code & 3) * blocks + (code >> 9)
            groups = [jnp.zeros((8, LANES), jnp.float32)] * 8
            for number in range(4 * blocks):
                hit = which_f == number
                for group in range(8):
                    block = pool_ref[
                        group // 4,
                        number // blocks,
                        group % 4 * 8 : group % 4 * 8 + 8,
                        lanes_at(number % blocks),
                    ]
                    groups[group] = jnp.where(hit, take(block, lane_f), groups[group])
            for group in range(8):
                value = groups[group] * sign if group < 4 else groups[group]
                length = 8 if group % 4 < 3 else 6
                at = 144 + (group // 4 * 4 + f) * 30 + group % 4 * 8
                dense_ref[at : at + length, lanes_at(db)] = value[:length]
        return carry

    for db in range(dense_blocks):
        pick(db, 0)
    before_ref[...] = dense_ref[0:64, :]
    chunks = LANES * out_ref.shape[0] // (send_blocks * LANES)
    for sb in range(send_blocks):
        rank = rows8(rank_ref[sb : sb + 1, :])
        lane = rank & (LANES - 1)
        hits = [(rank >> 7) == b for b in range(dense_blocks)]
        for group in range(dense_ref.shape[0] // 8):
            rows = slice(group * 8, group * 8 + 8)
            value = jnp.zeros((8, LANES), jnp.float32)
            for b in range(dense_blocks):
                value = jnp.where(hits[b], take(dense_ref[rows, lanes_at(b)], lane), value)
            feature_ref[rows, :] = value
        out_ref[sb * chunks : (sb + 1) * chunks] = jnp.transpose(feature_ref[...]).reshape(
            chunks, LANES // chunks, feature_ref.shape[0]
        )


def unpack_kernel(
    width, received_ref, table_ref, lift_ref,
    out_ref, back_ref,
    feature_ref, picked_ref, held_ref, sorted_ref, normal_ref, flux_ref,
):
    nbr_ref, slots_ref = table_ref.at[0:4], table_ref.at[4:5]
    slot_blocks = received_ref.shape[0] // LANES
    feature_ref[...] = jnp.transpose(received_ref[...])
    slot = rows8(slots_ref[...])
    lane, which = slot & (LANES - 1), slot >> 7
    hits = [which == b for b in range(slot_blocks)]
    for group in range(feature_ref.shape[0] // 8):
        at = slice(group * 8, group * 8 + 8)
        value = take(feature_ref[at, 0:LANES], lane)
        for b in range(1, slot_blocks):
            value = jnp.where(hits[b], take(feature_ref[at, lanes_at(b)], lane), value)
        picked_ref[at, :] = value
    spread_normals(lambda c, f: picked_ref[129 + 4 * c + f : 130 + 4 * c + f, :], normal_ref)
    frozen_code = 4 * LANES + 4 * 2 * width
    for eh in range(2):
        for f in range(4):
            frozen = jnp.broadcast_to(nbr_ref[f : f + 1, :] == frozen_code, (30, LANES))
            at = 144 + (eh * 4 + f) * 30
            held_ref[f, 0:30, :] = jnp.where(frozen, picked_ref[at : at + 30, :], 0.0)
        regroup(held_ref, sorted_ref)
        flux = crossed([normal_ref[c] for c in range(3)], [sorted_ref[c] for c in range(3)])
        for c in range(3):
            flux_ref[:, lanes_at(eh * 3 + c)] = flux[c]
    lifted = dot(0.5 * lift_ref[...], flux_ref[...])
    place = lax.broadcasted_iota(jnp.int32, (8, LANES), 1)
    both = take(table_ref[...], (place >> 2) & (width - 1))
    lane = jnp.where(place < LANES // 2, rows8(both[6:7, :]), rows8(both[5:6, :]))
    picked_ref[144:264, :] = jnp.concatenate(
        [lifted[:, k * LANES : (k + 1) * LANES] for k in range(6)]
    )
    picked_ref[264:268, :] = nbr_ref[...].astype(jnp.float32)
    picked_ref[268:272, :] = lane[0:4, :].astype(jnp.float32)
    for k in range(out_ref.shape[0]):
        out_ref[k] = picked_ref[0:272, :]
    backs = inverse_of(lambda b: slots_ref[...], 1, slot_blocks, 0)
    for b in range(slot_blocks):
        back_ref[b : b + 1, :] = backs[b]


def window_state(spot_ref, parts, rows, block_ref):
    size = parts[0].shape[0]

    def fetch(w, carry):
        spot = spot_ref[w]
        for number, part in enumerate(parts):

            @pl.when((spot >= number * size) & (spot < number * size + size))
            def _(number=number, part=part):
                block_ref[w, 0:rows, :] = part[spot - number * size, 0:rows, :]

        return carry

    lax.fori_loop(0, 2 * REACH + 1, fetch, 0)


def window_steps(
    derivatives_ref, lift_ref, block_ref, efield_ref, hfield_ref, pool_ref, export_ref, jump_ref,
    sorted_ref, spread_ref, flux_ref, grad_ref, lifted_ref, stack_ref,
):
    blocks = 2 * REACH + 1
    stack_derivatives(derivatives_ref, stack_ref)
    lift = 0.5 * lift_ref[...]
    half_lanes = lax.broadcasted_iota(jnp.int32, (8, LANES), 1) < LANES // 2
    face = lax.broadcasted_iota(jnp.int32, (8, LANES), 1) & 3
    zero = jnp.zeros((8, LANES), jnp.float32)

    def prepare(w, carry):
        for c in range(3):
            efield_ref[:, lanes_at(w * 3 + c)] = block_ref[w, c * 20 : c * 20 + 20, :]
            hfield_ref[:, lanes_at(w * 3 + c)] = block_ref[w, 60 + c * 20 : 80 + c * 20, :]
        spread_normals(
            lambda c, f: block_ref[w, 129 + 4 * c + f : 130 + 4 * c + f, :], spread_ref.at[w]
        )
        return carry

    for w in range(blocks):
        prepare(w, 0)
    for level in range(1, REACH + 1):
        magnetic = level % 2 == 1
        source_ref, target_ref = (efield_ref, hfield_ref) if magnetic else (hfield_ref, efield_ref)
        step = -FINE_STEP if magnetic else FINE_STEP
        held = 144 if magnetic else 204
        first, last = level, blocks - level

        def expose(w, carry, source_ref=source_ref):
            for f in range(4):
                for c in range(3):
                    for place, node, length in RUNS[f]:
                        pool_ref[w, f, c * 10 + place : c * 10 + place + length, :] = source_ref[
                            node : node + length, lanes_at(w * 3 + c)
                        ]
            lane = rows8(block_ref[w, 268:269, :]).astype(jnp.int32)
            groups = gather32(
                [lambda g, f=f: pool_ref[w, f, g * 8 : g * 8 + 8, :] for f in range(4)],
                face, lane, [zero] * 4,
            )
            for g in range(4):
                export_ref[w, g * 8 : g * 8 + 8, :] = groups[g]
            return carry

        for w in range(first - 1, last + 1):
            expose(w, 0)

        def gather(w, carry):
            sources = [
                lambda g, f=f: pool_ref[w, f, g * 8 : g * 8 + 8, :] for f in range(4)
            ]
            halo = [
                jnp.where(
                    half_lanes,
                    export_ref[w - 1, g * 8 : g * 8 + 8, :],
                    export_ref[w + 1, g * 8 : g * 8 + 8, :],
                )
                for g in range(4)
            ]
            sources.append(lambda g: halo[g])
            for f in range(4):
                code = rows8(block_ref[w, 264 + f : 265 + f, :]).astype(jnp.int32)
                local = code < 4 * LANES
                which = jnp.where(local, code & 3, code >> 7)
                lane = jnp.where(local, code >> 2, code) & (LANES - 1)
                groups = gather32(sources, which, lane, [zero] * 4)
                for g in range(4):
                    jump_ref[w, f, g * 8 : g * 8 + 8, :] = (
                        groups[g] - pool_ref[w, f, g * 8 : g * 8 + 8, :]
                    )
            regroup(jump_ref.at[w], sorted_ref.at[w])
            flux = crossed([spread_ref[w, c] for c in range(3)], [sorted_ref[w, c] for c in range(3)])
            for c in range(3):
                flux_ref[:, lanes_at(w * 3 + c)] = flux[c]
            return carry

        for w in range(first, last):
            gather(w, 0)
        span = slice(first * 3 * LANES, last * 3 * LANES)
        grad_ref[:, span] = dot(stack_ref[...], source_ref[:, span])
        lifted_ref[:, span] = dot(lift, flux_ref[:, span])

        def update(w, carry, target_ref=target_ref, step=step, held=held):
            def factor(m, a):
                return block_ref[w, 120 + 3 * m + a : 121 + 3 * m + a, :]

            def grad(a, c):
                return grad_ref[a * 24 : a * 24 + 20, lanes_at(w * 3 + c)]

            for c in range(3):
                at = lanes_at(w * 3 + c)
                rate = (
                    curl_part(c, factor, grad)
                    + lifted_ref[:, at]
                    + block_ref[w, held + c * 20 : held + c * 20 + 20, :]
                )
                target_ref[:, at] = target_ref[:, at] + step * rate
            return carry

        for w in range(first, last):
            update(w, 0)


def first_window_kernel(
    spot_ref, row_ref, next_ref, twin_ref, derivatives_ref, lift_ref,
    out_ref,
    block_ref, efield_ref, hfield_ref, *scratch,
):
    window_state(spot_ref, (row_ref, next_ref, twin_ref), 272, block_ref)
    window_steps(derivatives_ref, lift_ref, block_ref, efield_ref, hfield_ref, *scratch)
    for c in range(3):
        electric = efield_ref[:, lanes_at(REACH * 3 + c)]
        magnetic = hfield_ref[:, lanes_at(REACH * 3 + c)]
        for k in range(out_ref.shape[0]):
            out_ref[k, c * 20 : c * 20 + 20, :] = electric
            out_ref[k, 60 + c * 20 : 80 + c * 20, :] = magnetic


def last_window_kernel(
    spot_ref, row_ref, next_ref, twin_ref, row_state_ref, next_state_ref, twin_state_ref,
    back_ref, derivatives_ref, lift_ref,
    out_ref,
    result_ref, feature_ref, block_ref, efield_ref, hfield_ref, *scratch,
):
    window_state(spot_ref, (row_ref, next_ref, twin_ref), 272, block_ref)
    window_state(spot_ref, (row_state_ref, next_state_ref, twin_state_ref), 120, block_ref)
    window_steps(derivatives_ref, lift_ref, block_ref, efield_ref, hfield_ref, *scratch)
    for c in range(3):
        result_ref[c * 20 : c * 20 + 20, :] = efield_ref[:, lanes_at(REACH * 3 + c)]
        result_ref[60 + c * 20 : 80 + c * 20, :] = hfield_ref[:, lanes_at(REACH * 3 + c)]
    result_ref[120:128, :] = jnp.zeros((8, LANES), jnp.float32)
    for b in range(back_ref.shape[0]):
        lane = rows8(back_ref[b : b + 1, :])
        for g in range(16):
            feature_ref[g * 8 : g * 8 + 8, lanes_at(b)] = take(
                result_ref[g * 8 : g * 8 + 8, :], lane
            )
    out_ref[...] = jnp.transpose(feature_ref[...])


def coarse_pool(field_ref, first, pool_ref):
    own = field_ref.shape[2]
    for f in range(4):
        for c in range(3):
            for place, node, length in RUNS[f]:
                pool_ref[f, c * 10 + place : c * 10 + place + length, 0:own] = field_ref[
                    first + c, node : node + length, :
                ]


def halo_rows(below, above):
    half = lax.broadcasted_iota(jnp.int32, below.shape, 1) >= LANES // 2
    return pltpu.roll(jnp.where(half, below, above), LANES // 2, 1)


def coarse_halo(halo, store):
    for f in range(4):
        for c in range(3):
            for place, node, length in RUNS[f]:
                store(f, c * 10 + place, length, halo[c * 20 + node : c * 20 + node + length, :])


def coarse_flux(
    sources, number_of, mirror, nbr_ref, normals_ref, scale_ref, own_ref, flux_ref, jump_ref,
    sorted_ref, spread_ref, ends=None,
):
    own_blocks = flux_ref.shape[2] // LANES
    lane_number = lax.broadcasted_iota(jnp.int32, (8, LANES), 1)
    zero = jnp.zeros((8, LANES), jnp.float32)

    def one(eb, outer):
        at = lanes_at(eb)
        for f in range(4):
            code = rows8(nbr_ref[f : f + 1, at])
            which, lane = number_of(f, at, code)
            groups = gather32(sources, which, lane, [zero] * 4)
            if mirror:
                wall = code == 4 * (lane_number + eb * LANES) + f
                sign = jnp.where(wall, -1.0, 1.0)
                groups = [group * sign for group in groups]
            if outer:
                face = jnp.where(code >= 4 * own_blocks * LANES, code & 3, 4)
                groups = gather32(ends, face, (code >> 2) & (LANES - 1), groups)
            for g in range(4):
                jump_ref[eb, f, g * 8 : g * 8 + 8, :] = (
                    groups[g] - own_ref[f, g * 8 : g * 8 + 8, at]
                )
        regroup(jump_ref.at[eb], sorted_ref.at[eb])
        scale = scale_ref[:, at]
        scaled = [normals_ref[c, :, at] * scale for c in range(3)]
        spread_normals(lambda c, f: scaled[c][f : f + 1, :], spread_ref.at[eb])
        flux = crossed([spread_ref[eb, c] for c in range(3)], [sorted_ref[eb, c] for c in range(3)])
        for c in range(3):
            flux_ref[c, :, at] = flux[c]

    for eb in range(own_blocks):
        one(eb, ends is not None and eb in (0, own_blocks - 1))


def own_faces(pool_ref, own):
    blocks = own // LANES
    sources = [
        lambda g, n=n: pool_ref[n // blocks, g * 8 : g * 8 + 8, lanes_at(n % blocks)]
        for n in range(4 * blocks)
    ]

    def number_of(f, at, code):
        block = code >> 9
        which = jnp.where(block < blocks, (code & 3) * blocks + block, 4 * blocks)
        return which, (code >> 2) & (LANES - 1)

    return sources, number_of


def coarse_update(
    step, source, target, out, geometry_ref, derivatives_ref, lift_ref, stack_ref, flux_ref,
    grad_ref, lifted_ref,
):
    own_blocks = flux_ref.shape[2] // LANES
    stack_derivatives(derivatives_ref, stack_ref)
    lift = 0.5 * lift_ref[...]
    for c in range(3):
        grad_ref[c] = dot(stack_ref[...], source(c))
        lifted_ref[c] = dot(lift, flux_ref[c])

    def one(eb):
        at = lanes_at(eb)

        def factor(m, a):
            return geometry_ref[3 * m + a : 3 * m + a + 1, at]

        def grad(a, c):
            return grad_ref[c, a * 24 : a * 24 + 20, at]

        for c in range(3):
            out(c, at, target(c, at) + step * (curl_part(c, factor, grad) + lifted_ref[c, :, at]))

    for eb in range(own_blocks):
        one(eb)


def early_kernel(
    fields_ref, home_ref, geometry_ref, normals_ref, scale_ref, nbr_ref, derivatives_ref, lift_ref,
    magnetic_ref, code_ref,
    pool_ref, flux_ref, jump_ref, sorted_ref, spread_ref, stack_ref, grad_ref, lifted_ref,
):
    own = fields_ref.shape[2]
    blocks = own // LANES
    coarse_pool(fields_ref, 0, pool_ref)
    sources, number_of = own_faces(pool_ref, own)
    coarse_flux(
        sources, number_of, True, nbr_ref, normals_ref, scale_ref, pool_ref, flux_ref, jump_ref,
        sorted_ref, spread_ref,
    )

    def out(c, at, value):
        magnetic_ref[c, :, at] = value

    coarse_update(
        -COARSE_STEP, lambda c: fields_ref[c], lambda c, at: fields_ref[3 + c, :, at], out,
        geometry_ref, derivatives_ref, lift_ref, stack_ref, flux_ref, grad_ref, lifted_ref,
    )
    width = LANES * 2

    def locate(eb, carry):
        at = lanes_at(eb)
        for f in range(4):
            code = rows8(nbr_ref[f : f + 1, at])
            home = jnp.full((8, LANES), -1, jnp.int32)
            for b in range(blocks):
                block = take(rows8(home_ref[b : b + 1, :]), (code >> 2) & (LANES - 1))
                home = jnp.where((code >> 9) == b, block, home)
            code_ref[f : f + 1, at] = jnp.where(home < 0, -1, (code & 3) * width + home)[0:1, :]
        return carry

    lax.fori_loop(0, blocks, locate, 0)


def merge_kernel(
    returned_ref, home_ref, slot_ref, before_ref, code_ref, magnetic_ref, fields_ref, below_ref,
    above_ref, geometry_ref, normals_ref, scale_ref, nbr_ref, derivatives_ref, lift_ref,
    merged_ref, ends_ref,
    flat_ref, back_ref, dense_ref, change_ref, fine_pool_ref, end_pool_ref,
    pool_ref, flux_ref, jump_ref, sorted_ref, spread_ref, stack_ref, grad_ref, lifted_ref,
):
    own = fields_ref.shape[2]
    slot_blocks = returned_ref.shape[0] // LANES
    dense_blocks = dense_ref.shape[1] // LANES
    back_ref[...] = jnp.transpose(returned_ref[...])
    for db in range(dense_blocks):
        slot = rows8(slot_ref[db : db + 1, :])
        lane = slot & (LANES - 1)
        hits = [(slot >> 7) == b for b in range(slot_blocks)]
        for group in range(15):
            rows = slice(group * 8, group * 8 + 8)
            value = jnp.zeros((8, LANES), jnp.float32)
            for b in range(slot_blocks):
                value = jnp.where(hits[b], take(back_ref[rows, lanes_at(b)], lane), value)
            dense_ref[rows, lanes_at(db)] = value
    for c in range(6):
        flat_ref[c * 20 : c * 20 + 20, :] = fields_ref[c]

    def merge(eb):
        at = lanes_at(eb)
        home = rows8(home_ref[eb : eb + 1, :])
        lane = home & (LANES - 1)
        hits = [(home >> 7) == b for b in range(dense_blocks)]
        for group in range(15):
            rows = slice(group * 8, group * 8 + 8)
            value = flat_ref[rows, at]
            for b in range(dense_blocks):
                value = jnp.where(hits[b], take(dense_ref[rows, lanes_at(b)], lane), value)
            flat_ref[rows, at] = value

    for eb in range(own // LANES):
        merge(eb)
    for c in range(6):
        merged_ref[c] = flat_ref[c * 20 : c * 20 + 20, :]
    for c in range(3):
        change_ref[c] = merged_ref[c] - fields_ref[c]
    coarse_pool(change_ref, 0, pool_ref)
    dense_ref[0:64, :] = dense_ref[0:64, :] - before_ref[...]
    for f in range(4):
        for c in range(3):
            for place, node, length in RUNS[f]:
                rows = slice(c * 10 + place, c * 10 + place + length)
                first = c * 20 + node
                fine_pool_ref[f, rows, :] = dense_ref[first : first + length, :]
    halo = halo_rows(below_ref[...], above_ref[...])

    def store(f, place, length, value):
        end_pool_ref[f, place : place + length, :] = value

    coarse_halo(halo, store)
    sources = [
        lambda g, n=n: fine_pool_ref[
            n // dense_blocks, g * 8 : g * 8 + 8, lanes_at(n % dense_blocks)
        ]
        for n in range(4 * dense_blocks)
    ]
    ends = [lambda g, f=f: end_pool_ref[f, g * 8 : g * 8 + 8, :] for f in range(4)]

    def number_of(f, at, code):
        fine = rows8(code_ref[f : f + 1, at])
        return fine >> 7, fine & (LANES - 1)

    coarse_flux(
        sources, number_of, True, nbr_ref, normals_ref, scale_ref, pool_ref, flux_ref, jump_ref,
        sorted_ref, spread_ref, ends,
    )

    def target(c, at):
        return magnetic_ref[c, :, at] + (merged_ref[3 + c, :, at] - fields_ref[3 + c, :, at])

    def out(c, at, value):
        merged_ref[3 + c, :, at] = value

    coarse_update(
        -COARSE_STEP, lambda c: change_ref[c], target, out,
        geometry_ref, derivatives_ref, lift_ref, stack_ref, flux_ref, grad_ref, lifted_ref,
    )
    low_half = lax.broadcasted_iota(jnp.int32, (20, LANES), 1) < LANES // 2
    for c in range(3):
        ends_ref[c * 20 : c * 20 + 20, :] = jnp.where(
            low_half, merged_ref[3 + c, :, 0:LANES], merged_ref[3 + c, :, own - LANES : own]
        )
    ends_ref[60:64, :] = jnp.zeros((4, LANES), jnp.float32)


def coarse_electric_kernel(
    merged_ref, geometry_ref, normals_ref, scale_ref, nbr_ref, derivatives_ref, lift_ref,
    out_ref,
    pool_ref, flux_ref, jump_ref, sorted_ref, spread_ref, stack_ref, grad_ref, lifted_ref,
):
    own = merged_ref.shape[2]
    coarse_pool(merged_ref, 3, pool_ref)
    sources, number_of = own_faces(pool_ref, own)
    coarse_flux(
        sources, number_of, False, nbr_ref, normals_ref, scale_ref, pool_ref, flux_ref, jump_ref,
        sorted_ref, spread_ref,
    )

    def out(c, at, value):
        out_ref[c, :, at] = value

    coarse_update(
        COARSE_STEP, lambda c: merged_ref[3 + c], lambda c, at: merged_ref[c, :, at], out,
        geometry_ref, derivatives_ref, lift_ref, stack_ref, flux_ref, grad_ref, lifted_ref,
    )


def finish_kernel(
    merged_ref, electric_ref, below_ref, above_ref, normals_ref, scale_ref, nbr_ref, lift_ref,
    out_ref,
    pool_ref, flux_ref, jump_ref, sorted_ref, spread_ref,
):
    own = merged_ref.shape[2]
    halo = halo_rows(below_ref[...], above_ref[...])

    def store(f, place, length, value):
        pool_ref[f, place : place + length, :] = value

    coarse_halo(halo, store)
    zero = jnp.zeros((8, LANES), jnp.float32)
    sources = [lambda g, f=f: pool_ref[f, g * 8 : g * 8 + 8, :] for f in range(4)]
    ends = (0, own // LANES - 1)
    for number, eb in enumerate(ends):
        at = lanes_at(eb)
        for f in range(4):
            code = rows8(nbr_ref[f : f + 1, at])
            which = jnp.where(code >= 4 * own, code & 3, 4)
            groups = gather32(sources, which, (code >> 2) & (LANES - 1), [zero] * 4)
            for g in range(4):
                jump_ref[f, g * 8 : g * 8 + 8, :] = groups[g]
        regroup(jump_ref, sorted_ref)
        scale = scale_ref[:, at]
        scaled = [normals_ref[c, :, at] * scale for c in range(3)]
        spread_normals(lambda c, f: scaled[c][f : f + 1, :], spread_ref)
        flux = crossed([spread_ref[c] for c in range(3)], [sorted_ref[c] for c in range(3)])
        for c in range(3):
            flux_ref[:, lanes_at(number * 3 + c)] = flux[c]
    lifted = dot(0.5 * lift_ref[...], flux_ref[...])
    for c in range(3):
        out_ref[c, :, LANES : own - LANES] = electric_ref[c, :, LANES : own - LANES]
        for number, eb in enumerate(ends):
            at = (number * 3 + c) * LANES
            out_ref[c, :, lanes_at(eb)] = (
                electric_ref[c, :, lanes_at(eb)] + COARSE_STEP * lifted[:, at : at + LANES]
            )
        out_ref[3 + c] = merged_ref[3 + c]


def call(kernel, outs, scratch, *args, hbm=(), smem=(), vmem=VMEM_BYTES):
    whole = pl.BlockSpec(memory_space=pltpu.VMEM)
    specs = [
        pl.BlockSpec(memory_space=pltpu.HBM if number in hbm else pltpu.SMEM if number in smem
                     else pltpu.VMEM)
        for number in range(len(args))
    ]
    return pl.pallas_call(
        kernel,
        out_shape=[jax.ShapeDtypeStruct(shape, dtype) for shape, dtype in outs],
        in_specs=specs,
        out_specs=[whole] * len(outs),
        scratch_shapes=[pltpu.VMEM(shape, dtype) for shape, dtype in scratch]
        + [pltpu.SemaphoreType.DMA(())] * len(hbm),
        compiler_params=pltpu.CompilerParams(vmem_limit_bytes=vmem),
    )(*args)


def device_of(block):
    sub = lax.axis_size("sub")
    return int(seats(lax.axis_size("dom"))[block // sub]) * sub + block % sub


def exchange(block):
    count = lax.axis_size(RING)
    up = [(i, (i + 1) % count) for i in range(count)]
    down = [(target, source) for source, target in up]
    return lax.ppermute(block, RING, up), lax.ppermute(block, RING, down)


def share(copies):
    row = lax.all_to_all(copies, "sub", 0, 0, tiled=True)
    count = lax.axis_size("dom")
    seat_of = seats(count)

    def swap(partner):
        pairs = [(int(seat_of[d]), int(seat_of[partner(d) % count])) for d in range(count)]
        return lax.ppermute(row, "dom", pairs)

    return row, swap(lambda d: d - 1 if d % 2 == 0 else d + 1), swap(lambda d: d ^ 1)


def spots(count, size):
    table = np.zeros((count, 16), np.int32)
    for block in range(count):
        d, s = divmod(block, size)
        for w in range(2 * REACH + 1):
            step, at = divmod(s + w - REACH, size)
            part = 0 if step == 0 else 2 if (d + step) % count == d ^ 1 else 1
            table[device_of(block), w] = part * size + at
    return table


def swap_slots(rows):
    width = rows.shape[-1]
    chunks = rows.reshape(lax.axis_size("dom"), -1, width)
    return lax.all_to_all(chunks, "dom", split_axis=0, concat_axis=0, tiled=True).reshape(-1, width)


def per_device(
    fields, geometry, normals, face_scale, derivatives, lift_matrix, face_nbr, send_rows,
    fine_slots, export_rows, fine_nbr,
):
    f32, i32 = jnp.float32, jnp.int32
    own = fields.shape[2]
    slots = send_rows.shape[0]
    fine = fine_slots.shape[0]
    width = export_rows.shape[1]
    table = jnp.concatenate(
        [
            fine_nbr,
            fine_slots.reshape(1, fine),
            jnp.pad(export_rows, ((0, 0), (0, fine - width))),
            jnp.zeros((1, fine), i32),
        ]
    )
    count = lax.axis_size(RING)
    table = lax.ppermute(table, RING, [(i, device_of(i)) for i in range(count)])
    me = lax.axis_index(RING)
    spot = lax.dynamic_index_in_dim(
        jnp.asarray(spots(count, lax.axis_size("sub"))), me, keepdims=False
    )
    traces = ((4, 32, fine), f32)
    send = send_rows.reshape(slots // LANES, LANES)
    order = slot_order(lax.axis_size("dom"), slots // lax.axis_size("dom"))
    dense = 2 * fine
    packed, ends, home, dense_slots, before = call(
        pack_kernel,
        [
            ((lax.axis_size("dom"), slots // lax.axis_size("dom"), 384), f32), ((64, LANES), f32),
            ((own // LANES, LANES), i32), ((dense // LANES, LANES), i32), ((64, dense), f32),
        ],
        [
            (send.shape, i32), (send.shape, i32), (fields.shape, f32), (face_nbr.shape, i32),
            (geometry.shape, f32), (normals.shape, f32), (face_scale.shape, f32),
            (send.shape, i32), (send.shape, i32), ((dense // LANES, LANES), i32),
            ((144, own), f32), ((8, own), i32), ((2, 4, 32, own), f32), ((384, dense), f32),
            ((384, LANES), f32),
        ],
        send, jnp.asarray(order.reshape(send.shape)), fields, face_nbr, geometry, normals,
        face_scale,
        hbm=range(7),
        vmem=PACK_VMEM_BYTES,
    )
    received = swap_slots(packed)
    ends_below, ends_above = exchange(ends)
    work = [
        ((3, 40, own), f32), ((own // LANES, 4, 32, LANES), f32),
        ((own // LANES, 3, 40, LANES), f32), ((own // LANES, 3, 40, LANES), f32),
        ((72, 20), f32), ((3, 72, own), f32), ((3, 20, own), f32),
    ]
    early, fine_code = call(
        early_kernel,
        [((3, 20, own), f32), (face_nbr.shape, i32)],
        [((4, 32, own), f32)] + work,
        fields, home, geometry, normals, face_scale, face_nbr, derivatives, lift_matrix,
    )
    received, table, ends_below, ends_above, early, fine_code, spot = lax.optimization_barrier(
        (received, table, ends_below, ends_above, early, fine_code, spot)
    )
    group = lax.axis_size("sub")
    blocks = 2 * REACH + 1
    copies, back = call(
        functools.partial(unpack_kernel, width),
        [((group, 272, fine), f32), ((slots // LANES, LANES), i32)],
        [
            ((384, slots), f32), ((384, fine), f32), traces, ((3, 40, fine), f32),
            ((3, 40, fine), f32), ((40, 6 * fine), f32),
        ],
        received, table, lift_matrix,
    )
    window = [
        ((blocks, 272, fine), f32), ((20, blocks * 3 * fine), f32), ((20, blocks * 3 * fine), f32),
        ((blocks, 4, 32, fine), f32), ((blocks, 32, fine), f32), ((blocks, 4, 32, fine), f32),
        ((blocks, 3, 40, fine), f32),
        ((blocks, 3, 40, fine), f32), ((40, blocks * 3 * fine), f32),
        ((72, blocks * 3 * fine), f32), ((20, blocks * 3 * fine), f32), ((72, 20), f32),
    ]
    rows = share(copies)
    (copies,) = call(
        first_window_kernel,
        [((group, 120, fine), f32)],
        window,
        spot, *rows, derivatives, lift_matrix,
        smem=(0,),
    )
    states = share(copies)
    (outgoing,) = call(
        last_window_kernel,
        [((slots, LANES), f32)],
        [((128, fine), f32), ((128, slots), f32)] + window,
        spot, *rows, *states, back, derivatives, lift_matrix,
        smem=(0,),
    )
    returned = swap_slots(outgoing)
    merged, ends = call(
        merge_kernel,
        [((6, 20, own), f32), ((64, LANES), f32)],
        [
            ((120, own), f32), ((128, slots), f32), ((120, dense), f32), ((3, 20, own), f32),
            ((4, 32, dense), f32), traces, ((4, 32, own), f32),
        ] + work,
        returned, home, dense_slots, before, fine_code, early, fields, ends_below, ends_above,
        geometry, normals, face_scale, face_nbr, derivatives, lift_matrix,
    )
    below, above = exchange(ends)
    (electric,) = call(
        coarse_electric_kernel,
        [((3, 20, own), f32)],
        [((4, 32, own), f32)] + work,
        merged, geometry, normals, face_scale, face_nbr, derivatives, lift_matrix,
    )
    (out,) = call(
        finish_kernel,
        [((6, 20, own), f32)],
        [
            traces, ((40, 6 * LANES), f32), ((4, 32, LANES), f32), ((3, 40, LANES), f32),
            ((3, 40, LANES), f32),
        ],
        merged, electric, below, above, normals, face_scale, face_nbr, lift_matrix,
    )
    return out


def solution(mesh):
    return jax.shard_map(
        per_device,
        mesh=mesh,
        in_specs=(
            P(None, None, ("dom", "sub")),
            P(None, ("dom", "sub")),
            P(None, None, ("dom", "sub")),
            P(None, ("dom", "sub")),
            P(),
            P(),
            P(None, ("dom", "sub")),
            P(("dom", "sub")),
            P(("dom", "sub")),
            P(None, ("dom", "sub")),
            P(None, ("dom", "sub")),
        ),
        out_specs=P(None, None, ("dom", "sub")),
        check_vma=False,
    )
```
